128 devices in a mesh: row: 8 (over z, core), col: 16 (over y, x).
Axes of the slice: x: 4, y: 4, z: 4, core: 2. Of those that a mesh axis runs over, the one named last changes fastest.
Arguments:
- descriptors: bfloat16 [32, 262144], P(None, ('row', 'col')), may hold values from -12 to 12
- send_slot: int32 [262144], P(('row', 'col')), may hold values from 0 to 2048, as said below
- recv_slot: int32 [131072], P(('row', 'col')), may hold values from 0 to 2047, as said below
- block_pairs: int32 [2, 131072], P(None, ('row', 'col')), may hold values from 0 to 127, as said below
- start: float32 [16, 1024, 128], P(None, ('row', 'col')), may hold values from -6 to 6
Outputs:
- alphas: float32 [3, 16, 16], replicated
- betas: float32 [3, 16, 16], replicated
- basis: float32 [16, 1024, 128], P(None, ('row', 'col'))
The draws below stay inside these ranges and needn't reach their ends.
Inputs may be any that keep to these rules, and one draw needn't show every extreme that they name: `send_slot`: A live slot of tile owner s holds d * 16 + k for the block owner d that receives it and its rank k among the segments from s to d; no two live slots of one device share a value; a slot that holds no segment has the value 128 * 16. Every tile owner has some empty slots, and the busiest holds close to twice the mean. The position's segment arrives from device recv_slot // 16 with rank recv_slot % 16; each value of a device's shard is one live send_slot value of that source aimed at this device. `block_pairs`: row 0 is below 128 and row 1 below 64. No pair (I, J) is listed twice, and none has I = J. The list is symmetric: for every listed pair (I, J) the pair (J, I) is listed too, on the device that owns it by the rule of the steps.
All inputs are finite; a program needn't handle non-finite values.
Results may differ from the reference program's by a relative error of at most 0.017.
Values may be sent and summed in bfloat16 or wider, within the bound.
No kernel may reach another device: no remote copies, remote signals or barrier semaphores. Data moves between devices by JAX's collectives and lax.ppermute only.
A program may use at most 64 MiB of HBM per device.

```python
import jax
import jax.numpy as jnp
import numpy as np
from jax import lax

FEAT = 32
VECS = 16
BLOCK = 128
STEPS = 3
BLK_DEV = 8
PAIRS_DEV = 1024
SEG_DEV = 1024
SRC_DEV = 2048
CAP = 16
SOURCES = 262144
NSEG = 131072
NBLK = 1024
N_ROW = 8
N_COL = 16
DEVICES = 128


def relay_plan(key):
    count = DEVICES
    half = count // 2
    keys = jax.random.split(jax.random.fold_in(key, 11), 5)
    order = jax.random.permutation(keys[0], count)
    extra = jax.random.randint(keys[1], (half,), 0, half)
    extra = extra.at[0].set(half - 1)
    loads = jnp.zeros((count,), jnp.int32)
    loads = loads.at[order[0::2]].set(half + extra).at[order[1::2]].set(half - extra)
    inclusive = jnp.cumsum(loads)
    begin = inclusive - loads
    tickets = jnp.arange(count * half, dtype=jnp.int32)
    owner = jnp.sum((inclusive[None, :] <= tickets[:, None]).astype(jnp.int32), axis=1)
    local = tickets - begin[owner]
    dest_order = jax.random.permutation(keys[2], count)
    target = dest_order[tickets % count]
    turn = tickets // count
    src_perm = jax.vmap(lambda k: jax.random.permutation(k, SRC_DEV))(jax.random.split(keys[3], count))
    dst_perm = jax.vmap(lambda k: jax.random.permutation(k, SEG_DEV))(jax.random.split(keys[4], count))
    rank = jnp.arange(CAP, dtype=jnp.int32)[None, :]
    src_pos = src_perm[owner[:, None], local[:, None] * CAP + rank]
    send = jnp.full((SOURCES,), count * CAP, jnp.int32)
    send = send.at[(owner[:, None] * SRC_DEV + src_pos).ravel()].set((target[:, None] * CAP + rank).ravel())
    dst_pos = dst_perm[target[:, None], turn[:, None] * CAP + rank]
    recv = jnp.zeros((NSEG,), jnp.int32)
    recv = recv.at[(target[:, None] * SEG_DEV + dst_pos).ravel()].set((owner[:, None] * CAP + rank).ravel())
    return (send.astype(jnp.int32), recv.astype(jnp.int32))


def draw_send_slot(key, part):
    send, recv = relay_plan(key)
    return send


def draw_recv_slot(key, part):
    send, recv = relay_plan(key)
    return recv


def draw_block_pairs(key, part):
    key = jax.random.fold_in(key, 5)
    keys = jax.random.split(key, 3)
    count = N_ROW * N_COL
    half = PAIRS_DEV // 2
    spread_count = min(half, count)
    upper = BLK_DEV * (BLK_DEV - 1) // 2
    tri_lower, tri_upper = np.triu_indices(BLK_DEV, 1)
    tri_lower = jnp.asarray(tri_lower, dtype=jnp.int32)
    tri_upper = jnp.asarray(tri_upper, dtype=jnp.int32)
    offsets = jax.random.permutation(keys[0], count).astype(jnp.int32)
    where_one = jnp.argmax(offsets == 1)
    moved = offsets[1]
    offsets = offsets.at[where_one].set(moved).at[1].set(1)
    offsets = offsets[:spread_count]
    orders = jax.vmap(lambda k: jax.random.permutation(k, upper))(jax.random.split(keys[1], count * spread_count))
    orders = orders.reshape(count, spread_count, upper).astype(jnp.int32)
    anchor = (N_COL - 1 - offsets[0]) % count
    forced = BLK_DEV - 2
    holder = orders[anchor, 0, 0]
    swapped = jnp.where(orders == holder, forced, jnp.where(orders == forced, holder, orders))
    marked = (jnp.arange(count)[:, None, None] == anchor) & (jnp.arange(spread_count)[None, :, None] == 0)
    orders = jnp.where(marked, swapped, orders)
    ticket = jnp.arange(half, dtype=jnp.int32)
    offset_pick = ticket % spread_count
    repeat_pick = ticket // spread_count
    picked = orders[:, offset_pick, repeat_pick]
    row_block = tri_lower[picked]
    col_block = tri_upper[picked]
    own = jnp.arange(count, dtype=jnp.int32)
    row_of = own // N_COL
    col_of = own % N_COL
    target = (own[:, None] + offsets[offset_pick][None, :]) % count
    target_row = target // N_COL
    target_col = target % N_COL
    rows_all = jnp.zeros((count, PAIRS_DEV), jnp.int32)
    cols_all = jnp.zeros((count, PAIRS_DEV), jnp.int32)
    rows_all = rows_all.at[:, :half].set(target_col * BLK_DEV + row_block)
    cols_all = cols_all.at[:, :half].set(target_row * BLK_DEV + col_block)
    mirror_slot = jnp.broadcast_to(half + ticket[None, :], (count, half))
    rows_all = rows_all.at[target, mirror_slot].set(col_of[:, None] * BLK_DEV + col_block)
    cols_all = cols_all.at[target, mirror_slot].set(row_of[:, None] * BLK_DEV + row_block)
    shuffle = jax.vmap(lambda k: jax.random.permutation(k, PAIRS_DEV))(jax.random.split(keys[2], count))
    rows_all = jnp.take_along_axis(rows_all, shuffle, axis=1)
    cols_all = jnp.take_along_axis(cols_all, shuffle, axis=1)
    return jnp.stack([rows_all.ravel(), cols_all.ravel()]).astype(jnp.int32)


def shard_levels(key, dims, cuts, low, top_value):
    loudness = 1.0
    for dim, blocks in cuts:
        steps = jax.random.uniform(jax.random.fold_in(jax.random.fold_in(key, 6), dim), (blocks,), jnp.float32, low / len(cuts), top_value / len(cuts))
        loudness = loudness * jnp.repeat(jnp.exp(steps), dims[dim] // blocks).reshape((-1,) + (1,) * (len(dims) - 1 - dim))
    return loudness


def noise(rng, dims, deviation, bound, shards=(), kind=jnp.bfloat16):
    drawn = deviation * jax.random.normal(rng, dims, jnp.float32)
    if shards:
        drawn = drawn * shard_levels(rng, dims, shards, -0.22, 0.18)
    return jnp.clip(drawn, -bound, bound).astype(kind)


def setup_inputs(seed: int = 0) -> dict:
    splits = jax.random.split(jax.random.key(seed), 6)
    return {
        "descriptors": noise(splits[0], (FEAT, SOURCES), 2.0, 12.0, ((1, 128),)),
        "send_slot": draw_send_slot(jax.random.fold_in(splits[5], 71), 0),
        "recv_slot": draw_recv_slot(jax.random.fold_in(splits[5], 71), 0),
        "block_pairs": draw_block_pairs(jax.random.fold_in(splits[5], 71), 0),
        "start": noise(splits[4], (VECS, NBLK, BLOCK), 1.0, 6.0, ((1, 128),), jnp.float32),
    }


def build(blocked, first, second):
    left = blocked[:, first].astype(jnp.float32)
    right = blocked[:, second].astype(jnp.float32)
    dots = jnp.einsum('fga,fgb->gab', left, right)
    left_sq = lax.optimization_barrier(jnp.sum(left * left, axis=0))
    right_sq = lax.optimization_barrier(jnp.sum(right * right, axis=0))
    return jnp.exp((2.0 * dots - left_sq[:, :, None] - right_sq[:, None, :]) / (2.0 * FEAT)).astype(jnp.bfloat16)

def sweep(blocked, first, second, vectors):
    if vectors is None:
        init = jnp.zeros((NBLK, BLOCK), jnp.float32)
    else:
        init = jnp.zeros((VECS, NBLK, BLOCK), jnp.float32)

    def one(total, pair):
        rows_idx, cols_idx = pair
        weights = build(blocked, rows_idx, cols_idx)
        if vectors is None:
            total = total.at[rows_idx].add(lax.optimization_barrier(jnp.sum(weights.astype(jnp.float32), axis=2)))
        else:
            picked = vectors[:, cols_idx].astype(jnp.float32)
            contrib = jnp.einsum('gab,vgb->vga', weights.astype(jnp.float32), picked)
            total = total.at[:, rows_idx].add(contrib)
        return (total, None)
    total, unused = lax.scan(one, init, (first, second))
    return total

def inner(left, right):
    return jnp.einsum('unb,vnb->uv', left, right, precision=lax.Precision.HIGHEST)

def lower_inverse(gram):
    factor = jnp.linalg.cholesky(gram)
    eye = jnp.eye(gram.shape[0], dtype=gram.dtype)
    return (factor, jax.scipy.linalg.solve_triangular(factor, eye, lower=True))

def reference(descriptors, send_slot, recv_slot, block_pairs, start):
    owner = jnp.arange(SOURCES, dtype=jnp.int32) // SRC_DEV
    live = send_slot < DEVICES * CAP
    keyed = jnp.where(live, owner * SRC_DEV + send_slot, SOURCES)
    table = jnp.zeros((SOURCES,), jnp.int32).at[keyed].set(jnp.arange(SOURCES, dtype=jnp.int32), mode='drop')
    dest = jnp.arange(NSEG, dtype=jnp.int32) // SEG_DEV
    source = recv_slot // CAP
    rank = recv_slot % CAP
    index = table[source * SRC_DEV + dest * CAP + rank]
    blocked = descriptors[:, index].reshape(FEAT, NBLK, BLOCK)
    device = jnp.arange(DEVICES, dtype=jnp.int32)
    row_of = device // N_COL
    col_of = device % N_COL
    local_rows = block_pairs[0].reshape(DEVICES, PAIRS_DEV)
    local_cols = block_pairs[1].reshape(DEVICES, PAIRS_DEV)
    first = (row_of[:, None] * N_COL + local_rows // BLK_DEV) * BLK_DEV + local_rows % BLK_DEV
    second = (local_cols // BLK_DEV * N_COL + col_of[:, None]) * BLK_DEV + local_cols % BLK_DEV
    own = device[:, None] * BLK_DEV + jnp.arange(BLK_DEV, dtype=jnp.int32)[None, :]
    first = jnp.concatenate([first, own], axis=1).astype(jnp.int32)
    second = jnp.concatenate([second, own], axis=1).astype(jnp.int32)
    degree = sweep(blocked, first, second, None)
    total = jnp.sum(degree)
    scale = lax.rsqrt(degree)
    trivial = jnp.sqrt(degree / total)
    coef0 = jnp.einsum('vnb,nb->v', start, trivial, precision=lax.Precision.HIGHEST)
    spread = start - coef0[:, None, None] * trivial[None]
    factor, inverse = lower_inverse(inner(spread, spread))
    basis = jnp.einsum('vu,unb->vnb', inverse, spread, precision=lax.Precision.HIGHEST)
    previous = jnp.zeros_like(basis)
    beta = jnp.zeros((VECS, VECS), jnp.float32)
    alpha_list = []
    beta_list = []
    for step in range(STEPS):
        coef = jnp.einsum('vnb,nb->v', basis, trivial, precision=lax.Precision.HIGHEST)
        scaled = (scale[None] * basis).astype(jnp.bfloat16)
        image = scale[None] * sweep(blocked, first, second, scaled) - coef[:, None, None] * trivial[None]
        alpha = inner(basis, image)
        image = image - jnp.einsum('uv,unb->vnb', alpha, basis, precision=lax.Precision.HIGHEST)
        image = image - jnp.einsum('vu,unb->vnb', beta, previous, precision=lax.Precision.HIGHEST)
        factor, inverse = lower_inverse(inner(image, image))
        beta = factor.T
        previous = basis
        basis = jnp.einsum('vu,unb->vnb', inverse, image, precision=lax.Precision.HIGHEST)
        alpha_list.append(alpha)
        beta_list.append(beta)
    alphas = jnp.stack(alpha_list)
    betas = jnp.stack(beta_list)
    return (alphas, betas, basis * jnp.sqrt(jnp.float32(NSEG)))
```

```python
import functools
import math

import jax
import jax.numpy as jnp
from jax import lax
from jax.experimental import pallas as pl
from jax.experimental.pallas import tpu as pltpu
from jax.sharding import PartitionSpec as P

FEAT = 32
BLOCK = 128
VECS = 16
GROUP_UNROLL = 43
EXP2_SCALE = math.log2(math.e) / (2.0 * FEAT)
AXES = ("row", "col")
F32 = jnp.float32
BF16 = jnp.bfloat16
HIGHEST = lax.Precision.HIGHEST
VMEM = pltpu.VMEM


def params(mib):
    return pltpu.CompilerParams(vmem_limit_bytes=mib << 20)


def whole():
    return pl.BlockSpec(memory_space=pltpu.VMEM)


def smem():
    return pl.BlockSpec(memory_space=pltpu.SMEM)


def iota(shape, dim):
    return lax.broadcasted_iota(jnp.int32, shape, dim)


def split3(x):
    high = x.astype(BF16).astype(F32)
    rest = x - high
    middle = rest.astype(BF16).astype(F32)
    low = (rest - middle).astype(BF16).astype(F32)
    return high, middle, low


def dot(left, right):
    return jnp.dot(left, right, precision=HIGHEST, preferred_element_type=F32)


def dot_t(left, right):
    return lax.dot_general(
        left, right, (((1,), (1,)), ((), ())), precision=HIGHEST, preferred_element_type=F32
    )


def encode(small):
    high, middle, low = split3(small)
    return (high + pltpu.roll(middle, 40, 1) + pltpu.roll(low, 80, 1)).astype(BF16)


def decode(tiles):
    total = sum(tiles)
    value = total + pltpu.roll(total, 88, 1) + pltpu.roll(total, 48, 1)
    return jnp.where(iota((VECS, BLOCK), 1) < 40, value, 0.0)


def pad_lanes(small):
    return jnp.concatenate([small, jnp.zeros((VECS, BLOCK - small.shape[1]), F32)], axis=1)


def factor_inverse(gram):
    rows = iota((VECS, BLOCK), 0)
    lanes = iota((VECS, BLOCK), 1)
    work = pad_lanes(gram) + jnp.where(lanes == rows + VECS, 1.0, 0.0)
    for k in range(VECS):
        pivot_row = work[k : k + 1, :]
        ratio = work[:, k : k + 1] / pivot_row[:, k : k + 1]
        work = work - jnp.where(rows > k, ratio, 0.0) * pivot_row
    diagonal = jnp.sum(jnp.where(lanes == rows, work, 0.0), axis=1, keepdims=True)
    scaled = work * lax.rsqrt(diagonal)
    upper = jnp.where(lanes >= rows, scaled, 0.0)[:, :VECS]
    return upper, scaled[:, VECS : 2 * VECS]


def relay_out_kernel(slot_ref, desc_ref, out_ref, hot_ref, spread_ref):
    slots = slot_ref.shape[0] * BLOCK
    rows = out_ref.shape[0]
    target = iota((rows, BLOCK), 0)
    for t in range(slots // BLOCK):
        cut = pl.ds(t * BLOCK, BLOCK)
        slot = slot_ref[t : t + 1, :]
        hot_ref[:, cut] = jnp.where(target == (slot >> 2), 1.0, 0.0).astype(BF16)
        desc = desc_ref[:, cut].astype(F32)
        quarter = slot & 3
        for q in range(4):
            spread_ref[q * FEAT : (q + 1) * FEAT, cut] = jnp.where(quarter == q, desc, 0.0).astype(
                BF16
            )
    out_ref[...] = lax.dot_general(
        hot_ref[...], spread_ref[...], (((1,), (1,)), ((), ())), preferred_element_type=F32
    ).astype(BF16)


def relay_in_kernel(slot_ref, recv_ref, row_ref, col_ref):
    rows = recv_ref.shape[0]
    nblk = slot_ref.shape[0]
    received = recv_ref[...].astype(F32).T.astype(BF16)
    source = iota((rows, BLOCK), 0)
    for b in range(nblk):
        slot = slot_ref[b : b + 1, :]
        hot = jnp.where(source == (slot >> 2), 1.0, 0.0).astype(BF16)
        picked = jnp.dot(received, hot, preferred_element_type=F32)
        quarter = slot & 3
        own = jnp.zeros((FEAT, BLOCK), F32)
        for q in range(4):
            own = own + jnp.where(quarter == q, picked[q * FEAT : (q + 1) * FEAT, :], 0.0)
        own = own.astype(BF16)
        for copy in range(row_ref.shape[0] // nblk):
            row_ref[copy * nblk + b] = own
        for copy in range(col_ref.shape[0] // nblk):
            col_ref[copy * nblk + b] = own


def empty_kernel(out_ref):
    out_ref[0, 0:16, 0:BLOCK] = jnp.zeros((16, BLOCK), BF16)


def features(block, sign):
    values = block.astype(F32)
    pieces = split3(jnp.sum(values * values, axis=0, keepdims=True))
    rows = iota((BLOCK - FEAT, BLOCK), 0)
    tail = jnp.zeros((BLOCK - FEAT, BLOCK), F32)
    for n in range(3):
        if sign:
            tail = jnp.where(rows == n, -pieces[n], tail)
            tail = jnp.where(rows == n + 3, 1.0, tail)
        else:
            tail = jnp.where(rows == n, 1.0, tail)
            tail = jnp.where(rows == n + 3, -pieces[n], tail)
    scale = 2.0 if sign else 1.0
    return jnp.concatenate([values * scale, tail], axis=0).astype(BF16)


def build_kernel(
    row_idx, col_idx, row_desc, col_desc, unused, weights, degree, left, right, total, *, unroll
):
    nrow, ncol = row_desc.shape[0], col_desc.shape[0]
    eye = jnp.where(
        iota((BLOCK, BLOCK), 0) == iota((BLOCK, BLOCK), 1), 1.0, 0.0
    ).astype(BF16)

    def prepare_row(n, carry):
        for k in range(8):
            right[n * 8 + k] = features(row_desc[n * 8 + k], True)
            total[n * 8 + k] = jnp.zeros((8, BLOCK), F32)
        return carry

    def prepare_col(n, carry):
        for k in range(8):
            rows = features(col_desc[n * 8 + k], False)
            left[n * 8 + k] = lax.dot_general(
                eye, rows, (((1,), (1,)), ((), ())), preferred_element_type=F32
            ).astype(BF16)
        return carry

    lax.fori_loop(0, nrow // 8, prepare_row, 0)
    lax.fori_loop(0, ncol // 8, prepare_col, 0)

    def several(step, carry):
        for u in range(unroll):
            group = step * unroll + u
            for q in range(4):
                i = row_idx[group * 4 + q]
                j = col_idx[group * 4 + q]
                power = jnp.dot(left[j], right[i], preferred_element_type=F32)
                block = jnp.exp2(power * EXP2_SCALE).astype(BF16)
                r, c = q // 2, q % 2
                weights[group, r * BLOCK : (r + 1) * BLOCK, c * BLOCK : (c + 1) * BLOCK] = block
                total[i] += jnp.sum(block.astype(F32).reshape(BLOCK // 8, 8, BLOCK), axis=0)
        return carry

    lax.fori_loop(0, weights.shape[0] // unroll, several, 0)
    for n in range(nrow):
        degree[n // 8, n % 8 : n % 8 + 1, :] = jnp.sum(total[n], axis=0, keepdims=True)


def sweep_kernel(row_idx, col_idx, weights, vectors, out, total, *, unroll, peers):
    total[...] = jnp.zeros_like(total)
    zero = jnp.zeros((VECS, BLOCK), BF16)

    def several(step, carry):
        for u in range(unroll):
            group = step * unroll + u
            picked = [vectors[col_idx[group * 4 + q]] for q in range(4)]
            lhs = jnp.concatenate(
                [
                    jnp.concatenate([picked[0], zero], 1),
                    jnp.concatenate([zero, picked[2]], 1),
                    jnp.concatenate([picked[1], zero], 1),
                    jnp.concatenate([zero, picked[3]], 1),
                ],
                0,
            )
            result = jnp.dot(lhs, weights[group], preferred_element_type=F32)
            for place, q in enumerate((0, 2, 1, 3)):
                half = (q % 2) * BLOCK
                total[row_idx[group * 4 + q]] += result[
                    place * VECS : (place + 1) * VECS, half : half + BLOCK
                ]
        return carry

    lax.fori_loop(0, weights.shape[0] // unroll, several, 0)
    small = encode(decode([vectors[p * 9 + 8].astype(F32) for p in range(peers)]))
    for n in range(total.shape[0]):
        out[n // 8, n % 8] = total[n].astype(BF16)
    for p in range(out.shape[0]):
        out[p, 8] = small


def row_vector(block):
    return jnp.concatenate([block[b : b + 1, :] for b in range(8)], axis=1)


def send(out, vectors, small):
    tile = encode(small)
    for b in range(8):
        part = vectors[:, b * BLOCK : (b + 1) * BLOCK].astype(BF16)
        for p in range(out.shape[0] // 9):
            out[p * 9 + b] = part
    for p in range(out.shape[0] // 9):
        out[p * 9 + 8] = tile


def receive(recv):
    peers = recv.shape[0]
    tiles = []
    for b in range(8):
        tile = recv[0, b].astype(F32)
        for p in range(1, peers):
            tile = tile + recv[p, b].astype(F32)
        tiles.append(tile)
    return jnp.concatenate(tiles, axis=1), decode([recv[p, 8].astype(F32) for p in range(peers)])


def stacked(parts):
    width = parts[0].shape[1]
    return jnp.concatenate(parts + [jnp.zeros((7, width), F32)], axis=0)


def scale_kernel(degree_ref, start_ref, out, degree_out, start_out):
    degree = degree_ref[0]
    for p in range(1, degree_ref.shape[0]):
        degree = degree + degree_ref[p]
    flat = row_vector(degree)
    scale = lax.rsqrt(flat)
    start = jnp.concatenate([start_ref[:, b, :] for b in range(8)], axis=1)
    degree_out[...] = flat
    start_out[...] = start
    root = jnp.sqrt(flat)
    small = pad_lanes(dot_t(start, stacked([start, jnp.zeros_like(start), root])))
    whole_sum = jnp.sum(flat, axis=1, keepdims=True)
    first = (iota((VECS, BLOCK), 0) == 0) & (iota((VECS, BLOCK), 1) == 33)
    small = small + jnp.where(first, whole_sum, 0.0)
    send(out, start * scale, small)


def first_kernel(recv, degree_ref, start_ref, out, basis_out, image_out, trivial_out):
    swept, small = receive(recv)
    degree = degree_ref[...]
    scale = lax.rsqrt(degree)
    total = small[0:1, 33:34]
    trivial = jnp.sqrt(degree / total)
    coef = small[:, 32:33] * lax.rsqrt(total)
    lanes = iota((VECS, BLOCK), 1)
    wide = jnp.where(lanes == 0, coef, 0.0)
    gram = small[:, :VECS] - dot_t(wide, wide)
    upper, inverse = factor_inverse(gram)
    along = coef * trivial
    both = dot(
        inverse,
        jnp.concatenate([start_ref[...] - along, swept * scale - along], axis=1),
    )
    width = degree.shape[1]
    basis, image = both[:, :width], both[:, width:]
    basis_out[...] = basis
    image_out[...] = image
    trivial_out[...] = trivial
    send(out, image * scale, pad_lanes(dot_t(image, stacked([basis, image, trivial]))))


def second_kernel(
    recv, degree_ref, trivial_ref, basis_ref, image_ref, out, basis_out, image_out, rest_out, mats
):
    swept, small = receive(recv)
    scale = lax.rsqrt(degree_ref[...])
    trivial = trivial_ref[...]
    alpha_t = small[:, :VECS]
    gram = small[:, VECS : 2 * VECS] - dot_t(alpha_t, alpha_t)
    upper, inverse = factor_inverse(gram)
    width = trivial.shape[1]
    mixed = dot(alpha_t, jnp.concatenate([basis_ref[...], image_ref[...]], axis=1))
    residual = image_ref[...] - mixed[:, :width]
    applied = swept * scale - small[:, 2 * VECS : 2 * VECS + 1] * trivial - mixed[:, width:]
    both = dot(inverse, jnp.concatenate([residual, applied], axis=1))
    basis, image = both[:, :width], both[:, width:]
    rest = image - dot(upper, basis_ref[...])
    basis_out[...] = basis
    image_out[...] = image
    rest_out[...] = rest
    mats[0] = alpha_t
    mats[1] = upper
    send(out, rest * scale, pad_lanes(dot_t(rest, stacked([basis, rest, trivial]))))


def third_kernel(
    recv, degree_ref, trivial_ref, basis_ref, image_ref, rest_ref, out, basis_out, rest_out, mats
):
    swept, small = receive(recv)
    scale = lax.rsqrt(degree_ref[...])
    trivial = trivial_ref[...]
    alpha_t = small[:, :VECS]
    gram = small[:, VECS : 2 * VECS] - dot_t(alpha_t, alpha_t)
    upper, inverse = factor_inverse(gram)
    width = trivial.shape[1]
    mixed = dot(alpha_t, jnp.concatenate([basis_ref[...], image_ref[...]], axis=1))
    residual = rest_ref[...] - mixed[:, :width]
    applied = swept * scale - small[:, 2 * VECS : 2 * VECS + 1] * trivial - mixed[:, width:]
    both = dot(inverse, jnp.concatenate([residual, applied], axis=1))
    basis, image = both[:, :width], both[:, width:]
    rest = image - dot(upper, basis_ref[...])
    basis_out[...] = basis
    rest_out[...] = rest
    mats[0] = alpha_t
    mats[1] = upper
    small = pad_lanes(
        dot_t(rest, jnp.concatenate([basis, rest], axis=0))
    )
    packed = small[0:4, :]
    for q in range(1, 4):
        packed = packed + pltpu.roll(small[4 * q : 4 * q + 4, :], 32 * q, 1)
    for p in range(out.shape[0]):
        out[p] = packed


def last_kernel(recv, basis_ref, rest_ref, mats_a, mats_b, alphas, betas, out, *, norm):
    packed = jnp.sum(recv[...], axis=0)
    lanes = iota((4, BLOCK), 1)
    rows = []
    for q in range(4):
        part = packed if q == 0 else pltpu.roll(packed, BLOCK - 32 * q, 1)
        rows.append(jnp.where(lanes < 32, part, 0.0))
    small = jnp.concatenate(rows, axis=0)
    alpha_t = small[:, :VECS]
    gram = small[:, VECS : 2 * VECS] - dot_t(alpha_t, alpha_t)
    upper, inverse = factor_inverse(gram)
    final = dot(inverse * norm, rest_ref[...] - dot(alpha_t, basis_ref[...]))
    for b in range(8):
        out[:, b, :] = final[:, b * BLOCK : (b + 1) * BLOCK]
    alphas[0] = mats_a[0].T
    alphas[1] = mats_b[0].T
    alphas[2] = alpha_t.T
    betas[0] = mats_a[1]
    betas[1] = mats_b[1]
    betas[2] = upper


def call(kernel, out_shape, mib, *args, scratch=(), specs=None, out_specs=None, aliases=None):
    outs = out_shape if isinstance(out_shape, (list, tuple)) else None
    return pl.pallas_call(
        kernel,
        out_shape=out_shape,
        in_specs=specs or [whole()] * len(args),
        out_specs=out_specs or ([whole()] * len(outs) if outs else whole()),
        scratch_shapes=list(scratch),
        input_output_aliases=aliases or {},
        compiler_params=params(mib),
    )(*args)


def exchange(values, axis):
    return lax.all_to_all(values, axis, split_axis=0, concat_axis=0, tiled=True)


def shape(dims, dtype=F32):
    return jax.ShapeDtypeStruct(dims, dtype)


def on_device(descriptors, send_slot, recv_slot, block_pairs, start):
    rows = lax.axis_size("row")
    cols = lax.axis_size("col")
    count = rows * cols
    slots = descriptors.shape[1]
    seg = recv_slot.shape[0]
    nblk = seg // BLOCK
    nrow, ncol = cols * nblk, rows * nblk
    own = jnp.arange(nblk, dtype=jnp.int32)
    row_idx = jnp.concatenate([block_pairs[0], lax.axis_index("col") * nblk + own])
    col_idx = jnp.concatenate([block_pairs[1], lax.axis_index("row") * nblk + own])
    skip_idx = col_idx + col_idx // nblk
    groups = row_idx.shape[0] // 4
    unroll = GROUP_UNROLL if groups % GROUP_UNROLL == 0 else 1

    with jax.named_scope("relay"):
        packed_rows = slots // 4
        outgoing = call(
            relay_out_kernel,
            shape((packed_rows, BLOCK), BF16),
            16,
            send_slot.reshape(slots // BLOCK, BLOCK),
            descriptors,
            scratch=[VMEM((packed_rows, slots), BF16), VMEM((BLOCK, slots), BF16)],
        )
        received = exchange(outgoing, AXES)
        row_copies, col_copies = call(
            relay_in_kernel,
            [shape((nrow, FEAT, BLOCK), BF16), shape((ncol, FEAT, BLOCK), BF16)],
            16,
            recv_slot.reshape(nblk, BLOCK),
            received,
        )
    with jax.named_scope("gather"):
        row_desc = exchange(row_copies, "col")
        col_desc = exchange(col_copies, "row")
    with jax.named_scope("build"):
        wshape = pltpu.VMEM((groups, 2 * BLOCK, 2 * BLOCK), BF16)
        empty = pl.pallas_call(
            empty_kernel,
            out_shape=wshape,
            out_specs=pl.BlockSpec(memory_space=pltpu.VMEM),
            compiler_params=params(1),
        )()
        empty = pltpu.with_memory_space_constraint(empty, pltpu.VMEM)
        weights, degree_part = call(
            functools.partial(build_kernel, unroll=unroll),
            [wshape, shape((cols, nblk, BLOCK))],
            16,
            row_idx,
            col_idx,
            row_desc,
            col_desc,
            empty,
            scratch=[
                VMEM((ncol, BLOCK, BLOCK), BF16),
                VMEM((nrow, BLOCK, BLOCK), BF16),
                VMEM((nrow, 8, BLOCK), F32),
            ],
            specs=[smem(), smem(), whole(), whole(), pl.BlockSpec(memory_space=pl.ANY)],
            aliases={4: 0},
        )
        weights = pltpu.with_memory_space_constraint(weights, pltpu.VMEM)
    with jax.named_scope("degree"):
        sent, degree, begin = call(
            scale_kernel,
            [shape((rows * 9, VECS, BLOCK), BF16), shape((1, seg)), shape((VECS, seg))],
            8,
            exchange(degree_part, "col"),
            start,
        )

    def sweep(sent):
        vectors = exchange(sent, "row")
        partial_sum = call(
            functools.partial(sweep_kernel, unroll=unroll, peers=rows),
            shape((cols, 9, VECS, BLOCK), BF16),
            8,
            row_idx,
            skip_idx,
            weights,
            vectors,
            scratch=[VMEM((nrow, VECS, BLOCK), F32)],
            specs=[smem(), smem(), whole(), whole()],
        )
        return exchange(partial_sum, "col")

    vec = shape((VECS, seg))
    sending = shape((rows * 9, VECS, BLOCK), BF16)
    mats = shape((2, VECS, VECS))
    with jax.named_scope("step0"):
        swept = sweep(sent)
        sent, basis0, image0, trivial = call(
            first_kernel, [sending, vec, vec, shape((1, seg))], 8, swept, degree, begin
        )
    with jax.named_scope("step1"):
        swept = sweep(sent)
        sent, basis1, image1, rest1, mats0 = call(
            second_kernel, [sending, vec, vec, vec, mats], 8, swept, degree, trivial, basis0, image0
        )
    with jax.named_scope("step2"):
        swept = sweep(sent)
        small, basis2, rest2, mats1 = call(
            third_kernel,
            [shape((count, 4, BLOCK)), vec, vec, mats],
            8,
            swept,
            degree,
            trivial,
            basis1,
            image1,
            rest1,
        )
    with jax.named_scope("finish"):
        three = shape((3, VECS, VECS))
        return tuple(
            call(
                functools.partial(last_kernel, norm=math.sqrt(count * seg)),
                [three, three, shape((VECS, nblk, BLOCK))],
                8,
                exchange(small, AXES),
                basis2,
                rest2,
                mats0,
                mats1,
            )
        )


def solution(mesh):
    return jax.shard_map(
        on_device,
        mesh=mesh,
        in_specs=(
            P(None, ("row", "col")),
            P(("row", "col")),
            P(("row", "col")),
            P(None, ("row", "col")),
            P(None, ("row", "col"), None),
        ),
        out_specs=(P(), P(), P(None, ("row", "col"), None)),
        check_vma=False,
    )
```

```python
import functools
import math

import jax
import jax.numpy as jnp
from jax import lax
from jax.experimental import pallas as pl
from jax.experimental.pallas import tpu as pltpu
from jax.sharding import PartitionSpec as P

FEAT = 32
BLOCK = 128
VECS = 16
GROUP_UNROLL = 43
PIECES = 2
EXP2_SCALE = math.log2(math.e) / (2.0 * FEAT)
AXES = ("row", "col")
F32 = jnp.float32
BF16 = jnp.bfloat16
HIGHEST = lax.Precision.HIGHEST
VMEM = pltpu.VMEM


def params(mib):
    return pltpu.CompilerParams(vmem_limit_bytes=mib << 20)


def whole():
    return pl.BlockSpec(memory_space=pltpu.VMEM)


def smem():
    return pl.BlockSpec(memory_space=pltpu.SMEM)


def iota(shape, dim):
    return lax.broadcasted_iota(jnp.int32, shape, dim)


def split3(x):
    high = x.astype(BF16).astype(F32)
    rest = x - high
    middle = rest.astype(BF16).astype(F32)
    low = (rest - middle).astype(BF16).astype(F32)
    return high, middle, low


def dot(left, right):
    return jnp.dot(left, right, precision=HIGHEST, preferred_element_type=F32)


def dot_t(left, right):
    return lax.dot_general(
        left, right, (((1,), (1,)), ((), ())), precision=HIGHEST, preferred_element_type=F32
    )


def encode(small):
    high, middle, low = split3(small)
    return (high + pltpu.roll(middle, 40, 1) + pltpu.roll(low, 80, 1)).astype(BF16)


def decode(tiles):
    total = sum(tiles)
    value = total + pltpu.roll(total, 88, 1) + pltpu.roll(total, 48, 1)
    return jnp.where(iota((VECS, BLOCK), 1) < 40, value, 0.0)


def pad_lanes(small):
    return jnp.concatenate([small, jnp.zeros((VECS, BLOCK - small.shape[1]), F32)], axis=1)


def factor_inverse(gram):
    rows = iota((VECS, BLOCK), 0)
    lanes = iota((VECS, BLOCK), 1)
    work = pad_lanes(gram) + jnp.where(lanes == rows + VECS, 1.0, 0.0)
    for k in range(VECS):
        pivot_row = work[k : k + 1, :]
        ratio = work[:, k : k + 1] / pivot_row[:, k : k + 1]
        work = work - jnp.where(rows > k, ratio, 0.0) * pivot_row
    diagonal = jnp.sum(jnp.where(lanes == rows, work, 0.0), axis=1, keepdims=True)
    scaled = work * lax.rsqrt(diagonal)
    upper = jnp.where(lanes >= rows, scaled, 0.0)[:, :VECS]
    return upper, scaled[:, VECS : 2 * VECS]


def relay_out_kernel(slot_ref, desc_ref, out_ref, hot_ref, spread_ref):
    slots = slot_ref.shape[0] * BLOCK
    rows = out_ref.shape[0]
    target = iota((rows, BLOCK), 0)
    for t in range(slots // BLOCK):
        cut = pl.ds(t * BLOCK, BLOCK)
        slot = slot_ref[t : t + 1, :]
        hot_ref[:, cut] = jnp.where(target == (slot >> 2), 1.0, 0.0).astype(BF16)
        desc = desc_ref[:, cut].astype(F32)
        quarter = slot & 3
        for q in range(4):
            spread_ref[q * FEAT : (q + 1) * FEAT, cut] = jnp.where(quarter == q, desc, 0.0).astype(
                BF16
            )
    out_ref[...] = lax.dot_general(
        hot_ref[...], spread_ref[...], (((1,), (1,)), ((), ())), preferred_element_type=F32
    ).astype(BF16)


def relay_in_kernel(slot_ref, recv_ref, row_ref, col_ref):
    rows = recv_ref.shape[0]
    nblk = slot_ref.shape[0]
    received = recv_ref[...].astype(F32).T.astype(BF16)
    source = iota((rows, BLOCK), 0)
    for b in range(nblk):
        slot = slot_ref[b : b + 1, :]
        hot = jnp.where(source == (slot >> 2), 1.0, 0.0).astype(BF16)
        picked = jnp.dot(received, hot, preferred_element_type=F32)
        quarter = slot & 3
        own = jnp.zeros((FEAT, BLOCK), F32)
        for q in range(4):
            own = own + jnp.where(quarter == q, picked[q * FEAT : (q + 1) * FEAT, :], 0.0)
        own = own.astype(BF16)
        for copy in range(row_ref.shape[0] // nblk):
            row_ref[copy * nblk + b] = own
        for copy in range(col_ref.shape[0] // nblk):
            col_ref[copy * nblk + b] = own


def empty_kernel(*refs):
    for ref in refs[-PIECES:]:
        ref[0, 0:16, 0:BLOCK] = jnp.zeros((16, BLOCK), BF16)


def features(block, sign):
    values = block.astype(F32)
    pieces = split3(jnp.sum(values * values, axis=0, keepdims=True))
    rows = iota((BLOCK - FEAT, BLOCK), 0)
    tail = jnp.zeros((BLOCK - FEAT, BLOCK), F32)
    for n in range(3):
        if sign:
            tail = jnp.where(rows == n, -pieces[n], tail)
            tail = jnp.where(rows == n + 3, 1.0, tail)
        else:
            tail = jnp.where(rows == n, 1.0, tail)
            tail = jnp.where(rows == n + 3, -pieces[n], tail)
    scale = 2.0 if sign else 1.0
    return jnp.concatenate([values * scale, tail], axis=0).astype(BF16)


def each_piece(pieces, body, unroll):
    first = 0
    for weights in pieces:
        count = weights.shape[0]
        lax.fori_loop(0, count // unroll, functools.partial(body, weights=weights, first=first), 0)
        first += count


def build_kernel(row_idx, col_idx, row_desc, col_desc, *refs, unroll):
    pieces = refs[PIECES : 2 * PIECES]
    degree, left, right, total = refs[2 * PIECES :]
    nrow, ncol = row_desc.shape[0], col_desc.shape[0]
    eye = jnp.where(
        iota((BLOCK, BLOCK), 0) == iota((BLOCK, BLOCK), 1), 1.0, 0.0
    ).astype(BF16)

    def prepare_row(n, carry):
        for k in range(8):
            right[n * 8 + k] = features(row_desc[n * 8 + k], True)
            total[n * 8 + k] = jnp.zeros((8, BLOCK), F32)
        return carry

    def prepare_col(n, carry):
        for k in range(8):
            rows = features(col_desc[n * 8 + k], False)
            left[n * 8 + k] = lax.dot_general(
                eye, rows, (((1,), (1,)), ((), ())), preferred_element_type=F32
            ).astype(BF16)
        return carry

    lax.fori_loop(0, nrow // 8, prepare_row, 0)
    lax.fori_loop(0, ncol // 8, prepare_col, 0)

    def several(step, carry, weights, first):
        for u in range(unroll):
            group = step * unroll + u
            for q in range(4):
                i = row_idx[(first + group) * 4 + q]
                j = col_idx[(first + group) * 4 + q]
                power = jnp.dot(left[j], right[i], preferred_element_type=F32)
                block = jnp.exp2(power * EXP2_SCALE).astype(BF16)
                r, c = q // 2, q % 2
                weights[group, r * BLOCK : (r + 1) * BLOCK, c * BLOCK : (c + 1) * BLOCK] = block
                total[i] += jnp.sum(block.astype(F32).reshape(BLOCK // 8, 8, BLOCK), axis=0)
        return carry

    each_piece(pieces, several, unroll)
    for n in range(nrow):
        degree[n // 8, n % 8 : n % 8 + 1, :] = jnp.sum(total[n], axis=0, keepdims=True)


def sweep_kernel(row_idx, col_idx, *refs, unroll, peers):
    pieces = refs[:PIECES]
    vectors, out, total = refs[PIECES:]
    total[...] = jnp.zeros_like(total)
    zero = jnp.zeros((VECS, BLOCK), BF16)

    def several(step, carry, weights, first):
        for u in range(unroll):
            group = step * unroll + u
            picked = [vectors[col_idx[(first + group) * 4 + q]] for q in range(4)]
            lhs = jnp.concatenate(
                [
                    jnp.concatenate([picked[0], zero], 1),
                    jnp.concatenate([zero, picked[2]], 1),
                    jnp.concatenate([picked[1], zero], 1),
                    jnp.concatenate([zero, picked[3]], 1),
                ],
                0,
            )
            result = jnp.dot(lhs, weights[group], preferred_element_type=F32)
            for place, q in enumerate((0, 2, 1, 3)):
                half = (q % 2) * BLOCK
                total[row_idx[(first + group) * 4 + q]] += result[
                    place * VECS : (place + 1) * VECS, half : half + BLOCK
                ]
        return carry

    each_piece(pieces, several, unroll)
    small = encode(decode([vectors[p * 9 + 8].astype(F32) for p in range(peers)]))
    for n in range(total.shape[0]):
        out[n // 8, n % 8] = total[n].astype(BF16)
    for p in range(out.shape[0]):
        out[p, 8] = small


def row_vector(block):
    return jnp.concatenate([block[b : b + 1, :] for b in range(8)], axis=1)


def send(out, vectors, small):
    tile = encode(small)
    for b in range(8):
        part = vectors[:, b * BLOCK : (b + 1) * BLOCK].astype(BF16)
        for p in range(out.shape[0] // 9):
            out[p * 9 + b] = part
    for p in range(out.shape[0] // 9):
        out[p * 9 + 8] = tile


def receive(recv):
    peers = recv.shape[0]
    tiles = []
    for b in range(8):
        tile = recv[0, b].astype(F32)
        for p in range(1, peers):
            tile = tile + recv[p, b].astype(F32)
        tiles.append(tile)
    return jnp.concatenate(tiles, axis=1), decode([recv[p, 8].astype(F32) for p in range(peers)])


def stacked(parts):
    width = parts[0].shape[1]
    return jnp.concatenate(parts + [jnp.zeros((7, width), F32)], axis=0)


def scale_kernel(degree_ref, start_ref, out, degree_out, start_out):
    degree = degree_ref[0]
    for p in range(1, degree_ref.shape[0]):
        degree = degree + degree_ref[p]
    flat = row_vector(degree)
    scale = lax.rsqrt(flat)
    start = jnp.concatenate([start_ref[:, b, :] for b in range(8)], axis=1)
    degree_out[...] = flat
    start_out[...] = start
    root = jnp.sqrt(flat)
    small = pad_lanes(dot_t(start, stacked([start, jnp.zeros_like(start), root])))
    whole_sum = jnp.sum(flat, axis=1, keepdims=True)
    first = (iota((VECS, BLOCK), 0) == 0) & (iota((VECS, BLOCK), 1) == 33)
    small = small + jnp.where(first, whole_sum, 0.0)
    send(out, start * scale, small)


def first_kernel(recv, degree_ref, start_ref, out, basis_out, image_out, trivial_out):
    swept, small = receive(recv)
    degree = degree_ref[...]
    scale = lax.rsqrt(degree)
    total = small[0:1, 33:34]
    trivial = jnp.sqrt(degree / total)
    coef = small[:, 32:33] * lax.rsqrt(total)
    lanes = iota((VECS, BLOCK), 1)
    wide = jnp.where(lanes == 0, coef, 0.0)
    gram = small[:, :VECS] - dot_t(wide, wide)
    upper, inverse = factor_inverse(gram)
    along = coef * trivial
    both = dot(
        inverse,
        jnp.concatenate([start_ref[...] - along, swept * scale - along], axis=1),
    )
    width = degree.shape[1]
    basis, image = both[:, :width], both[:, width:]
    basis_out[...] = basis
    image_out[...] = image
    trivial_out[...] = trivial
    send(out, image * scale, pad_lanes(dot_t(image, stacked([basis, image, trivial]))))


def second_kernel(
    recv, degree_ref, trivial_ref, basis_ref, image_ref, out, basis_out, image_out, rest_out, mats
):
    swept, small = receive(recv)
    scale = lax.rsqrt(degree_ref[...])
    trivial = trivial_ref[...]
    alpha_t = small[:, :VECS]
    gram = small[:, VECS : 2 * VECS] - dot_t(alpha_t, alpha_t)
    upper, inverse = factor_inverse(gram)
    width = trivial.shape[1]
    mixed = dot(alpha_t, jnp.concatenate([basis_ref[...], image_ref[...]], axis=1))
    residual = image_ref[...] - mixed[:, :width]
    applied = swept * scale - small[:, 2 * VECS : 2 * VECS + 1] * trivial - mixed[:, width:]
    both = dot(inverse, jnp.concatenate([residual, applied], axis=1))
    basis, image = both[:, :width], both[:, width:]
    rest = image - dot(upper, basis_ref[...])
    basis_out[...] = basis
    image_out[...] = image
    rest_out[...] = rest
    mats[0] = alpha_t
    mats[1] = upper
    send(out, rest * scale, pad_lanes(dot_t(rest, stacked([basis, rest, trivial]))))


def third_kernel(
    recv, degree_ref, trivial_ref, basis_ref, image_ref, rest_ref, out, basis_out, rest_out, mats
):
    swept, small = receive(recv)
    scale = lax.rsqrt(degree_ref[...])
    trivial = trivial_ref[...]
    alpha_t = small[:, :VECS]
    gram = small[:, VECS : 2 * VECS] - dot_t(alpha_t, alpha_t)
    upper, inverse = factor_inverse(gram)
    width = trivial.shape[1]
    mixed = dot(alpha_t, jnp.concatenate([basis_ref[...], image_ref[...]], axis=1))
    residual = rest_ref[...] - mixed[:, :width]
    applied = swept * scale - small[:, 2 * VECS : 2 * VECS + 1] * trivial - mixed[:, width:]
    both = dot(inverse, jnp.concatenate([residual, applied], axis=1))
    basis, image = both[:, :width], both[:, width:]
    rest = image - dot(upper, basis_ref[...])
    basis_out[...] = basis
    rest_out[...] = rest
    mats[0] = alpha_t
    mats[1] = upper
    small = pad_lanes(
        dot_t(rest, jnp.concatenate([basis, rest], axis=0))
    )
    packed = small[0:4, :]
    for q in range(1, 4):
        packed = packed + pltpu.roll(small[4 * q : 4 * q + 4, :], 32 * q, 1)
    for p in range(out.shape[0]):
        out[p] = packed


def last_kernel(recv, basis_ref, rest_ref, mats_a, mats_b, alphas, betas, out, *, norm):
    packed = jnp.sum(recv[...], axis=0)
    lanes = iota((4, BLOCK), 1)
    rows = []
    for q in range(4):
        part = packed if q == 0 else pltpu.roll(packed, BLOCK - 32 * q, 1)
        rows.append(jnp.where(lanes < 32, part, 0.0))
    small = jnp.concatenate(rows, axis=0)
    alpha_t = small[:, :VECS]
    gram = small[:, VECS : 2 * VECS] - dot_t(alpha_t, alpha_t)
    upper, inverse = factor_inverse(gram)
    final = dot(inverse * norm, rest_ref[...] - dot(alpha_t, basis_ref[...]))
    for b in range(8):
        out[:, b, :] = final[:, b * BLOCK : (b + 1) * BLOCK]
    alphas[0] = mats_a[0].T
    alphas[1] = mats_b[0].T
    alphas[2] = alpha_t.T
    betas[0] = mats_a[1]
    betas[1] = mats_b[1]
    betas[2] = upper


def call(kernel, out_shape, mib, *args, scratch=(), specs=None, out_specs=None, aliases=None):
    outs = out_shape if isinstance(out_shape, (list, tuple)) else None
    return pl.pallas_call(
        kernel,
        out_shape=out_shape,
        in_specs=specs or [whole()] * len(args),
        out_specs=out_specs or ([whole()] * len(outs) if outs else whole()),
        scratch_shapes=list(scratch),
        input_output_aliases=aliases or {},
        compiler_params=params(mib),
    )(*args)


def exchange(values, axis):
    return lax.all_to_all(values, axis, split_axis=0, concat_axis=0, tiled=True)


def shape(dims, dtype=F32):
    return jax.ShapeDtypeStruct(dims, dtype)


def on_device(descriptors, send_slot, recv_slot, block_pairs, start):
    rows = lax.axis_size("row")
    cols = lax.axis_size("col")
    count = rows * cols
    slots = descriptors.shape[1]
    seg = recv_slot.shape[0]
    nblk = seg // BLOCK
    nrow, ncol = cols * nblk, rows * nblk
    own = jnp.arange(nblk, dtype=jnp.int32)
    row_idx = jnp.concatenate([block_pairs[0], lax.axis_index("col") * nblk + own])
    col_idx = jnp.concatenate([block_pairs[1], lax.axis_index("row") * nblk + own])
    skip_idx = col_idx + col_idx // nblk
    groups = row_idx.shape[0] // 4
    unroll = math.gcd(GROUP_UNROLL, groups // PIECES)

    with jax.named_scope("relay"):
        packed_rows = slots // 4
        outgoing = call(
            relay_out_kernel,
            shape((packed_rows, BLOCK), BF16),
            16,
            send_slot.reshape(slots // BLOCK, BLOCK),
            descriptors,
            scratch=[VMEM((packed_rows, slots), BF16), VMEM((BLOCK, slots), BF16)],
        )
        received = exchange(outgoing, AXES)
        row_copies, col_copies = call(
            relay_in_kernel,
            [shape((nrow, FEAT, BLOCK), BF16), shape((ncol, FEAT, BLOCK), BF16)],
            16,
            recv_slot.reshape(nblk, BLOCK),
            received,
        )
    with jax.named_scope("gather"):
        row_desc = exchange(row_copies, "col")
        col_desc = exchange(col_copies, "row")
    with jax.named_scope("build"):
        wshape = pltpu.VMEM((groups // PIECES, 2 * BLOCK, 2 * BLOCK), BF16)
        empty = call(
            empty_kernel,
            [wshape] * PIECES,
            1,
            row_desc,
            col_desc,
            row_idx,
            col_idx,
            skip_idx,
            specs=[pl.BlockSpec(memory_space=pl.ANY)] * 5,
        )
        empty = [pltpu.with_memory_space_constraint(piece, pltpu.VMEM) for piece in empty]
        *weights, degree_part = call(
            functools.partial(build_kernel, unroll=unroll),
            [wshape] * PIECES + [shape((cols, nblk, BLOCK))],
            8,
            row_idx,
            col_idx,
            row_desc,
            col_desc,
            *empty,
            scratch=[
                VMEM((ncol, BLOCK, BLOCK), BF16),
                VMEM((nrow, BLOCK, BLOCK), BF16),
                VMEM((nrow, 8, BLOCK), F32),
            ],
            specs=[smem(), smem(), whole(), whole()] + [pl.BlockSpec(memory_space=pl.ANY)] * PIECES,
            aliases={4 + k: k for k in range(PIECES)},
        )
        weights = [pltpu.with_memory_space_constraint(piece, pltpu.VMEM) for piece in weights]
    with jax.named_scope("degree"):
        sent, degree, begin = call(
            scale_kernel,
            [shape((rows * 9, VECS, BLOCK), BF16), shape((1, seg)), shape((VECS, seg))],
            8,
            exchange(degree_part, "col"),
            start,
        )

    def sweep(sent):
        vectors = exchange(sent, "row")
        partial_sum = call(
            functools.partial(sweep_kernel, unroll=unroll, peers=rows),
            shape((cols, 9, VECS, BLOCK), BF16),
            8,
            row_idx,
            skip_idx,
            *weights,
            vectors,
            scratch=[VMEM((nrow, VECS, BLOCK), F32)],
            specs=[smem(), smem()] + [whole()] * (PIECES + 1),
        )
        return exchange(partial_sum, "col")

    vec = shape((VECS, seg))
    sending = shape((rows * 9, VECS, BLOCK), BF16)
    mats = shape((2, VECS, VECS))
    with jax.named_scope("step0"):
        swept = sweep(sent)
        sent, basis0, image0, trivial = call(
            first_kernel, [sending, vec, vec, shape((1, seg))], 8, swept, degree, begin
        )
    with jax.named_scope("step1"):
        swept = sweep(sent)
        sent, basis1, image1, rest1, mats0 = call(
            second_kernel, [sending, vec, vec, vec, mats], 8, swept, degree, trivial, basis0, image0
        )
    with jax.named_scope("step2"):
        swept = sweep(sent)
        small, basis2, rest2, mats1 = call(
            third_kernel,
            [shape((count, 4, BLOCK)), vec, vec, mats],
            8,
            swept,
            degree,
            trivial,
            basis1,
            image1,
            rest1,
        )
    with jax.named_scope("finish"):
        three = shape((3, VECS, VECS))
        return tuple(
            call(
                functools.partial(last_kernel, norm=math.sqrt(count * seg)),
                [three, three, shape((VECS, nblk, BLOCK))],
                8,
                exchange(small, AXES),
                basis2,
                rest2,
                mats0,
                mats1,
            )
        )


def solution(mesh):
    return jax.shard_map(
        on_device,
        mesh=mesh,
        in_specs=(
            P(None, ("row", "col")),
            P(("row", "col")),
            P(("row", "col")),
            P(None, ("row", "col")),
            P(None, ("row", "col"), None),
        ),
        out_specs=(P(), P(), P(None, ("row", "col"), None)),
        check_vma=False,
    )
```

```python
import functools
import math

import jax
import jax.numpy as jnp
from jax import lax
from jax.experimental import pallas as pl
from jax.experimental.pallas import tpu as pltpu
from jax.sharding import PartitionSpec as P

FEAT = 32
BLOCK = 128
VECS = 16
GROUP_UNROLL = 43
PIECES = 2
EXP2_SCALE = math.log2(math.e) / (2.0 * FEAT)
AXES = ("row", "col")
F32 = jnp.float32
BF16 = jnp.bfloat16
HIGHEST = lax.Precision.HIGHEST
VMEM = pltpu.VMEM


def params(mib):
    return pltpu.CompilerParams(vmem_limit_bytes=mib << 20)


def whole():
    return pl.BlockSpec(memory_space=pltpu.VMEM)


def smem():
    return pl.BlockSpec(memory_space=pltpu.SMEM)


def iota(shape, dim):
    return lax.broadcasted_iota(jnp.int32, shape, dim)


def split3(x):
    high = x.astype(BF16).astype(F32)
    rest = x - high
    middle = rest.astype(BF16).astype(F32)
    low = (rest - middle).astype(BF16).astype(F32)
    return high, middle, low


def dot(left, right):
    return jnp.dot(left, right, precision=HIGHEST, preferred_element_type=F32)


def dot_t(left, right):
    return lax.dot_general(
        left, right, (((1,), (1,)), ((), ())), precision=HIGHEST, preferred_element_type=F32
    )


def encode(small):
    high, middle, low = split3(small)
    return (high + pltpu.roll(middle, 40, 1) + pltpu.roll(low, 80, 1)).astype(BF16)


def decode(tiles):
    total = sum(tiles)
    value = total + pltpu.roll(total, 88, 1) + pltpu.roll(total, 48, 1)
    return jnp.where(iota((VECS, BLOCK), 1) < 40, value, 0.0)


def pad_lanes(small):
    return jnp.concatenate([small, jnp.zeros((VECS, BLOCK - small.shape[1]), F32)], axis=1)


def factor_inverse(gram):
    rows = iota((VECS, BLOCK), 0)
    lanes = iota((VECS, BLOCK), 1)
    work = pad_lanes(gram) + jnp.where(lanes == rows + VECS, 1.0, 0.0)
    for k in range(0, VECS, 2):
        upper_row, lower_row = work[k : k + 1, :], work[k + 1 : k + 2, :]
        corner, beside = upper_row[:, k : k + 1], upper_row[:, k + 1 : k + 2]
        low_corner = lower_row[:, k + 1 : k + 2]
        inverse = 1.0 / corner
        lower_row = lower_row - (beside * inverse) * upper_row
        low_inverse = 1.0 / (low_corner - beside * inverse * beside)
        ratio = work[:, k : k + 1] * inverse
        low_ratio = (work[:, k + 1 : k + 2] - ratio * beside) * low_inverse
        work = (
            work
            - jnp.where(rows > k, ratio, 0.0) * upper_row
            - jnp.where(rows > k + 1, low_ratio, 0.0) * lower_row
        )
    diagonal = jnp.sum(jnp.where(lanes == rows, work, 0.0), axis=1, keepdims=True)
    scaled = work * lax.rsqrt(diagonal)
    upper = jnp.where(lanes >= rows, scaled, 0.0)[:, :VECS]
    return upper, scaled[:, VECS : 2 * VECS]


def relay_out_kernel(slot_ref, desc_ref, out_ref, hot_ref, spread_ref):
    slots = slot_ref.shape[0] * BLOCK
    rows = out_ref.shape[0]
    target = iota((rows, BLOCK), 0)
    for t in range(slots // BLOCK):
        cut = pl.ds(t * BLOCK, BLOCK)
        slot = slot_ref[t : t + 1, :]
        hot_ref[:, cut] = jnp.where(target == (slot >> 2), 1.0, 0.0).astype(BF16)
        desc = desc_ref[:, cut].astype(F32)
        quarter = slot & 3
        for q in range(4):
            spread_ref[q * FEAT : (q + 1) * FEAT, cut] = jnp.where(quarter == q, desc, 0.0).astype(
                BF16
            )
    out_ref[...] = lax.dot_general(
        hot_ref[...], spread_ref[...], (((1,), (1,)), ((), ())), preferred_element_type=F32
    ).astype(BF16)


def relay_in_kernel(slot_ref, recv_ref, row_ref, own_ref):
    rows = recv_ref.shape[0]
    nblk = slot_ref.shape[0]
    received = recv_ref[...].astype(F32).T.astype(BF16)
    source = iota((rows, BLOCK), 0)
    for b in range(nblk):
        slot = slot_ref[b : b + 1, :]
        hot = jnp.where(source == (slot >> 2), 1.0, 0.0).astype(BF16)
        picked = jnp.dot(received, hot, preferred_element_type=F32)
        quarter = slot & 3
        own = jnp.zeros((FEAT, BLOCK), F32)
        for q in range(4):
            own = own + jnp.where(quarter == q, picked[q * FEAT : (q + 1) * FEAT, :], 0.0)
        own = own.astype(BF16)
        for copy in range(row_ref.shape[0] // nblk):
            row_ref[copy * nblk + b] = own
        own_ref[b] = own


def empty_kernel(*refs):
    for ref in refs[-PIECES:]:
        ref[0, 0:16, 0:BLOCK] = jnp.zeros((16, BLOCK), BF16)


def features(block, sign):
    values = block.astype(F32)
    pieces = split3(jnp.sum(values * values, axis=0, keepdims=True))
    rows = iota((BLOCK - FEAT, BLOCK), 0)
    tail = jnp.zeros((BLOCK - FEAT, BLOCK), F32)
    for n in range(3):
        if sign:
            tail = jnp.where(rows == n, -pieces[n], tail)
            tail = jnp.where(rows == n + 3, 1.0, tail)
        else:
            tail = jnp.where(rows == n, 1.0, tail)
            tail = jnp.where(rows == n + 3, -pieces[n], tail)
    scale = 2.0 if sign else 1.0
    return jnp.concatenate([values * scale, tail], axis=0).astype(BF16)


def each_piece(pieces, body, unroll):
    first = 0
    for weights in pieces:
        count = weights.shape[0]
        lax.fori_loop(0, count // unroll, functools.partial(body, weights=weights, first=first), 0)
        first += count


def build_kernel(row_idx, col_idx, row_desc, *refs, unroll, peers):
    col_desc = refs[:peers]
    pieces = refs[peers + PIECES : peers + 2 * PIECES]
    degree, left, right, total = refs[peers + 2 * PIECES :]
    nrow, nblk = row_desc.shape[0], col_desc[0].shape[0]
    me = row_idx[row_idx.shape[0] - 1]
    eye = jnp.where(
        iota((BLOCK, BLOCK), 0) == iota((BLOCK, BLOCK), 1), 1.0, 0.0
    ).astype(BF16)

    def prepare_row(n, carry):
        for k in range(8):
            right[n * 8 + k] = features(row_desc[n * 8 + k], True)
            total[n * 8 + k] = jnp.zeros((8, BLOCK), F32)
        return carry

    for m in range(peers):
        for k in range(nblk):
            rows = features(col_desc[m][k], False)
            left[(me ^ m) * nblk + k] = lax.dot_general(
                eye, rows, (((1,), (1,)), ((), ())), preferred_element_type=F32
            ).astype(BF16)

    lax.fori_loop(0, nrow // 8, prepare_row, 0)

    def several(step, carry, weights, first):
        for u in range(unroll):
            group = step * unroll + u
            for q in range(4):
                i = row_idx[(first + group) * 4 + q]
                j = col_idx[(first + group) * 4 + q]
                power = jnp.dot(left[j], right[i], preferred_element_type=F32)
                block = jnp.exp2(power * EXP2_SCALE).astype(BF16)
                r, c = q // 2, q % 2
                weights[group, r * BLOCK : (r + 1) * BLOCK, c * BLOCK : (c + 1) * BLOCK] = block
                total[i] += jnp.sum(block.astype(F32).reshape(BLOCK // 8, 8, BLOCK), axis=0)
        return carry

    each_piece(pieces, several, unroll)
    for n in range(nrow):
        degree[n // 8, n % 8 : n % 8 + 1, :] = jnp.sum(total[n], axis=0, keepdims=True)


def sweep_kernel(row_idx, col_idx, *refs, unroll, peers):
    pieces = refs[:PIECES]
    vectors, out, total = refs[PIECES:]
    total[...] = jnp.zeros_like(total)
    zero = jnp.zeros((VECS, BLOCK), BF16)

    def several(step, carry, weights, first):
        for u in range(unroll):
            group = step * unroll + u
            picked = [vectors[col_idx[(first + group) * 4 + q]] for q in range(4)]
            lhs = jnp.concatenate(
                [
                    jnp.concatenate([picked[0], zero], 1),
                    jnp.concatenate([zero, picked[2]], 1),
                    jnp.concatenate([picked[1], zero], 1),
                    jnp.concatenate([zero, picked[3]], 1),
                ],
                0,
            )
            result = jnp.dot(lhs, weights[group], preferred_element_type=F32)
            for place, q in enumerate((0, 2, 1, 3)):
                half = (q % 2) * BLOCK
                total[row_idx[(first + group) * 4 + q]] += result[
                    place * VECS : (place + 1) * VECS, half : half + BLOCK
                ]
        return carry

    each_piece(pieces, several, unroll)
    small = encode(decode([vectors[p * 9 + 8].astype(F32) for p in range(peers)]))
    for n in range(total.shape[0]):
        out[n // 8, n % 8] = total[n].astype(BF16)
    for p in range(out.shape[0]):
        out[p, 8] = small


def row_vector(block):
    return jnp.concatenate([block[b : b + 1, :] for b in range(8)], axis=1)


def send(out, vectors, small):
    tile = encode(small)
    for b in range(8):
        part = vectors[:, b * BLOCK : (b + 1) * BLOCK].astype(BF16)
        for p in range(out.shape[0] // 9):
            out[p * 9 + b] = part
    for p in range(out.shape[0] // 9):
        out[p * 9 + 8] = tile


def receive(recv):
    peers = recv.shape[0]
    tiles = []
    for b in range(8):
        tile = recv[0, b].astype(F32)
        for p in range(1, peers):
            tile = tile + recv[p, b].astype(F32)
        tiles.append(tile)
    return jnp.concatenate(tiles, axis=1), decode([recv[p, 8].astype(F32) for p in range(peers)])


def stacked(parts):
    width = parts[0].shape[1]
    return jnp.concatenate(parts + [jnp.zeros((7, width), F32)], axis=0)


def scale_kernel(degree_ref, start_ref, out, degree_out, start_out):
    degree = degree_ref[0]
    for p in range(1, degree_ref.shape[0]):
        degree = degree + degree_ref[p]
    flat = row_vector(degree)
    scale = lax.rsqrt(flat)
    start = jnp.concatenate([start_ref[:, b, :] for b in range(8)], axis=1)
    degree_out[...] = flat
    start_out[...] = start
    root = jnp.sqrt(flat)
    small = pad_lanes(dot_t(start, stacked([start, jnp.zeros_like(start), root])))
    whole_sum = jnp.sum(flat, axis=1, keepdims=True)
    first = (iota((VECS, BLOCK), 0) == 0) & (iota((VECS, BLOCK), 1) == 33)
    small = small + jnp.where(first, whole_sum, 0.0)
    send(out, start * scale, small)


def first_kernel(recv, degree_ref, start_ref, out, basis_out, image_out, trivial_out):
    swept, small = receive(recv)
    degree = degree_ref[...]
    scale = lax.rsqrt(degree)
    total = small[0:1, 33:34]
    trivial = jnp.sqrt(degree / total)
    coef = small[:, 32:33] * lax.rsqrt(total)
    lanes = iota((VECS, BLOCK), 1)
    wide = jnp.where(lanes == 0, coef, 0.0)
    gram = small[:, :VECS] - dot_t(wide, wide)
    upper, inverse = factor_inverse(gram)
    along = coef * trivial
    both = dot(
        inverse,
        jnp.concatenate([start_ref[...] - along, swept * scale - along], axis=1),
    )
    width = degree.shape[1]
    basis, image = both[:, :width], both[:, width:]
    basis_out[...] = basis
    image_out[...] = image
    trivial_out[...] = trivial
    send(out, image * scale, pad_lanes(dot_t(image, stacked([basis, image, trivial]))))


def second_kernel(
    recv, degree_ref, trivial_ref, basis_ref, image_ref, out, basis_out, image_out, rest_out, mats
):
    swept, small = receive(recv)
    scale = lax.rsqrt(degree_ref[...])
    trivial = trivial_ref[...]
    alpha_t = small[:, :VECS]
    gram = small[:, VECS : 2 * VECS] - dot_t(alpha_t, alpha_t)
    upper, inverse = factor_inverse(gram)
    width = trivial.shape[1]
    mixed = dot(alpha_t, jnp.concatenate([basis_ref[...], image_ref[...]], axis=1))
    residual = image_ref[...] - mixed[:, :width]
    applied = swept * scale - small[:, 2 * VECS : 2 * VECS + 1] * trivial - mixed[:, width:]
    both = dot(inverse, jnp.concatenate([residual, applied], axis=1))
    basis, image = both[:, :width], both[:, width:]
    rest = image - dot(upper, basis_ref[...])
    basis_out[...] = basis
    image_out[...] = image
    rest_out[...] = rest
    mats[0] = alpha_t
    mats[1] = upper
    send(out, rest * scale, pad_lanes(dot_t(rest, stacked([basis, rest, trivial]))))


def third_kernel(
    recv, degree_ref, trivial_ref, basis_ref, image_ref, rest_ref, out, basis_out, rest_out, mats
):
    swept, small = receive(recv)
    scale = lax.rsqrt(degree_ref[...])
    trivial = trivial_ref[...]
    alpha_t = small[:, :VECS]
    gram = small[:, VECS : 2 * VECS] - dot_t(alpha_t, alpha_t)
    upper, inverse = factor_inverse(gram)
    width = trivial.shape[1]
    mixed = dot(alpha_t, jnp.concatenate([basis_ref[...], image_ref[...]], axis=1))
    residual = rest_ref[...] - mixed[:, :width]
    applied = swept * scale - small[:, 2 * VECS : 2 * VECS + 1] * trivial - mixed[:, width:]
    both = dot(inverse, jnp.concatenate([residual, applied], axis=1))
    basis, image = both[:, :width], both[:, width:]
    rest = image - dot(upper, basis_ref[...])
    basis_out[...] = basis
    rest_out[...] = rest
    mats[0] = alpha_t
    mats[1] = upper
    small = pad_lanes(
        dot_t(rest, jnp.concatenate([basis, rest], axis=0))
    )
    packed = small[0:4, :]
    for q in range(1, 4):
        packed = packed + pltpu.roll(small[4 * q : 4 * q + 4, :], 32 * q, 1)
    for p in range(out.shape[0]):
        out[p] = packed


def last_kernel(recv, basis_ref, rest_ref, mats_a, mats_b, alphas, betas, out, *, norm):
    packed = jnp.sum(recv[...], axis=0)
    lanes = iota((4, BLOCK), 1)
    rows = []
    for q in range(4):
        part = packed if q == 0 else pltpu.roll(packed, BLOCK - 32 * q, 1)
        rows.append(jnp.where(lanes < 32, part, 0.0))
    small = jnp.concatenate(rows, axis=0)
    alpha_t = small[:, :VECS]
    gram = small[:, VECS : 2 * VECS] - dot_t(alpha_t, alpha_t)
    upper, inverse = factor_inverse(gram)
    final = dot(inverse * norm, rest_ref[...] - dot(alpha_t, basis_ref[...]))
    for b in range(8):
        out[:, b, :] = final[:, b * BLOCK : (b + 1) * BLOCK]
    alphas[0] = mats_a[0].T
    alphas[1] = mats_b[0].T
    alphas[2] = alpha_t.T
    betas[0] = mats_a[1]
    betas[1] = mats_b[1]
    betas[2] = upper


def call(kernel, out_shape, mib, *args, scratch=(), specs=None, out_specs=None, aliases=None):
    outs = out_shape if isinstance(out_shape, (list, tuple)) else None
    return pl.pallas_call(
        kernel,
        out_shape=out_shape,
        in_specs=specs or [whole()] * len(args),
        out_specs=out_specs or ([whole()] * len(outs) if outs else whole()),
        scratch_shapes=list(scratch),
        input_output_aliases=aliases or {},
        compiler_params=params(mib),
    )(*args)


def exchange(values, axis):
    return lax.all_to_all(values, axis, split_axis=0, concat_axis=0, tiled=True)


def column_parts(own, rows):
    parts = [own] + [toggled(own, m, rows) for m in range(2, rows, 2)]
    return [p for part in parts for p in (part, toggled(part, 1, rows))]


def toggled(values, bits, size):
    return lax.ppermute(values, "row", [(i, i ^ bits) for i in range(size)])


def shape(dims, dtype=F32):
    return jax.ShapeDtypeStruct(dims, dtype)


def on_device(descriptors, send_slot, recv_slot, block_pairs, start):
    rows = lax.axis_size("row")
    cols = lax.axis_size("col")
    count = rows * cols
    slots = descriptors.shape[1]
    seg = recv_slot.shape[0]
    nblk = seg // BLOCK
    nrow, ncol = cols * nblk, rows * nblk
    own = jnp.arange(nblk, dtype=jnp.int32)
    me = lax.axis_index("row")
    row_idx = jnp.concatenate([block_pairs[0], lax.axis_index("col") * nblk + own, me[None]])
    col_idx = jnp.concatenate([block_pairs[1], me * nblk + own])
    skip_idx = col_idx + col_idx // nblk
    groups = col_idx.shape[0] // 4
    unroll = math.gcd(GROUP_UNROLL, groups // PIECES)

    with jax.named_scope("relay"):
        packed_rows = slots // 4
        outgoing = call(
            relay_out_kernel,
            shape((packed_rows, BLOCK), BF16),
            16,
            send_slot.reshape(slots // BLOCK, BLOCK),
            descriptors,
            scratch=[VMEM((packed_rows, slots), BF16), VMEM((BLOCK, slots), BF16)],
        )
        received = exchange(outgoing, AXES)
        row_copies, own_desc = call(
            relay_in_kernel,
            [shape((nrow, FEAT, BLOCK), BF16), shape((nblk, FEAT, BLOCK), BF16)],
            16,
            recv_slot.reshape(nblk, BLOCK),
            received,
        )
    with jax.named_scope("gather"):
        row_desc = exchange(row_copies, "col")
        col_desc = column_parts(own_desc, rows)
    with jax.named_scope("build"):
        wshape = pltpu.VMEM((groups // PIECES, 2 * BLOCK, 2 * BLOCK), BF16)
        empty = call(
            empty_kernel,
            [wshape] * PIECES,
            1,
            row_desc,
            *col_desc,
            row_idx,
            col_idx,
            skip_idx,
            specs=[pl.BlockSpec(memory_space=pl.ANY)] * (rows + 4),
        )
        empty = [pltpu.with_memory_space_constraint(piece, pltpu.VMEM) for piece in empty]
        *weights, degree_part = call(
            functools.partial(build_kernel, unroll=unroll, peers=rows),
            [wshape] * PIECES + [shape((cols, nblk, BLOCK))],
            8,
            row_idx,
            col_idx,
            row_desc,
            *col_desc,
            *empty,
            scratch=[
                VMEM((ncol, BLOCK, BLOCK), BF16),
                VMEM((nrow, BLOCK, BLOCK), BF16),
                VMEM((nrow, 8, BLOCK), F32),
            ],
            specs=[smem(), smem()]
            + [whole()] * (rows + 1)
            + [pl.BlockSpec(memory_space=pl.ANY)] * PIECES,
            aliases={rows + 3 + k: k for k in range(PIECES)},
        )
        weights = [pltpu.with_memory_space_constraint(piece, pltpu.VMEM) for piece in weights]
    with jax.named_scope("degree"):
        sent, degree, begin = call(
            scale_kernel,
            [shape((rows * 9, VECS, BLOCK), BF16), shape((1, seg)), shape((VECS, seg))],
            8,
            exchange(degree_part, "col"),
            start,
        )

    def sweep(sent):
        vectors = exchange(sent, "row")
        partial_sum = call(
            functools.partial(sweep_kernel, unroll=unroll, peers=rows),
            shape((cols, 9, VECS, BLOCK), BF16),
            8,
            row_idx,
            skip_idx,
            *weights,
            vectors,
            scratch=[VMEM((nrow, VECS, BLOCK), F32)],
            specs=[smem(), smem()] + [whole()] * (PIECES + 1),
        )
        return exchange(partial_sum, "col")

    vec = shape((VECS, seg))
    sending = shape((rows * 9, VECS, BLOCK), BF16)
    mats = shape((2, VECS, VECS))
    with jax.named_scope("step0"):
        swept = sweep(sent)
        sent, basis0, image0, trivial = call(
            first_kernel, [sending, vec, vec, shape((1, seg))], 8, swept, degree, begin
        )
    with jax.named_scope("step1"):
        swept = sweep(sent)
        sent, basis1, image1, rest1, mats0 = call(
            second_kernel, [sending, vec, vec, vec, mats], 8, swept, degree, trivial, basis0, image0
        )
    with jax.named_scope("step2"):
        swept = sweep(sent)
        small, basis2, rest2, mats1 = call(
            third_kernel,
            [shape((count, 4, BLOCK)), vec, vec, mats],
            8,
            swept,
            degree,
            trivial,
            basis1,
            image1,
            rest1,
        )
    with jax.named_scope("finish"):
        three = shape((3, VECS, VECS))
        return tuple(
            call(
                functools.partial(last_kernel, norm=math.sqrt(count * seg)),
                [three, three, shape((VECS, nblk, BLOCK))],
                8,
                exchange(small, AXES),
                basis2,
                rest2,
                mats0,
                mats1,
            )
        )


def solution(mesh):
    return jax.shard_map(
        on_device,
        mesh=mesh,
        in_specs=(
            P(None, ("row", "col")),
            P(("row", "col")),
            P(("row", "col")),
            P(None, ("row", "col")),
            P(None, ("row", "col"), None),
        ),
        out_specs=(P(), P(), P(None, ("row", "col"), None)),
        check_vma=False,
    )
```

```python
import functools
import math

import jax
import jax.numpy as jnp
from jax import lax
from jax.experimental import pallas as pl
from jax.experimental.pallas import tpu as pltpu
from jax.sharding import PartitionSpec as P

FEAT = 32
BLOCK = 128
VECS = 16
GROUP_UNROLL = 43
PIECES = 2
EXP2_SCALE = math.log2(math.e) / (2.0 * FEAT)
AXES = ("row", "col")
F32 = jnp.float32
BF16 = jnp.bfloat16
HIGHEST = lax.Precision.HIGHEST
VMEM = pltpu.VMEM


def params(mib):
    return pltpu.CompilerParams(vmem_limit_bytes=mib << 20)


def whole():
    return pl.BlockSpec(memory_space=pltpu.VMEM)


def smem():
    return pl.BlockSpec(memory_space=pltpu.SMEM)


def iota(shape, dim):
    return lax.broadcasted_iota(jnp.int32, shape, dim)


def split3(x):
    high = x.astype(BF16).astype(F32)
    rest = x - high
    middle = rest.astype(BF16).astype(F32)
    low = (rest - middle).astype(BF16).astype(F32)
    return high, middle, low


def dot(left, right):
    return jnp.dot(left, right, precision=HIGHEST, preferred_element_type=F32)


def dot_t(left, right):
    return lax.dot_general(
        left, right, (((1,), (1,)), ((), ())), precision=HIGHEST, preferred_element_type=F32
    )


def encode(small):
    high, middle, low = split3(small)
    return (high + pltpu.roll(middle, 40, 1) + pltpu.roll(low, 80, 1)).astype(BF16)


def decode(tiles):
    total = sum(tiles)
    value = total + pltpu.roll(total, 88, 1) + pltpu.roll(total, 48, 1)
    return jnp.where(iota((VECS, BLOCK), 1) < 40, value, 0.0)


def pad_lanes(small):
    return jnp.concatenate([small, jnp.zeros((VECS, BLOCK - small.shape[1]), F32)], axis=1)


def factor_inverse(gram):
    rows = iota((VECS, BLOCK), 0)
    lanes = iota((VECS, BLOCK), 1)
    work = pad_lanes(gram) + jnp.where(lanes == rows + VECS, 1.0, 0.0)
    columns = [jnp.broadcast_to(work[:, k : k + 1], work.shape) for k in range(VECS)]
    for k in range(VECS):
        inverse = 1.0 / columns[k][k : k + 1, :]
        ratio = jnp.where(rows > k, columns[k], 0.0) * inverse
        for n in range(k + 1, VECS):
            columns[n] = columns[n] - ratio * columns[n][k : k + 1, :]
        work = work - ratio * work[k : k + 1, :]
    diagonal = jnp.sum(jnp.where(lanes == rows, work, 0.0), axis=1, keepdims=True)
    scaled = work * lax.rsqrt(diagonal)
    upper = jnp.where(lanes >= rows, scaled, 0.0)[:, :VECS]
    return upper, scaled[:, VECS : 2 * VECS]


def relay_out_kernel(slot_ref, desc_ref, recv_slot_ref, out_ref, recv_slot_out, hot_ref, spread_ref):
    recv_slot_out[...] = recv_slot_ref[...]
    slots = slot_ref.shape[0] * BLOCK
    rows = out_ref.shape[0]
    target = iota((rows, BLOCK), 0)
    for t in range(slots // BLOCK):
        cut = pl.ds(t * BLOCK, BLOCK)
        slot = slot_ref[t : t + 1, :]
        hot_ref[:, cut] = jnp.where(target == (slot >> 2), 1.0, 0.0).astype(BF16)
        desc = desc_ref[:, cut].astype(F32)
        quarter = slot & 3
        for q in range(4):
            spread_ref[q * FEAT : (q + 1) * FEAT, cut] = jnp.where(quarter == q, desc, 0.0).astype(
                BF16
            )
    out_ref[...] = lax.dot_general(
        hot_ref[...], spread_ref[...], (((1,), (1,)), ((), ())), preferred_element_type=F32
    ).astype(BF16)


def relay_in_kernel(slot_ref, recv_ref, row_ref, own_ref):
    rows = recv_ref.shape[0]
    nblk = slot_ref.shape[0]
    received = recv_ref[...].astype(F32).T.astype(BF16)
    source = iota((rows, BLOCK), 0)
    for b in range(nblk):
        slot = slot_ref[b : b + 1, :]
        hot = jnp.where(source == (slot >> 2), 1.0, 0.0).astype(BF16)
        picked = jnp.dot(received, hot, preferred_element_type=F32)
        quarter = slot & 3
        own = jnp.zeros((FEAT, BLOCK), F32)
        for q in range(4):
            own = own + jnp.where(quarter == q, picked[q * FEAT : (q + 1) * FEAT, :], 0.0)
        own = own.astype(BF16)
        for copy in range(row_ref.shape[0] // nblk):
            row_ref[copy * nblk + b] = own
        own_ref[b] = own


def empty_kernel(*refs):
    for ref in refs[-PIECES:]:
        ref[0, 0:16, 0:BLOCK] = jnp.zeros((16, BLOCK), BF16)


def features(block, sign):
    values = block.astype(F32)
    pieces = split3(jnp.sum(values * values, axis=0, keepdims=True))
    rows = iota((BLOCK - FEAT, BLOCK), 0)
    tail = jnp.zeros((BLOCK - FEAT, BLOCK), F32)
    for n in range(3):
        if sign:
            tail = jnp.where(rows == n, -pieces[n], tail)
            tail = jnp.where(rows == n + 3, 1.0, tail)
        else:
            tail = jnp.where(rows == n, 1.0, tail)
            tail = jnp.where(rows == n + 3, -pieces[n], tail)
    scale = 2.0 if sign else 1.0
    return jnp.concatenate([values * scale, tail], axis=0).astype(BF16)


def each_piece(pieces, body, unroll):
    first = 0
    for weights in pieces:
        count = weights.shape[0]
        lax.fori_loop(0, count // unroll, functools.partial(body, weights=weights, first=first), 0)
        first += count


def left_kernel(row_idx, *refs):
    col_desc, left = refs[:-1], refs[-1]
    me = row_idx[row_idx.shape[0] - 1]
    eye = jnp.where(
        iota((BLOCK, BLOCK), 0) == iota((BLOCK, BLOCK), 1), 1.0, 0.0
    ).astype(BF16)
    for m, part in enumerate(col_desc):
        nblk = part.shape[0]
        for k in range(nblk):
            rows = features(part[k], False)
            left[(me ^ m) * nblk + k] = lax.dot_general(
                eye, rows, (((1,), (1,)), ((), ())), preferred_element_type=F32
            ).astype(BF16)


def build_kernel(row_idx, col_idx, row_desc, left, *refs, unroll):
    pieces = refs[PIECES : 2 * PIECES]
    degree, right, total = refs[2 * PIECES :]
    nrow = row_desc.shape[0]

    def prepare_row(n, carry):
        for k in range(8):
            right[n * 8 + k] = features(row_desc[n * 8 + k], True)
            total[n * 8 + k] = jnp.zeros((8, BLOCK), F32)
        return carry

    lax.fori_loop(0, nrow // 8, prepare_row, 0)

    def several(step, carry, weights, first):
        for u in range(unroll):
            group = step * unroll + u
            for q in range(4):
                i = row_idx[(first + group) * 4 + q]
                j = col_idx[(first + group) * 4 + q]
                power = jnp.dot(left[j], right[i], preferred_element_type=F32)
                block = jnp.exp2(power * EXP2_SCALE).astype(BF16)
                r, c = q // 2, q % 2
                weights[group, r * BLOCK : (r + 1) * BLOCK, c * BLOCK : (c + 1) * BLOCK] = block
                total[i] += jnp.sum(block.astype(F32).reshape(BLOCK // 8, 8, BLOCK), axis=0)
        return carry

    each_piece(pieces, several, unroll)
    for n in range(nrow):
        degree[n // 8, n % 8 : n % 8 + 1, :] = jnp.sum(total[n], axis=0, keepdims=True)


def sweep_kernel(row_idx, col_idx, *refs, unroll, peers):
    pieces = refs[:PIECES]
    parts = refs[PIECES : PIECES + peers]
    out, vectors, total = refs[PIECES + peers :]
    me = row_idx[row_idx.shape[0] - 1]
    for m in range(peers):
        for b in range(9):
            vectors[(me ^ m) * 9 + b] = parts[m][b]
    total[...] = jnp.zeros_like(total)
    zero = jnp.zeros((VECS, BLOCK), BF16)

    def several(step, carry, weights, first):
        for u in range(unroll):
            group = step * unroll + u
            picked = [vectors[col_idx[(first + group) * 4 + q]] for q in range(4)]
            lhs = jnp.concatenate(
                [
                    jnp.concatenate([picked[0], zero], 1),
                    jnp.concatenate([zero, picked[2]], 1),
                    jnp.concatenate([picked[1], zero], 1),
                    jnp.concatenate([zero, picked[3]], 1),
                ],
                0,
            )
            result = jnp.dot(lhs, weights[group], preferred_element_type=F32)
            for place, q in enumerate((0, 2, 1, 3)):
                half = (q % 2) * BLOCK
                total[row_idx[(first + group) * 4 + q]] += result[
                    place * VECS : (place + 1) * VECS, half : half + BLOCK
                ]
        return carry

    each_piece(pieces, several, unroll)
    small = encode(decode([part[8].astype(F32) for part in parts]))
    for n in range(total.shape[0]):
        out[n // 8, n % 8] = total[n].astype(BF16)
    for p in range(out.shape[0]):
        out[p, 8] = small


def row_vector(block):
    return jnp.concatenate([block[b : b + 1, :] for b in range(8)], axis=1)


def send(out, vectors, small):
    tile = encode(small)
    for b in range(8):
        out[b] = vectors[:, b * BLOCK : (b + 1) * BLOCK].astype(BF16)
    out[8] = tile


def receive(recv):
    peers = recv.shape[0]
    tiles = []
    for b in range(8):
        tile = recv[0, b].astype(F32)
        for p in range(1, peers):
            tile = tile + recv[p, b].astype(F32)
        tiles.append(tile)
    return jnp.concatenate(tiles, axis=1), decode([recv[p, 8].astype(F32) for p in range(peers)])


def stacked(parts):
    width = parts[0].shape[1]
    return jnp.concatenate(parts + [jnp.zeros((7, width), F32)], axis=0)


def scale_kernel(degree_ref, start_ref, out, degree_out, start_out):
    degree = degree_ref[0]
    for p in range(1, degree_ref.shape[0]):
        degree = degree + degree_ref[p]
    flat = row_vector(degree)
    scale = lax.rsqrt(flat)
    start = jnp.concatenate([start_ref[:, b, :] for b in range(8)], axis=1)
    degree_out[...] = flat
    start_out[...] = start
    root = jnp.sqrt(flat)
    small = pad_lanes(dot_t(start, stacked([start, jnp.zeros_like(start), root])))
    whole_sum = jnp.sum(flat, axis=1, keepdims=True)
    first = (iota((VECS, BLOCK), 0) == 0) & (iota((VECS, BLOCK), 1) == 33)
    small = small + jnp.where(first, whole_sum, 0.0)
    send(out, start * scale, small)


def first_kernel(recv, degree_ref, start_ref, out, basis_out, image_out, trivial_out):
    swept, small = receive(recv)
    degree = degree_ref[...]
    scale = lax.rsqrt(degree)
    total = small[0:1, 33:34]
    trivial = jnp.sqrt(degree / total)
    coef = small[:, 32:33] * lax.rsqrt(total)
    lanes = iota((VECS, BLOCK), 1)
    wide = jnp.where(lanes == 0, coef, 0.0)
    gram = small[:, :VECS] - dot_t(wide, wide)
    upper, inverse = factor_inverse(gram)
    along = coef * trivial
    both = dot(
        inverse,
        jnp.concatenate([start_ref[...] - along, swept * scale - along], axis=1),
    )
    width = degree.shape[1]
    basis, image = both[:, :width], both[:, width:]
    basis_out[...] = basis
    image_out[...] = image
    trivial_out[...] = trivial
    send(out, image * scale, pad_lanes(dot_t(image, stacked([basis, image, trivial]))))


def second_kernel(
    recv, degree_ref, trivial_ref, basis_ref, image_ref, out, basis_out, image_out, rest_out, mats
):
    swept, small = receive(recv)
    scale = lax.rsqrt(degree_ref[...])
    trivial = trivial_ref[...]
    alpha_t = small[:, :VECS]
    gram = small[:, VECS : 2 * VECS] - dot_t(alpha_t, alpha_t)
    upper, inverse = factor_inverse(gram)
    width = trivial.shape[1]
    mixed = dot(alpha_t, jnp.concatenate([basis_ref[...], image_ref[...]], axis=1))
    residual = image_ref[...] - mixed[:, :width]
    applied = swept * scale - small[:, 2 * VECS : 2 * VECS + 1] * trivial - mixed[:, width:]
    both = dot(inverse, jnp.concatenate([residual, applied], axis=1))
    basis, image = both[:, :width], both[:, width:]
    rest = image - dot(upper, basis_ref[...])
    basis_out[...] = basis
    image_out[...] = image
    rest_out[...] = rest
    mats[0] = alpha_t
    mats[1] = upper
    send(out, rest * scale, pad_lanes(dot_t(rest, stacked([basis, rest, trivial]))))


def third_kernel(
    recv, degree_ref, trivial_ref, basis_ref, image_ref, rest_ref, out, basis_out, rest_out, mats
):
    swept, small = receive(recv)
    scale = lax.rsqrt(degree_ref[...])
    trivial = trivial_ref[...]
    alpha_t = small[:, :VECS]
    gram = small[:, VECS : 2 * VECS] - dot_t(alpha_t, alpha_t)
    upper, inverse = factor_inverse(gram)
    width = trivial.shape[1]
    mixed = dot(alpha_t, jnp.concatenate([basis_ref[...], image_ref[...]], axis=1))
    residual = rest_ref[...] - mixed[:, :width]
    applied = swept * scale - small[:, 2 * VECS : 2 * VECS + 1] * trivial - mixed[:, width:]
    both = dot(inverse, jnp.concatenate([residual, applied], axis=1))
    basis, image = both[:, :width], both[:, width:]
    rest = image - dot(upper, basis_ref[...])
    basis_out[...] = basis
    rest_out[...] = rest
    mats[0] = alpha_t
    mats[1] = upper
    small = pad_lanes(
        dot_t(rest, jnp.concatenate([basis, rest], axis=0))
    )
    packed = small[0:4, :]
    for q in range(1, 4):
        packed = packed + pltpu.roll(small[4 * q : 4 * q + 4, :], 32 * q, 1)
    for p in range(out.shape[0]):
        out[p] = packed


def last_kernel(recv, basis_ref, rest_ref, mats_a, mats_b, alphas, betas, out, *, norm):
    packed = jnp.sum(recv[...], axis=0)
    lanes = iota((4, BLOCK), 1)
    rows = []
    for q in range(4):
        part = packed if q == 0 else pltpu.roll(packed, BLOCK - 32 * q, 1)
        rows.append(jnp.where(lanes < 32, part, 0.0))
    small = jnp.concatenate(rows, axis=0)
    alpha_t = small[:, :VECS]
    gram = small[:, VECS : 2 * VECS] - dot_t(alpha_t, alpha_t)
    upper, inverse = factor_inverse(gram)
    final = dot(inverse * norm, rest_ref[...] - dot(alpha_t, basis_ref[...]))
    for b in range(8):
        out[:, b, :] = final[:, b * BLOCK : (b + 1) * BLOCK]
    alphas[0] = mats_a[0].T
    alphas[1] = mats_b[0].T
    alphas[2] = alpha_t.T
    betas[0] = mats_a[1]
    betas[1] = mats_b[1]
    betas[2] = upper


def call(kernel, out_shape, mib, *args, scratch=(), specs=None, out_specs=None, aliases=None):
    outs = out_shape if isinstance(out_shape, (list, tuple)) else None
    return pl.pallas_call(
        kernel,
        out_shape=out_shape,
        in_specs=specs or [whole()] * len(args),
        out_specs=out_specs or ([whole()] * len(outs) if outs else whole()),
        scratch_shapes=list(scratch),
        input_output_aliases=aliases or {},
        compiler_params=params(mib),
    )(*args)


def exchange(values, axis):
    return lax.all_to_all(values, axis, split_axis=0, concat_axis=0, tiled=True)


def column_parts(own, rows):
    parts = [own] + [toggled(own, m, rows) for m in range(2, rows, 2)]
    return [p for part in parts for p in (part, toggled(part, 1, rows))]


def toggled(values, bits, size):
    return lax.ppermute(values, "row", [(i, i ^ bits) for i in range(size)])


def shape(dims, dtype=F32):
    return jax.ShapeDtypeStruct(dims, dtype)


def on_device(descriptors, send_slot, recv_slot, block_pairs, start):
    rows = lax.axis_size("row")
    cols = lax.axis_size("col")
    count = rows * cols
    slots = descriptors.shape[1]
    seg = recv_slot.shape[0]
    nblk = seg // BLOCK
    nrow, ncol = cols * nblk, rows * nblk
    own = jnp.arange(nblk, dtype=jnp.int32)
    me = lax.axis_index("row")
    row_idx = jnp.concatenate([block_pairs[0], lax.axis_index("col") * nblk + own, me[None]])
    col_idx = jnp.concatenate([block_pairs[1], me * nblk + own])
    skip_idx = col_idx + col_idx // nblk
    groups = col_idx.shape[0] // 4
    unroll = math.gcd(GROUP_UNROLL, groups // PIECES)

    with jax.named_scope("relay"):
        packed_rows = slots // 4
        outgoing, slots_in = call(
            relay_out_kernel,
            [shape((packed_rows, BLOCK), BF16), shape((nblk, BLOCK), jnp.int32)],
            16,
            send_slot.reshape(slots // BLOCK, BLOCK),
            descriptors,
            recv_slot.reshape(nblk, BLOCK),
            scratch=[VMEM((packed_rows, slots), BF16), VMEM((BLOCK, slots), BF16)],
        )
        received = exchange(outgoing, AXES)
        row_copies, own_desc = call(
            relay_in_kernel,
            [shape((nrow, FEAT, BLOCK), BF16), shape((nblk, FEAT, BLOCK), BF16)],
            16,
            slots_in,
            received,
        )
    with jax.named_scope("gather"):
        row_desc = exchange(row_copies, "col")
        left = call(
            left_kernel,
            shape((ncol, BLOCK, BLOCK), BF16),
            4,
            row_idx,
            *column_parts(own_desc, rows),
            specs=[smem()] + [whole()] * rows,
        )
    with jax.named_scope("build"):
        wshape = pltpu.VMEM((groups // PIECES, 2 * BLOCK, 2 * BLOCK), BF16)
        empty = call(
            empty_kernel,
            [wshape] * PIECES,
            1,
            row_desc,
            left,
            row_idx,
            col_idx,
            skip_idx,
            specs=[pl.BlockSpec(memory_space=pl.ANY)] * 5,
        )
        empty = [pltpu.with_memory_space_constraint(piece, pltpu.VMEM) for piece in empty]
        *weights, degree_part = call(
            functools.partial(build_kernel, unroll=unroll),
            [wshape] * PIECES + [shape((cols, nblk, BLOCK))],
            8,
            row_idx,
            col_idx,
            row_desc,
            left,
            *empty,
            scratch=[
                VMEM((nrow, BLOCK, BLOCK), BF16),
                VMEM((nrow, 8, BLOCK), F32),
            ],
            specs=[smem(), smem(), whole(), whole()] + [pl.BlockSpec(memory_space=pl.ANY)] * PIECES,
            aliases={4 + k: k for k in range(PIECES)},
        )
        weights = [pltpu.with_memory_space_constraint(piece, pltpu.VMEM) for piece in weights]
    with jax.named_scope("degree"):
        sent, degree, begin = call(
            scale_kernel,
            [shape((9, VECS, BLOCK), BF16), shape((1, seg)), shape((VECS, seg))],
            8,
            exchange(degree_part, "col"),
            start,
        )

    def sweep(sent):
        vectors = column_parts(sent, rows)
        partial_sum = call(
            functools.partial(sweep_kernel, unroll=unroll, peers=rows),
            shape((cols, 9, VECS, BLOCK), BF16),
            8,
            row_idx,
            skip_idx,
            *weights,
            *vectors,
            scratch=[VMEM((rows * 9, VECS, BLOCK), BF16), VMEM((nrow, VECS, BLOCK), F32)],
            specs=[smem(), smem()] + [whole()] * (PIECES + rows),
        )
        return exchange(partial_sum, "col")

    vec = shape((VECS, seg))
    sending = shape((9, VECS, BLOCK), BF16)
    mats = shape((2, VECS, VECS))
    with jax.named_scope("step0"):
        swept = sweep(sent)
        sent, basis0, image0, trivial = call(
            first_kernel, [sending, vec, vec, shape((1, seg))], 8, swept, degree, begin
        )
    with jax.named_scope("step1"):
        swept = sweep(sent)
        sent, basis1, image1, rest1, mats0 = call(
            second_kernel, [sending, vec, vec, vec, mats], 8, swept, degree, trivial, basis0, image0
        )
    with jax.named_scope("step2"):
        swept = sweep(sent)
        small, basis2, rest2, mats1 = call(
            third_kernel,
            [shape((count, 4, BLOCK)), vec, vec, mats],
            8,
            swept,
            degree,
            trivial,
            basis1,
            image1,
            rest1,
        )
    with jax.named_scope("finish"):
        three = shape((3, VECS, VECS))
        return tuple(
            call(
                functools.partial(last_kernel, norm=math.sqrt(count * seg)),
                [three, three, shape((VECS, nblk, BLOCK))],
                8,
                exchange(small, AXES),
                basis2,
                rest2,
                mats0,
                mats1,
            )
        )


def solution(mesh):
    return jax.shard_map(
        on_device,
        mesh=mesh,
        in_specs=(
            P(None, ("row", "col")),
            P(("row", "col")),
            P(("row", "col")),
            P(None, ("row", "col")),
            P(None, ("row", "col"), None),
        ),
        out_specs=(P(), P(), P(None, ("row", "col"), None)),
        check_vma=False,
    )
```

```python
import functools
import math

import jax
import jax.numpy as jnp
from jax import lax
from jax.experimental import pallas as pl
from jax.experimental.pallas import tpu as pltpu
from jax.sharding import PartitionSpec as P

FEAT = 32
BLOCK = 128
VECS = 16
GROUP_UNROLL = 43
PIECES = 2
EXP2_SCALE = math.log2(math.e) / (2.0 * FEAT)
AXES = ("row", "col")
F32 = jnp.float32
BF16 = jnp.bfloat16
HIGHEST = lax.Precision.HIGHEST
VMEM = pltpu.VMEM


def params(mib):
    return pltpu.CompilerParams(vmem_limit_bytes=mib << 20)


def whole():
    return pl.BlockSpec(memory_space=pltpu.VMEM)


def smem():
    return pl.BlockSpec(memory_space=pltpu.SMEM)


def iota(shape, dim):
    return lax.broadcasted_iota(jnp.int32, shape, dim)


def split3(x):
    high = x.astype(BF16).astype(F32)
    rest = x - high
    middle = rest.astype(BF16).astype(F32)
    low = (rest - middle).astype(BF16).astype(F32)
    return high, middle, low


def dot(left, right):
    return jnp.dot(left, right, precision=HIGHEST, preferred_element_type=F32)


def dot_t(left, right):
    return lax.dot_general(
        left, right, (((1,), (1,)), ((), ())), precision=HIGHEST, preferred_element_type=F32
    )


def encode(small):
    high, middle, low = split3(small)
    return (high + pltpu.roll(middle, 40, 1) + pltpu.roll(low, 80, 1)).astype(BF16)


def decode(tiles):
    total = sum(tiles)
    value = total + pltpu.roll(total, 88, 1) + pltpu.roll(total, 48, 1)
    return jnp.where(iota((VECS, BLOCK), 1) < 40, value, 0.0)


def pad_lanes(small):
    return jnp.concatenate([small, jnp.zeros((VECS, BLOCK - small.shape[1]), F32)], axis=1)


def factor_inverse(gram):
    rows = iota((VECS, BLOCK), 0)
    lanes = iota((VECS, BLOCK), 1)
    work = pad_lanes(gram) + jnp.where(lanes == rows + VECS, 1.0, 0.0)
    columns = [jnp.broadcast_to(work[:, k : k + 1], work.shape) for k in range(VECS)]
    for k in range(VECS):
        inverse = 1.0 / columns[k][k : k + 1, :]
        ratio = jnp.where(rows > k, columns[k], 0.0) * inverse
        for n in range(k + 1, VECS):
            columns[n] = columns[n] - ratio * columns[n][k : k + 1, :]
        work = work - ratio * work[k : k + 1, :]
    diagonal = jnp.sum(jnp.where(lanes == rows, work, 0.0), axis=1, keepdims=True)
    scaled = work * lax.rsqrt(diagonal)
    upper = jnp.where(lanes >= rows, scaled, 0.0)[:, :VECS]
    return upper, scaled[:, VECS : 2 * VECS]


def relay_out_kernel(slot_ref, desc_ref, recv_slot_ref, out_ref, recv_slot_out, hot_ref, spread_ref):
    recv_slot_out[...] = recv_slot_ref[...]
    slots = slot_ref.shape[0] * BLOCK
    rows = out_ref.shape[0]
    target = iota((rows, BLOCK), 0)
    for t in range(slots // BLOCK):
        cut = pl.ds(t * BLOCK, BLOCK)
        slot = slot_ref[t : t + 1, :]
        hot_ref[:, cut] = jnp.where(target == (slot >> 2), 1.0, 0.0).astype(BF16)
        desc = desc_ref[:, cut].astype(F32)
        quarter = slot & 3
        for q in range(4):
            spread_ref[q * FEAT : (q + 1) * FEAT, cut] = jnp.where(quarter == q, desc, 0.0).astype(
                BF16
            )
    out_ref[...] = lax.dot_general(
        hot_ref[...], spread_ref[...], (((1,), (1,)), ((), ())), preferred_element_type=F32
    ).astype(BF16)


def relay_in_kernel(slot_ref, recv_ref, row_ref, own_ref):
    rows = recv_ref.shape[0]
    nblk = slot_ref.shape[0]
    received = recv_ref[...].astype(F32).T.astype(BF16)
    source = iota((rows, BLOCK), 0)
    for b in range(nblk):
        slot = slot_ref[b : b + 1, :]
        hot = jnp.where(source == (slot >> 2), 1.0, 0.0).astype(BF16)
        picked = jnp.dot(received, hot, preferred_element_type=F32)
        quarter = slot & 3
        own = jnp.zeros((FEAT, BLOCK), F32)
        for q in range(4):
            own = own + jnp.where(quarter == q, picked[q * FEAT : (q + 1) * FEAT, :], 0.0)
        own = own.astype(BF16)
        for copy in range(row_ref.shape[0] // nblk):
            row_ref[copy * nblk + b] = own
        own_ref[b] = own


def empty_kernel(*refs):
    for ref in refs[-PIECES:]:
        ref[0, 0:16, 0:BLOCK] = jnp.zeros((16, BLOCK), BF16)


def features(block, sign):
    values = block.astype(F32)
    pieces = split3(jnp.sum(values * values, axis=0, keepdims=True))
    rows = iota((BLOCK - FEAT, BLOCK), 0)
    tail = jnp.zeros((BLOCK - FEAT, BLOCK), F32)
    for n in range(3):
        if sign:
            tail = jnp.where(rows == n, -pieces[n], tail)
            tail = jnp.where(rows == n + 3, 1.0, tail)
        else:
            tail = jnp.where(rows == n, 1.0, tail)
            tail = jnp.where(rows == n + 3, -pieces[n], tail)
    scale = 2.0 if sign else 1.0
    return jnp.concatenate([values * scale, tail], axis=0).astype(BF16)


def each_piece(pieces, body, unroll):
    first = 0
    for weights in pieces:
        count = weights.shape[0]
        lax.fori_loop(0, count // unroll, functools.partial(body, weights=weights, first=first), 0)
        first += count


def left_kernel(row_idx, *refs):
    col_desc, left = refs[:-1], refs[-1]
    me = row_idx[row_idx.shape[0] - 1]
    eye = jnp.where(
        iota((BLOCK, BLOCK), 0) == iota((BLOCK, BLOCK), 1), 1.0, 0.0
    ).astype(BF16)
    for m, part in enumerate(col_desc):
        nblk = part.shape[0]
        for k in range(nblk):
            rows = features(part[k], False)
            left[(me ^ m) * nblk + k] = lax.dot_general(
                eye, rows, (((1,), (1,)), ((), ())), preferred_element_type=F32
            ).astype(BF16)


def build_kernel(row_idx, col_idx, row_desc, left, *refs, unroll):
    pieces = refs[PIECES : 2 * PIECES]
    degree, right, total = refs[2 * PIECES :]
    nrow = row_desc.shape[0]
    depth = right.shape[1]
    total[...] = jnp.zeros_like(total)

    def prepare_row(n, carry):
        for k in range(8):
            right[n * 8 + k] = features(row_desc[n * 8 + k], True)[:depth]
        return carry

    lax.fori_loop(0, nrow // 8, prepare_row, 0)

    def several(step, carry, weights, first):
        for u in range(unroll):
            group = step * unroll + u
            for q in range(4):
                i = row_idx[(first + group) * 4 + q]
                j = col_idx[(first + group) * 4 + q]
                power = jnp.dot(left[j, :, :depth], right[i], preferred_element_type=F32)
                block = jnp.exp2(power * EXP2_SCALE).astype(BF16)
                r, c = q // 2, q % 2
                weights[group, r * BLOCK : (r + 1) * BLOCK, c * BLOCK : (c + 1) * BLOCK] = block
                total[j] += block.astype(F32)
        return carry

    each_piece(pieces, several, unroll)
    ones = jnp.ones((16, 2 * BLOCK), BF16)
    for n in range(total.shape[0]):
        value = total[n]
        high = value.astype(BF16)
        low = (value - high.astype(F32)).astype(BF16)
        sums = lax.dot_general(
            ones,
            jnp.concatenate([high, low], axis=1),
            (((1,), (1,)), ((), ())),
            preferred_element_type=F32,
        )
        degree[n : n + 1, :] = sums[0:1]


def apply_weights(row_idx, col_idx, pieces, vectors, total, unroll):
    total[...] = jnp.zeros_like(total)
    zero = jnp.zeros((VECS, BLOCK), BF16)

    def several(step, carry, weights, first):
        for u in range(unroll):
            group = step * unroll + u
            picked = [vectors[col_idx[(first + group) * 4 + q]] for q in range(4)]
            lhs = jnp.concatenate(
                [
                    jnp.concatenate([picked[0], zero], 1),
                    jnp.concatenate([zero, picked[2]], 1),
                    jnp.concatenate([picked[1], zero], 1),
                    jnp.concatenate([zero, picked[3]], 1),
                ],
                0,
            )
            result = jnp.dot(lhs, weights[group], preferred_element_type=F32)
            for place, q in enumerate((0, 2, 1, 3)):
                half = (q % 2) * BLOCK
                total[row_idx[(first + group) * 4 + q]] += result[
                    place * VECS : (place + 1) * VECS, half : half + BLOCK
                ]
        return carry

    each_piece(pieces, several, unroll)


def store_sums(out, total, small):
    tile = encode(small)
    for n in range(total.shape[0]):
        out[n // 8, n % 8] = total[n].astype(BF16)
    for p in range(out.shape[0]):
        out[p, 8] = tile


def sweep_kernel(row_idx, col_idx, *refs, unroll, peers):
    pieces = refs[:PIECES]
    parts = refs[PIECES : PIECES + peers]
    out, vectors, total = refs[PIECES + peers :]
    me = row_idx[row_idx.shape[0] - 1]
    for m in range(peers):
        for b in range(9):
            vectors[(me ^ m) * 9 + b] = parts[m][b]
    apply_weights(row_idx, col_idx, pieces, vectors, total, unroll)
    store_sums(out, total, decode([part[8].astype(F32) for part in parts]))


def first_sweep_kernel(row_idx, col_idx, *refs, unroll, peers):
    pieces = refs[:PIECES]
    starts = refs[PIECES : PIECES + peers]
    degrees = refs[PIECES + peers : PIECES + 2 * peers]
    out, degree_out, vectors, total, degree_ref = refs[PIECES + 2 * peers :]
    me = row_idx[row_idx.shape[0] - 1]
    degree = degrees[0][...]
    for m in range(1, peers):
        degree = degree + degrees[m][...]
    degree_ref[...] = degree
    along = jnp.zeros((VECS, BLOCK), F32)
    small = jnp.zeros((VECS, BLOCK), F32)
    for m in range(peers):
        for b in range(8):
            block = degree_ref[pl.ds((me ^ m) * 8 + b, 1), :]
            scale = lax.rsqrt(block)
            start = starts[m][b]
            vectors[(me ^ m) * 9 + b] = (start * scale).astype(BF16)
            along = along + start * (block * scale)
        small = small + starts[m][8]
    for b in range(8):
        degree_out[:, b * BLOCK : (b + 1) * BLOCK] = degree_ref[pl.ds(me * 8 + b, 1), :]
    rows, lanes = iota((VECS, BLOCK), 0), iota((VECS, BLOCK), 1)
    small = small + jnp.where(lanes == 32, jnp.sum(along, axis=1, keepdims=True), 0.0)
    whole_sum = jnp.sum(jnp.sum(degree, axis=0, keepdims=True), axis=1, keepdims=True)
    small = small + jnp.where((rows == 0) & (lanes == 33), whole_sum, 0.0)
    apply_weights(row_idx, col_idx, pieces, vectors, total, unroll)
    store_sums(out, total, small)


def send(out, vectors, small):
    tile = encode(small)
    for b in range(8):
        out[b] = vectors[:, b * BLOCK : (b + 1) * BLOCK].astype(BF16)
    out[8] = tile


def receive(recv):
    peers = recv.shape[0]
    tiles = []
    for b in range(8):
        tile = recv[0, b].astype(F32)
        for p in range(1, peers):
            tile = tile + recv[p, b].astype(F32)
        tiles.append(tile)
    return jnp.concatenate(tiles, axis=1), decode([recv[p, 8].astype(F32) for p in range(peers)])


def stacked(parts):
    width = parts[0].shape[1]
    return jnp.concatenate(parts + [jnp.zeros((7, width), F32)], axis=0)


def start_kernel(start_ref, after_ref, out, flat_out):
    start = jnp.concatenate([start_ref[:, b, :] for b in range(8)], axis=1)
    flat_out[...] = start
    for b in range(8):
        out[b] = start[:, b * BLOCK : (b + 1) * BLOCK]
    out[8] = pad_lanes(dot_t(start, start))


def first_kernel(recv, degree_ref, start_ref, out, basis_out, image_out, trivial_out):
    swept, small = receive(recv)
    degree = degree_ref[...]
    scale = lax.rsqrt(degree)
    total = small[0:1, 33:34]
    trivial = jnp.sqrt(degree / total)
    coef = small[:, 32:33] * lax.rsqrt(total)
    lanes = iota((VECS, BLOCK), 1)
    wide = jnp.where(lanes == 0, coef, 0.0)
    gram = small[:, :VECS] - dot_t(wide, wide)
    upper, inverse = factor_inverse(gram)
    along = coef * trivial
    both = dot(
        inverse,
        jnp.concatenate([start_ref[...] - along, swept * scale - along], axis=1),
    )
    width = degree.shape[1]
    basis, image = both[:, :width], both[:, width:]
    basis_out[...] = basis
    image_out[...] = image
    trivial_out[...] = trivial
    send(out, image * scale, pad_lanes(dot_t(image, stacked([basis, image, trivial]))))


def second_kernel(
    recv, degree_ref, trivial_ref, basis_ref, image_ref, out, basis_out, image_out, rest_out, mats
):
    swept, small = receive(recv)
    scale = lax.rsqrt(degree_ref[...])
    trivial = trivial_ref[...]
    alpha_t = small[:, :VECS]
    gram = small[:, VECS : 2 * VECS] - dot_t(alpha_t, alpha_t)
    upper, inverse = factor_inverse(gram)
    width = trivial.shape[1]
    mixed = dot(alpha_t, jnp.concatenate([basis_ref[...], image_ref[...]], axis=1))
    residual = image_ref[...] - mixed[:, :width]
    applied = swept * scale - small[:, 2 * VECS : 2 * VECS + 1] * trivial - mixed[:, width:]
    both = dot(inverse, jnp.concatenate([residual, applied], axis=1))
    basis, image = both[:, :width], both[:, width:]
    rest = image - dot(upper, basis_ref[...])
    basis_out[...] = basis
    image_out[...] = image
    rest_out[...] = rest
    mats[0] = alpha_t
    mats[1] = upper
    send(out, rest * scale, pad_lanes(dot_t(rest, stacked([basis, rest, trivial]))))


def third_kernel(
    recv, degree_ref, trivial_ref, basis_ref, image_ref, rest_ref, out, basis_out, rest_out, mats
):
    swept, small = receive(recv)
    scale = lax.rsqrt(degree_ref[...])
    trivial = trivial_ref[...]
    alpha_t = small[:, :VECS]
    gram = small[:, VECS : 2 * VECS] - dot_t(alpha_t, alpha_t)
    upper, inverse = factor_inverse(gram)
    width = trivial.shape[1]
    mixed = dot(alpha_t, jnp.concatenate([basis_ref[...], image_ref[...]], axis=1))
    residual = rest_ref[...] - mixed[:, :width]
    applied = swept * scale - small[:, 2 * VECS : 2 * VECS + 1] * trivial - mixed[:, width:]
    both = dot(inverse, jnp.concatenate([residual, applied], axis=1))
    basis, image = both[:, :width], both[:, width:]
    rest = image - dot(upper, basis_ref[...])
    basis_out[...] = basis
    rest_out[...] = rest
    mats[0] = alpha_t
    mats[1] = upper
    small = pad_lanes(
        dot_t(rest, jnp.concatenate([basis, rest], axis=0))
    )
    packed = small[0:4, :]
    for q in range(1, 4):
        packed = packed + pltpu.roll(small[4 * q : 4 * q + 4, :], 32 * q, 1)
    tile = jnp.concatenate([packed] * 4, axis=0).astype(BF16)
    for p in range(out.shape[0] // 16):
        out[p * 16 : (p + 1) * 16, :] = tile


def last_kernel(recv, basis_ref, rest_ref, mats_a, mats_b, alphas, betas, out, *, norm):
    tile = recv[0:16, :].astype(F32)
    for p in range(1, recv.shape[0] // 16):
        tile = tile + recv[p * 16 : (p + 1) * 16, :].astype(F32)
    packed = tile[0:4, :] + tile[4:8, :] + tile[8:12, :] + tile[12:16, :]
    lanes = iota((4, BLOCK), 1)
    rows = []
    for q in range(4):
        part = packed if q == 0 else pltpu.roll(packed, BLOCK - 32 * q, 1)
        rows.append(jnp.where(lanes < 32, part, 0.0))
    small = jnp.concatenate(rows, axis=0)
    alpha_t = small[:, :VECS]
    gram = small[:, VECS : 2 * VECS] - dot_t(alpha_t, alpha_t)
    upper, inverse = factor_inverse(gram)
    final = dot(inverse * norm, rest_ref[...] - dot(alpha_t, basis_ref[...]))
    for b in range(8):
        out[:, b, :] = final[:, b * BLOCK : (b + 1) * BLOCK]
    alphas[0] = mats_a[0].T
    alphas[1] = mats_b[0].T
    alphas[2] = alpha_t.T
    betas[0] = mats_a[1]
    betas[1] = mats_b[1]
    betas[2] = upper


def call(kernel, out_shape, mib, *args, scratch=(), specs=None, out_specs=None, aliases=None):
    outs = out_shape if isinstance(out_shape, (list, tuple)) else None
    return pl.pallas_call(
        kernel,
        out_shape=out_shape,
        in_specs=specs or [whole()] * len(args),
        out_specs=out_specs or ([whole()] * len(outs) if outs else whole()),
        scratch_shapes=list(scratch),
        input_output_aliases=aliases or {},
        compiler_params=params(mib),
    )(*args)


def exchange(values, axis):
    return lax.all_to_all(values, axis, split_axis=0, concat_axis=0, tiled=True)


def column_parts(own, rows):
    parts = [own] + [toggled(own, m, rows) for m in range(2, rows, 2)]
    return [p for part in parts for p in (part, toggled(part, 1, rows))]


def toggled(values, bits, size):
    return lax.ppermute(values, "row", [(i, i ^ bits) for i in range(size)])


def shape(dims, dtype=F32):
    return jax.ShapeDtypeStruct(dims, dtype)


def on_device(descriptors, send_slot, recv_slot, block_pairs, start):
    rows = lax.axis_size("row")
    cols = lax.axis_size("col")
    count = rows * cols
    slots = descriptors.shape[1]
    seg = recv_slot.shape[0]
    nblk = seg // BLOCK
    nrow, ncol = cols * nblk, rows * nblk
    own = jnp.arange(nblk, dtype=jnp.int32)
    me = lax.axis_index("row")
    row_idx = jnp.concatenate([block_pairs[0], lax.axis_index("col") * nblk + own, me[None]])
    col_idx = jnp.concatenate([block_pairs[1], me * nblk + own])
    skip_idx = col_idx + col_idx // nblk
    groups = col_idx.shape[0] // 4
    unroll = math.gcd(GROUP_UNROLL, groups // PIECES)

    with jax.named_scope("relay"):
        packed_rows = slots // 4
        outgoing, slots_in = call(
            relay_out_kernel,
            [shape((packed_rows, BLOCK), BF16), shape((nblk, BLOCK), jnp.int32)],
            16,
            send_slot.reshape(slots // BLOCK, BLOCK),
            descriptors,
            recv_slot.reshape(nblk, BLOCK),
            scratch=[VMEM((packed_rows, slots), BF16), VMEM((BLOCK, slots), BF16)],
        )
        received = exchange(outgoing, AXES)
        row_copies, own_desc = call(
            relay_in_kernel,
            [shape((nrow, FEAT, BLOCK), BF16), shape((nblk, FEAT, BLOCK), BF16)],
            16,
            slots_in,
            received,
        )
    with jax.named_scope("gather"):
        row_desc = exchange(row_copies, "col")
        begin_tiles, begin = call(
            start_kernel,
            [shape((nblk + 1, VECS, BLOCK)), shape((VECS, seg))],
            4,
            start,
            own_desc,
            specs=[whole(), pl.BlockSpec(memory_space=pl.ANY)],
        )
        begins = column_parts(begin_tiles, rows)
        left = call(
            left_kernel,
            shape((ncol, BLOCK, BLOCK), BF16),
            4,
            row_idx,
            *column_parts(own_desc, rows),
            specs=[smem()] + [whole()] * rows,
        )
    with jax.named_scope("build"):
        wshape = pltpu.VMEM((groups // PIECES, 2 * BLOCK, 2 * BLOCK), BF16)
        empty = call(
            empty_kernel,
            [wshape] * PIECES,
            1,
            row_desc,
            left,
            row_idx,
            col_idx,
            skip_idx,
            specs=[pl.BlockSpec(memory_space=pl.ANY)] * 5,
        )
        empty = [pltpu.with_memory_space_constraint(piece, pltpu.VMEM) for piece in empty]
        *weights, degree_part = call(
            functools.partial(build_kernel, unroll=unroll),
            [wshape] * PIECES + [shape((ncol, BLOCK))],
            8,
            row_idx,
            col_idx,
            row_desc,
            left,
            *empty,
            scratch=[
                VMEM((nrow, BLOCK // 2, BLOCK), BF16),
                VMEM((ncol, BLOCK, BLOCK), F32),
            ],
            specs=[smem(), smem(), whole(), whole()] + [pl.BlockSpec(memory_space=pl.ANY)] * PIECES,
            aliases={4 + k: k for k in range(PIECES)},
        )
        weights = [pltpu.with_memory_space_constraint(piece, pltpu.VMEM) for piece in weights]
    def sweep(sent):
        vectors = column_parts(sent, rows)
        partial_sum = call(
            functools.partial(sweep_kernel, unroll=unroll, peers=rows),
            shape((cols, 9, VECS, BLOCK), BF16),
            8,
            row_idx,
            skip_idx,
            *weights,
            *vectors,
            scratch=[VMEM((rows * 9, VECS, BLOCK), BF16), VMEM((nrow, VECS, BLOCK), F32)],
            specs=[smem(), smem()] + [whole()] * (PIECES + rows),
        )
        return exchange(partial_sum, "col")

    vec = shape((VECS, seg))
    sending = shape((9, VECS, BLOCK), BF16)
    mats = shape((2, VECS, VECS))
    with jax.named_scope("step0"):
        partial_sum, degree = call(
            functools.partial(first_sweep_kernel, unroll=unroll, peers=rows),
            [shape((cols, 9, VECS, BLOCK), BF16), shape((1, seg))],
            8,
            row_idx,
            skip_idx,
            *weights,
            *begins,
            *column_parts(degree_part, rows),
            scratch=[
                VMEM((rows * 9, VECS, BLOCK), BF16),
                VMEM((nrow, VECS, BLOCK), F32),
                VMEM((ncol, BLOCK), F32),
            ],
            specs=[smem(), smem()] + [whole()] * (PIECES + 2 * rows),
        )
        swept = exchange(partial_sum, "col")
        sent, basis0, image0, trivial = call(
            first_kernel, [sending, vec, vec, shape((1, seg))], 8, swept, degree, begin
        )
    with jax.named_scope("step1"):
        swept = sweep(sent)
        sent, basis1, image1, rest1, mats0 = call(
            second_kernel, [sending, vec, vec, vec, mats], 8, swept, degree, trivial, basis0, image0
        )
    with jax.named_scope("step2"):
        swept = sweep(sent)
        small, basis2, rest2, mats1 = call(
            third_kernel,
            [shape((count * 4, BLOCK), BF16), vec, vec, mats],
            8,
            swept,
            degree,
            trivial,
            basis1,
            image1,
            rest1,
        )
    with jax.named_scope("finish"):
        three = shape((3, VECS, VECS))
        return tuple(
            call(
                functools.partial(last_kernel, norm=math.sqrt(count * seg)),
                [three, three, shape((VECS, nblk, BLOCK))],
                8,
                exchange(small, AXES),
                basis2,
                rest2,
                mats0,
                mats1,
            )
        )


def solution(mesh):
    return jax.shard_map(
        on_device,
        mesh=mesh,
        in_specs=(
            P(None, ("row", "col")),
            P(("row", "col")),
            P(("row", "col")),
            P(None, ("row", "col")),
            P(None, ("row", "col"), None),
        ),
        out_specs=(P(), P(), P(None, ("row", "col"), None)),
        check_vma=False,
    )
```

```python
import functools
import math

import jax
import jax.numpy as jnp
from jax import lax
from jax.experimental import pallas as pl
from jax.experimental.pallas import tpu as pltpu
from jax.sharding import PartitionSpec as P

FEAT = 32
BLOCK = 128
VECS = 16
BUILD_UNROLL = 43
SWEEP_UNROLL = 129
PIECES = 2
EXP2_SCALE = math.log2(math.e) / (2.0 * FEAT)
AXES = ("row", "col")
F32 = jnp.float32
BF16 = jnp.bfloat16
HIGHEST = lax.Precision.HIGHEST
VMEM = pltpu.VMEM


def params(mib):
    return pltpu.CompilerParams(vmem_limit_bytes=mib << 20)


def whole():
    return pl.BlockSpec(memory_space=pltpu.VMEM)


def smem():
    return pl.BlockSpec(memory_space=pltpu.SMEM)


def iota(shape, dim):
    return lax.broadcasted_iota(jnp.int32, shape, dim)


def split3(x):
    high = x.astype(BF16).astype(F32)
    rest = x - high
    middle = rest.astype(BF16).astype(F32)
    low = (rest - middle).astype(BF16).astype(F32)
    return high, middle, low


def dot(left, right):
    return jnp.dot(left, right, precision=HIGHEST, preferred_element_type=F32)


def dot_t(left, right):
    return lax.dot_general(
        left, right, (((1,), (1,)), ((), ())), precision=HIGHEST, preferred_element_type=F32
    )


def encode(small):
    high, middle, low = split3(small)
    return (high + pltpu.roll(middle, 40, 1) + pltpu.roll(low, 80, 1)).astype(BF16)


def decode(tiles):
    total = sum(tiles)
    value = total + pltpu.roll(total, 88, 1) + pltpu.roll(total, 48, 1)
    return jnp.where(iota((VECS, BLOCK), 1) < 40, value, 0.0)


def pad_lanes(small):
    return jnp.concatenate([small, jnp.zeros((VECS, BLOCK - small.shape[1]), F32)], axis=1)


def factor_inverse(gram):
    rows = iota((VECS, BLOCK), 0)
    lanes = iota((VECS, BLOCK), 1)
    work = pad_lanes(gram) + jnp.where(lanes == rows + VECS, 1.0, 0.0)
    columns = [jnp.broadcast_to(work[:, k : k + 1], work.shape) for k in range(VECS)]
    for k in range(VECS):
        inverse = 1.0 / columns[k][k : k + 1, :]
        ratio = jnp.where(rows > k, columns[k], 0.0) * inverse
        for n in range(k + 1, VECS):
            columns[n] = columns[n] - ratio * columns[n][k : k + 1, :]
        work = work - ratio * work[k : k + 1, :]
    diagonal = jnp.sum(jnp.where(lanes == rows, work, 0.0), axis=1, keepdims=True)
    scaled = work * lax.rsqrt(diagonal)
    upper = jnp.where(lanes >= rows, scaled, 0.0)[:, :VECS]
    return upper, scaled[:, VECS : 2 * VECS]


def relay_out_kernel(
    slot_in, desc_in, recv_slot_in, out_ref, recv_slot_out, slot_ref, desc_ref, hot_ref, spread_ref, sems
):
    copies = [
        pltpu.make_async_copy(slot_in, slot_ref, sems.at[0]),
        pltpu.make_async_copy(desc_in, desc_ref, sems.at[1]),
        pltpu.make_async_copy(recv_slot_in, recv_slot_out, sems.at[2]),
    ]
    for copy in copies:
        copy.start()
    for copy in copies:
        copy.wait()
    slots = slot_ref.shape[0] * BLOCK
    rows = out_ref.shape[0]
    target = iota((rows, BLOCK), 0)
    for t in range(slots // BLOCK):
        cut = pl.ds(t * BLOCK, BLOCK)
        slot = slot_ref[t : t + 1, :]
        hot_ref[:, cut] = jnp.where(target == (slot >> 2), 1.0, 0.0).astype(BF16)
        desc = desc_ref[:, cut].astype(F32)
        quarter = slot & 3
        for q in range(4):
            spread_ref[q * FEAT : (q + 1) * FEAT, cut] = jnp.where(quarter == q, desc, 0.0).astype(
                BF16
            )
    out_ref[...] = lax.dot_general(
        hot_ref[...], spread_ref[...], (((1,), (1,)), ((), ())), preferred_element_type=F32
    ).astype(BF16)


def relay_in_kernel(slot_ref, recv_ref, row_ref, own_ref):
    rows = recv_ref.shape[0]
    nblk = slot_ref.shape[0]
    received = recv_ref[...].astype(F32).T.astype(BF16)
    source = iota((rows, BLOCK), 0)
    for b in range(nblk):
        slot = slot_ref[b : b + 1, :]
        hot = jnp.where(source == (slot >> 2), 1.0, 0.0).astype(BF16)
        picked = jnp.dot(received, hot, preferred_element_type=F32)
        quarter = slot & 3
        own = jnp.zeros((FEAT, BLOCK), F32)
        for q in range(4):
            own = own + jnp.where(quarter == q, picked[q * FEAT : (q + 1) * FEAT, :], 0.0)
        own = own.astype(BF16)
        for copy in range(row_ref.shape[0] // nblk):
            row_ref[copy * nblk + b] = own
        own_ref[b] = own


def empty_kernel(*refs):
    for ref in refs[-PIECES:]:
        ref[0, 0:16, 0:BLOCK] = jnp.zeros((16, BLOCK), BF16)


def features(block, sign):
    values = block.astype(F32)
    pieces = split3(jnp.sum(values * values, axis=0, keepdims=True))
    rows = iota((BLOCK - FEAT, BLOCK), 0)
    tail = jnp.zeros((BLOCK - FEAT, BLOCK), F32)
    for n in range(3):
        if sign:
            tail = jnp.where(rows == n, -pieces[n], tail)
            tail = jnp.where(rows == n + 3, 1.0, tail)
        else:
            tail = jnp.where(rows == n, 1.0, tail)
            tail = jnp.where(rows == n + 3, -pieces[n], tail)
    scale = 2.0 if sign else 1.0
    return jnp.concatenate([values * scale, tail], axis=0).astype(BF16)


def each_piece(pieces, body, unroll):
    first = 0
    for weights in pieces:
        count = weights.shape[0]
        lax.fori_loop(0, count // unroll, functools.partial(body, weights=weights, first=first), 0)
        first += count


def left_kernel(row_idx, *refs):
    col_desc, left = refs[:-1], refs[-1]
    me = row_idx[row_idx.shape[0] - 1]
    eye = jnp.where(
        iota((BLOCK, BLOCK), 0) == iota((BLOCK, BLOCK), 1), 1.0, 0.0
    ).astype(BF16)
    for m, part in enumerate(col_desc):
        nblk = part.shape[0]
        for k in range(nblk):
            rows = features(part[k], False)
            left[(me ^ m) * nblk + k] = lax.dot_general(
                eye, rows, (((1,), (1,)), ((), ())), preferred_element_type=F32
            ).astype(BF16)


def build_kernel(row_idx, col_idx, row_desc, left, *refs, unroll):
    pieces = refs[PIECES : 2 * PIECES]
    degree, right, total = refs[2 * PIECES :]
    nrow = row_desc.shape[0]

    def prepare_row(n, carry):
        for k in range(8):
            right[n * 8 + k] = features(row_desc[n * 8 + k], True)
            total[n * 8 + k] = jnp.zeros((8, BLOCK), F32)
        return carry

    lax.fori_loop(0, nrow // 8, prepare_row, 0)

    def several(step, carry, weights, first):
        for u in range(unroll):
            group = step * unroll + u
            for q in range(4):
                i = row_idx[(first + group) * 4 + q]
                j = col_idx[(first + group) * 4 + q]
                power = jnp.dot(left[j], right[i], preferred_element_type=F32)
                block = jnp.exp2(power * EXP2_SCALE).astype(BF16)
                r, c = q // 2, q % 2
                weights[group, r * BLOCK : (r + 1) * BLOCK, c * BLOCK : (c + 1) * BLOCK] = block
                total[i] += jnp.sum(block.astype(F32).reshape(BLOCK // 8, 8, BLOCK), axis=0)
        return carry

    each_piece(pieces, several, unroll)
    for n in range(nrow):
        degree[n // 8, n % 8 : n % 8 + 1, :] = jnp.sum(total[n], axis=0, keepdims=True)


def sweep_kernel(row_idx, col_idx, *refs, unroll, peers):
    pieces = refs[:PIECES]
    parts = refs[PIECES : PIECES + peers]
    out, vectors, total = refs[PIECES + peers :]
    me = row_idx[row_idx.shape[0] - 1]
    for m in range(peers):
        for b in range(9):
            vectors[(me ^ m) * 9 + b] = parts[m][b]
    total[...] = jnp.zeros_like(total)
    zero = jnp.zeros((VECS, BLOCK), BF16)

    def several(step, carry, weights, first):
        for u in range(unroll):
            group = step * unroll + u
            picked = [vectors[col_idx[(first + group) * 4 + q]] for q in range(4)]
            lhs = jnp.concatenate(
                [
                    jnp.concatenate([picked[0], zero], 1),
                    jnp.concatenate([zero, picked[2]], 1),
                    jnp.concatenate([picked[1], zero], 1),
                    jnp.concatenate([zero, picked[3]], 1),
                ],
                0,
            )
            result = jnp.dot(lhs, weights[group], preferred_element_type=F32)
            for place, q in enumerate((0, 2, 1, 3)):
                half = (q % 2) * BLOCK
                total[row_idx[(first + group) * 4 + q]] += result[
                    place * VECS : (place + 1) * VECS, half : half + BLOCK
                ]
        return carry

    each_piece(pieces, several, unroll)
    small = encode(decode([part[8].astype(F32) for part in parts]))
    for n in range(total.shape[0]):
        out[n // 8, n % 8] = total[n].astype(BF16)
    for p in range(out.shape[0]):
        out[p, 8] = small


def row_vector(block):
    return jnp.concatenate([block[b : b + 1, :] for b in range(8)], axis=1)


def send(out, vectors, small):
    tile = encode(small)
    for b in range(8):
        out[b] = vectors[:, b * BLOCK : (b + 1) * BLOCK].astype(BF16)
    out[8] = tile


def receive(recv):
    peers = recv.shape[0]
    tiles = []
    for b in range(8):
        tile = recv[0, b].astype(F32)
        for p in range(1, peers):
            tile = tile + recv[p, b].astype(F32)
        tiles.append(tile)
    return jnp.concatenate(tiles, axis=1), decode([recv[p, 8].astype(F32) for p in range(peers)])


def stacked(parts):
    width = parts[0].shape[1]
    return jnp.concatenate(parts + [jnp.zeros((7, width), F32)], axis=0)


def scale_kernel(degree_ref, start_ref, out, degree_out, start_out):
    degree = degree_ref[0]
    for p in range(1, degree_ref.shape[0]):
        degree = degree + degree_ref[p]
    flat = row_vector(degree)
    scale = lax.rsqrt(flat)
    start = jnp.concatenate([start_ref[:, b, :] for b in range(8)], axis=1)
    degree_out[...] = flat
    start_out[...] = start
    root = jnp.sqrt(flat)
    small = pad_lanes(dot_t(start, stacked([start, jnp.zeros_like(start), root])))
    whole_sum = jnp.sum(flat, axis=1, keepdims=True)
    first = (iota((VECS, BLOCK), 0) == 0) & (iota((VECS, BLOCK), 1) == 33)
    small = small + jnp.where(first, whole_sum, 0.0)
    send(out, start * scale, small)


def first_kernel(recv, degree_ref, start_ref, out, basis_out, image_out, trivial_out):
    swept, small = receive(recv)
    degree = degree_ref[...]
    scale = lax.rsqrt(degree)
    total = small[0:1, 33:34]
    trivial = jnp.sqrt(degree / total)
    coef = small[:, 32:33] * lax.rsqrt(total)
    lanes = iota((VECS, BLOCK), 1)
    wide = jnp.where(lanes == 0, coef, 0.0)
    gram = small[:, :VECS] - dot_t(wide, wide)
    upper, inverse = factor_inverse(gram)
    along = coef * trivial
    both = dot(
        inverse,
        jnp.concatenate([start_ref[...] - along, swept * scale - along], axis=1),
    )
    width = degree.shape[1]
    basis, image = both[:, :width], both[:, width:]
    basis_out[...] = basis
    image_out[...] = image
    trivial_out[...] = trivial
    send(out, image * scale, pad_lanes(dot_t(image, stacked([basis, image, trivial]))))


def second_kernel(
    recv, degree_ref, trivial_ref, basis_ref, image_ref, out, basis_out, image_out, rest_out, mats
):
    swept, small = receive(recv)
    scale = lax.rsqrt(degree_ref[...])
    trivial = trivial_ref[...]
    alpha_t = small[:, :VECS]
    gram = small[:, VECS : 2 * VECS] - dot_t(alpha_t, alpha_t)
    upper, inverse = factor_inverse(gram)
    width = trivial.shape[1]
    mixed = dot(alpha_t, jnp.concatenate([basis_ref[...], image_ref[...]], axis=1))
    residual = image_ref[...] - mixed[:, :width]
    applied = swept * scale - small[:, 2 * VECS : 2 * VECS + 1] * trivial - mixed[:, width:]
    both = dot(inverse, jnp.concatenate([residual, applied], axis=1))
    basis, image = both[:, :width], both[:, width:]
    rest = image - dot(upper, basis_ref[...])
    basis_out[...] = basis
    image_out[...] = image
    rest_out[...] = rest
    mats[0] = alpha_t
    mats[1] = upper
    send(out, rest * scale, pad_lanes(dot_t(rest, stacked([basis, rest, trivial]))))


def third_kernel(
    recv, degree_ref, trivial_ref, basis_ref, image_ref, rest_ref, out, basis_out, rest_out, mats
):
    swept, small = receive(recv)
    scale = lax.rsqrt(degree_ref[...])
    trivial = trivial_ref[...]
    alpha_t = small[:, :VECS]
    gram = small[:, VECS : 2 * VECS] - dot_t(alpha_t, alpha_t)
    upper, inverse = factor_inverse(gram)
    width = trivial.shape[1]
    mixed = dot(alpha_t, jnp.concatenate([basis_ref[...], image_ref[...]], axis=1))
    residual = rest_ref[...] - mixed[:, :width]
    applied = swept * scale - small[:, 2 * VECS : 2 * VECS + 1] * trivial - mixed[:, width:]
    both = dot(inverse, jnp.concatenate([residual, applied], axis=1))
    basis, image = both[:, :width], both[:, width:]
    rest = image - dot(upper, basis_ref[...])
    basis_out[...] = basis
    rest_out[...] = rest
    mats[0] = alpha_t
    mats[1] = upper
    small = pad_lanes(
        dot_t(rest, jnp.concatenate([basis, rest], axis=0))
    )
    packed = small[0:4, :]
    for q in range(1, 4):
        packed = packed + pltpu.roll(small[4 * q : 4 * q + 4, :], 32 * q, 1)
    tile = jnp.concatenate([packed] * 4, axis=0).astype(BF16)
    for p in range(out.shape[0] // 16):
        out[p * 16 : (p + 1) * 16, :] = tile


def last_kernel(recv, basis_ref, rest_ref, mats_a, mats_b, alphas, betas, out, *, norm):
    tile = recv[0:16, :].astype(F32)
    for p in range(1, recv.shape[0] // 16):
        tile = tile + recv[p * 16 : (p + 1) * 16, :].astype(F32)
    packed = tile[0:4, :] + tile[4:8, :] + tile[8:12, :] + tile[12:16, :]
    lanes = iota((4, BLOCK), 1)
    rows = []
    for q in range(4):
        part = packed if q == 0 else pltpu.roll(packed, BLOCK - 32 * q, 1)
        rows.append(jnp.where(lanes < 32, part, 0.0))
    small = jnp.concatenate(rows, axis=0)
    alpha_t = small[:, :VECS]
    gram = small[:, VECS : 2 * VECS] - dot_t(alpha_t, alpha_t)
    upper, inverse = factor_inverse(gram)
    final = dot(inverse * norm, rest_ref[...] - dot(alpha_t, basis_ref[...]))
    for b in range(8):
        out[:, b, :] = final[:, b * BLOCK : (b + 1) * BLOCK]
    alphas[0] = mats_a[0].T
    alphas[1] = mats_b[0].T
    alphas[2] = alpha_t.T
    betas[0] = mats_a[1]
    betas[1] = mats_b[1]
    betas[2] = upper


def call(kernel, out_shape, mib, *args, scratch=(), specs=None, out_specs=None, aliases=None):
    outs = out_shape if isinstance(out_shape, (list, tuple)) else None
    return pl.pallas_call(
        kernel,
        out_shape=out_shape,
        in_specs=specs or [whole()] * len(args),
        out_specs=out_specs or ([whole()] * len(outs) if outs else whole()),
        scratch_shapes=list(scratch),
        input_output_aliases=aliases or {},
        compiler_params=params(mib),
    )(*args)


def exchange(values, axis):
    return lax.all_to_all(values, axis, split_axis=0, concat_axis=0, tiled=True)


def column_parts(own, rows):
    parts = [own] + [toggled(own, m, rows) for m in range(2, rows, 2)]
    return [p for part in parts for p in (part, toggled(part, 1, rows))]


def toggled(values, bits, size):
    return lax.ppermute(values, "row", [(i, i ^ bits) for i in range(size)])


def shape(dims, dtype=F32):
    return jax.ShapeDtypeStruct(dims, dtype)


def on_device(descriptors, send_slot, recv_slot, block_pairs, start):
    rows = lax.axis_size("row")
    cols = lax.axis_size("col")
    count = rows * cols
    feat, slots = descriptors.shape
    seg = recv_slot.shape[0]
    nblk = seg // BLOCK
    nrow, ncol = cols * nblk, rows * nblk
    own = jnp.arange(nblk, dtype=jnp.int32)
    me = lax.axis_index("row")
    row_idx = jnp.concatenate([block_pairs[0], lax.axis_index("col") * nblk + own, me[None]])
    col_idx = jnp.concatenate([block_pairs[1], me * nblk + own])
    skip_idx = col_idx + col_idx // nblk
    groups = col_idx.shape[0] // 4
    build_unroll = math.gcd(BUILD_UNROLL, groups // PIECES)
    sweep_unroll = math.gcd(SWEEP_UNROLL, groups // PIECES)

    with jax.named_scope("relay"):
        packed_rows = slots // 4
        outgoing, slots_in = call(
            relay_out_kernel,
            [shape((packed_rows, BLOCK), BF16), shape((nblk, BLOCK), jnp.int32)],
            16,
            pltpu.with_memory_space_constraint(send_slot.reshape(slots // BLOCK, BLOCK), pltpu.HBM),
            pltpu.with_memory_space_constraint(descriptors, pltpu.HBM),
            pltpu.with_memory_space_constraint(recv_slot.reshape(nblk, BLOCK), pltpu.HBM),
            scratch=[
                VMEM((slots // BLOCK, BLOCK), jnp.int32),
                VMEM((feat, slots), BF16),
                VMEM((packed_rows, slots), BF16),
                VMEM((BLOCK, slots), BF16),
                pltpu.SemaphoreType.DMA((3,)),
            ],
            specs=[pl.BlockSpec(memory_space=pltpu.HBM)] * 3,
        )
        received = exchange(outgoing, AXES)
        row_copies, own_desc = call(
            relay_in_kernel,
            [shape((nrow, FEAT, BLOCK), BF16), shape((nblk, FEAT, BLOCK), BF16)],
            16,
            slots_in,
            received,
        )
    with jax.named_scope("gather"):
        row_desc = exchange(row_copies, "col")
        left = call(
            left_kernel,
            shape((ncol, BLOCK, BLOCK), BF16),
            4,
            row_idx,
            *column_parts(own_desc, rows),
            specs=[smem()] + [whole()] * rows,
        )
    with jax.named_scope("build"):
        wshape = pltpu.VMEM((groups // PIECES, 2 * BLOCK, 2 * BLOCK), BF16)
        empty = call(
            empty_kernel,
            [wshape] * PIECES,
            1,
            row_desc,
            left,
            row_idx,
            col_idx,
            skip_idx,
            specs=[pl.BlockSpec(memory_space=pl.ANY)] * 5,
        )
        empty = [pltpu.with_memory_space_constraint(piece, pltpu.VMEM) for piece in empty]
        *weights, degree_part = call(
            functools.partial(build_kernel, unroll=build_unroll),
            [wshape] * PIECES + [shape((cols, nblk, BLOCK))],
            8,
            row_idx,
            col_idx,
            row_desc,
            left,
            *empty,
            scratch=[
                VMEM((nrow, BLOCK, BLOCK), BF16),
                VMEM((nrow, 8, BLOCK), F32),
            ],
            specs=[smem(), smem(), whole(), whole()] + [pl.BlockSpec(memory_space=pl.ANY)] * PIECES,
            aliases={4 + k: k for k in range(PIECES)},
        )
        weights = [pltpu.with_memory_space_constraint(piece, pltpu.VMEM) for piece in weights]
    with jax.named_scope("degree"):
        sent, degree, begin = call(
            scale_kernel,
            [shape((9, VECS, BLOCK), BF16), shape((1, seg)), shape((VECS, seg))],
            8,
            exchange(degree_part, "col"),
            start,
        )

    def sweep(sent):
        vectors = column_parts(sent, rows)
        partial_sum = call(
            functools.partial(sweep_kernel, unroll=sweep_unroll, peers=rows),
            shape((cols, 9, VECS, BLOCK), BF16),
            8,
            row_idx,
            skip_idx,
            *weights,
            *vectors,
            scratch=[VMEM((rows * 9, VECS, BLOCK), BF16), VMEM((nrow, VECS, BLOCK), F32)],
            specs=[smem(), smem()] + [whole()] * (PIECES + rows),
        )
        return exchange(partial_sum, "col")

    vec = shape((VECS, seg))
    sending = shape((9, VECS, BLOCK), BF16)
    mats = shape((2, VECS, VECS))
    with jax.named_scope("step0"):
        swept = sweep(sent)
        sent, basis0, image0, trivial = call(
            first_kernel, [sending, vec, vec, shape((1, seg))], 8, swept, degree, begin
        )
    with jax.named_scope("step1"):
        swept = sweep(sent)
        sent, basis1, image1, rest1, mats0 = call(
            second_kernel, [sending, vec, vec, vec, mats], 8, swept, degree, trivial, basis0, image0
        )
    with jax.named_scope("step2"):
        swept = sweep(sent)
        small, basis2, rest2, mats1 = call(
            third_kernel,
            [shape((count * 4, BLOCK), BF16), vec, vec, mats],
            8,
            swept,
            degree,
            trivial,
            basis1,
            image1,
            rest1,
        )
    with jax.named_scope("finish"):
        three = shape((3, VECS, VECS))
        return tuple(
            call(
                functools.partial(last_kernel, norm=math.sqrt(count * seg)),
                [three, three, shape((VECS, nblk, BLOCK))],
                8,
                exchange(small, AXES),
                basis2,
                rest2,
                mats0,
                mats1,
            )
        )


def solution(mesh):
    return jax.shard_map(
        on_device,
        mesh=mesh,
        in_specs=(
            P(None, ("row", "col")),
            P(("row", "col")),
            P(("row", "col")),
            P(None, ("row", "col")),
            P(None, ("row", "col"), None),
        ),
        out_specs=(P(), P(), P(None, ("row", "col"), None)),
        check_vma=False,
    )
```

```python
import functools
import math

import jax
import jax.numpy as jnp
from jax import lax
from jax.experimental import pallas as pl
from jax.experimental.pallas import tpu as pltpu
from jax.sharding import PartitionSpec as P

FEAT = 32
BLOCK = 128
VECS = 16
BUILD_UNROLL = 43
SWEEP_UNROLL = 43
PIECES = 2
EXP2_SCALE = math.log2(math.e) / (2.0 * FEAT)
AXES = ("row", "col")
F32 = jnp.float32
BF16 = jnp.bfloat16
HIGHEST = lax.Precision.HIGHEST
VMEM = pltpu.VMEM


def params(mib):
    return pltpu.CompilerParams(vmem_limit_bytes=mib << 20)


def whole():
    return pl.BlockSpec(memory_space=pltpu.VMEM)


def smem():
    return pl.BlockSpec(memory_space=pltpu.SMEM)


def iota(shape, dim):
    return lax.broadcasted_iota(jnp.int32, shape, dim)


def split3(x):
    high = x.astype(BF16).astype(F32)
    rest = x - high
    middle = rest.astype(BF16).astype(F32)
    low = (rest - middle).astype(BF16).astype(F32)
    return high, middle, low


def dot(left, right):
    return jnp.dot(left, right, precision=HIGHEST, preferred_element_type=F32)


def dot_t(left, right):
    return lax.dot_general(
        left, right, (((1,), (1,)), ((), ())), precision=HIGHEST, preferred_element_type=F32
    )


def encode(small):
    high, middle, low = split3(small)
    return (high + pltpu.roll(middle, 40, 1) + pltpu.roll(low, 80, 1)).astype(BF16)


def decode(tiles):
    total = sum(tiles)
    value = total + pltpu.roll(total, 88, 1) + pltpu.roll(total, 48, 1)
    return jnp.where(iota((VECS, BLOCK), 1) < 40, value, 0.0)


def pad_lanes(small):
    return jnp.concatenate([small, jnp.zeros((VECS, BLOCK - small.shape[1]), F32)], axis=1)


def factor_inverse(gram):
    rows = iota((VECS, BLOCK), 0)
    lanes = iota((VECS, BLOCK), 1)
    work = pad_lanes(gram) + jnp.where(lanes == rows + VECS, 1.0, 0.0)
    columns = [jnp.broadcast_to(work[:, k : k + 1], work.shape) for k in range(VECS)]
    for k in range(VECS):
        inverse = 1.0 / columns[k][k : k + 1, :]
        ratio = jnp.where(rows > k, columns[k], 0.0) * inverse
        for n in range(k + 1, VECS):
            columns[n] = columns[n] - ratio * columns[n][k : k + 1, :]
        work = work - ratio * work[k : k + 1, :]
    diagonal = jnp.sum(jnp.where(lanes == rows, work, 0.0), axis=1, keepdims=True)
    scaled = work * lax.rsqrt(diagonal)
    upper = jnp.where(lanes >= rows, scaled, 0.0)[:, :VECS]
    return upper, scaled[:, VECS : 2 * VECS]


def relay_out_kernel(
    slot_in, desc_in, recv_slot_in, out_ref, recv_slot_out, slot_ref, desc_ref, hot_ref, spread_ref, sems
):
    copies = [
        pltpu.make_async_copy(slot_in, slot_ref, sems.at[0]),
        pltpu.make_async_copy(desc_in, desc_ref, sems.at[1]),
        pltpu.make_async_copy(recv_slot_in, recv_slot_out, sems.at[2]),
    ]
    for copy in copies:
        copy.start()
    for copy in copies:
        copy.wait()
    slots = slot_ref.shape[0] * BLOCK
    rows = out_ref.shape[0]
    target = iota((rows, BLOCK), 0)
    for t in range(slots // BLOCK):
        cut = pl.ds(t * BLOCK, BLOCK)
        slot = slot_ref[t : t + 1, :]
        hot_ref[:, cut] = jnp.where(target == (slot >> 2), 1.0, 0.0).astype(BF16)
        desc = desc_ref[:, cut].astype(F32)
        quarter = slot & 3
        for q in range(4):
            spread_ref[q * FEAT : (q + 1) * FEAT, cut] = jnp.where(quarter == q, desc, 0.0).astype(
                BF16
            )
    out_ref[...] = lax.dot_general(
        hot_ref[...], spread_ref[...], (((1,), (1,)), ((), ())), preferred_element_type=F32
    ).astype(BF16)


def relay_in_kernel(slot_ref, recv_ref, row_ref, own_ref):
    rows = recv_ref.shape[0]
    nblk = slot_ref.shape[0]
    received = recv_ref[...].astype(F32).T.astype(BF16)
    source = iota((rows, BLOCK), 0)
    for b in range(nblk):
        slot = slot_ref[b : b + 1, :]
        hot = jnp.where(source == (slot >> 2), 1.0, 0.0).astype(BF16)
        picked = jnp.dot(received, hot, preferred_element_type=F32)
        quarter = slot & 3
        own = jnp.zeros((FEAT, BLOCK), F32)
        for q in range(4):
            own = own + jnp.where(quarter == q, picked[q * FEAT : (q + 1) * FEAT, :], 0.0)
        own = own.astype(BF16)
        for copy in range(row_ref.shape[0] // nblk):
            row_ref[copy * nblk + b] = own
        own_ref[b] = own


def empty_kernel(*refs):
    for ref in refs[-PIECES:]:
        ref[0, 0:16, 0:BLOCK] = jnp.zeros((16, BLOCK), BF16)


def features(block, sign):
    values = block.astype(F32)
    pieces = split3(jnp.sum(values * values, axis=0, keepdims=True))
    rows = iota((BLOCK - FEAT, BLOCK), 0)
    tail = jnp.zeros((BLOCK - FEAT, BLOCK), F32)
    for n in range(3):
        if sign:
            tail = jnp.where(rows == n, -pieces[n], tail)
            tail = jnp.where(rows == n + 3, 1.0, tail)
        else:
            tail = jnp.where(rows == n, 1.0, tail)
            tail = jnp.where(rows == n + 3, -pieces[n], tail)
    scale = 2.0 if sign else 1.0
    return jnp.concatenate([values * scale, tail], axis=0).astype(BF16)


def each_piece(pieces, body, unroll):
    first = 0
    for weights in pieces:
        count = weights.shape[0]
        lax.fori_loop(0, count // unroll, functools.partial(body, weights=weights, first=first), 0)
        first += count


def left_kernel(row_idx, *refs):
    col_desc, left = refs[:-1], refs[-1]
    me = row_idx[row_idx.shape[0] - 1]
    eye = jnp.where(
        iota((BLOCK, BLOCK), 0) == iota((BLOCK, BLOCK), 1), 1.0, 0.0
    ).astype(BF16)
    for m, part in enumerate(col_desc):
        nblk = part.shape[0]
        for k in range(nblk):
            rows = features(part[k], False)
            left[(me ^ m) * nblk + k] = lax.dot_general(
                eye, rows, (((1,), (1,)), ((), ())), preferred_element_type=F32
            ).astype(BF16)


def build_kernel(row_idx, col_idx, row_desc, left, *refs, unroll):
    pieces = refs[PIECES : 2 * PIECES]
    degree, right, total = refs[2 * PIECES :]
    nrow = row_desc.shape[0]

    def prepare_row(n, carry):
        for k in range(8):
            right[n * 8 + k] = features(row_desc[n * 8 + k], True)
            total[n * 8 + k] = jnp.zeros((8, BLOCK), F32)
        return carry

    lax.fori_loop(0, nrow // 8, prepare_row, 0)

    def several(step, carry, weights, first):
        for u in range(unroll):
            group = step * unroll + u
            for q in range(4):
                i = row_idx[(first + group) * 4 + q]
                j = col_idx[(first + group) * 4 + q]
                power = jnp.dot(left[j], right[i], preferred_element_type=F32)
                block = jnp.exp2(power * EXP2_SCALE).astype(BF16)
                r, c = q // 2, q % 2
                weights[group, r * BLOCK : (r + 1) * BLOCK, c * BLOCK : (c + 1) * BLOCK] = block
                total[i] += jnp.sum(block.astype(F32).reshape(BLOCK // 8, 8, BLOCK), axis=0)
        return carry

    each_piece(pieces, several, unroll)
    for n in range(nrow):
        degree[n // 8, n % 8 : n % 8 + 1, :] = jnp.sum(total[n], axis=0, keepdims=True)


def sweep_kernel(row_idx, col_idx, *refs, unroll, peers):
    pieces = refs[:PIECES]
    parts = refs[PIECES : PIECES + peers]
    out, vectors, total = refs[PIECES + peers :]
    me = row_idx[row_idx.shape[0] - 1]
    for m in range(peers):
        for b in range(9):
            vectors[(me ^ m) * 9 + b] = parts[m][b]
    total[...] = jnp.zeros_like(total)
    zero = jnp.zeros((VECS, BLOCK), BF16)

    def several(step, carry, weights, first):
        for u in range(unroll):
            group = step * unroll + u
            picked = [vectors[col_idx[(first + group) * 4 + q]] for q in range(4)]
            lhs = jnp.concatenate(
                [
                    jnp.concatenate([picked[0], zero], 1),
                    jnp.concatenate([zero, picked[2]], 1),
                    jnp.concatenate([picked[1], zero], 1),
                    jnp.concatenate([zero, picked[3]], 1),
                ],
                0,
            )
            result = jnp.dot(lhs, weights[group], preferred_element_type=F32)
            for place, q in enumerate((0, 2, 1, 3)):
                half = (q % 2) * BLOCK
                total[row_idx[(first + group) * 4 + q]] += result[
                    place * VECS : (place + 1) * VECS, half : half + BLOCK
                ]
        return carry

    each_piece(pieces, several, unroll)
    small = encode(decode([part[8].astype(F32) for part in parts]))
    for n in range(total.shape[0]):
        out[n // 8, n % 8] = total[n].astype(BF16)
    for p in range(out.shape[0]):
        out[p, 8] = small


def row_vector(block):
    return jnp.concatenate([block[b : b + 1, :] for b in range(8)], axis=1)


def send(out, vectors, small):
    tile = encode(small)
    for b in range(8):
        out[b] = vectors[:, b * BLOCK : (b + 1) * BLOCK].astype(BF16)
    out[8] = tile


def receive(recv):
    peers = recv.shape[0]
    tiles = []
    for b in range(8):
        tile = recv[0, b].astype(F32)
        for p in range(1, peers):
            tile = tile + recv[p, b].astype(F32)
        tiles.append(tile)
    return jnp.concatenate(tiles, axis=1), decode([recv[p, 8].astype(F32) for p in range(peers)])


def stacked(parts):
    width = parts[0].shape[1]
    return jnp.concatenate(parts + [jnp.zeros((7, width), F32)], axis=0)


def scale_kernel(degree_ref, start_ref, out, degree_out, start_out):
    degree = degree_ref[0]
    for p in range(1, degree_ref.shape[0]):
        degree = degree + degree_ref[p]
    flat = row_vector(degree)
    scale = lax.rsqrt(flat)
    start = jnp.concatenate([start_ref[:, b, :] for b in range(8)], axis=1)
    degree_out[...] = flat
    start_out[...] = start
    root = jnp.sqrt(flat)
    small = pad_lanes(dot_t(start, stacked([start, jnp.zeros_like(start), root])))
    whole_sum = jnp.sum(flat, axis=1, keepdims=True)
    first = (iota((VECS, BLOCK), 0) == 0) & (iota((VECS, BLOCK), 1) == 33)
    small = small + jnp.where(first, whole_sum, 0.0)
    send(out, start * scale, small)


def first_kernel(recv, degree_ref, start_ref, out, basis_out, image_out, trivial_out):
    swept, small = receive(recv)
    degree = degree_ref[...]
    scale = lax.rsqrt(degree)
    total = small[0:1, 33:34]
    trivial = jnp.sqrt(degree / total)
    coef = small[:, 32:33] * lax.rsqrt(total)
    lanes = iota((VECS, BLOCK), 1)
    wide = jnp.where(lanes == 0, coef, 0.0)
    gram = small[:, :VECS] - dot_t(wide, wide)
    upper, inverse = factor_inverse(gram)
    along = coef * trivial
    both = dot(
        inverse,
        jnp.concatenate([start_ref[...] - along, swept * scale - along], axis=1),
    )
    width = degree.shape[1]
    basis, image = both[:, :width], both[:, width:]
    basis_out[...] = basis
    image_out[...] = image
    trivial_out[...] = trivial
    send(out, image * scale, pad_lanes(dot_t(image, stacked([basis, image, trivial]))))


def second_kernel(
    recv, degree_ref, trivial_ref, basis_ref, image_ref, out, basis_out, image_out, rest_out, mats
):
    swept, small = receive(recv)
    scale = lax.rsqrt(degree_ref[...])
    trivial = trivial_ref[...]
    alpha_t = small[:, :VECS]
    gram = small[:, VECS : 2 * VECS] - dot_t(alpha_t, alpha_t)
    upper, inverse = factor_inverse(gram)
    width = trivial.shape[1]
    mixed = dot(alpha_t, jnp.concatenate([basis_ref[...], image_ref[...]], axis=1))
    residual = image_ref[...] - mixed[:, :width]
    applied = swept * scale - small[:, 2 * VECS : 2 * VECS + 1] * trivial - mixed[:, width:]
    both = dot(inverse, jnp.concatenate([residual, applied], axis=1))
    basis, image = both[:, :width], both[:, width:]
    rest = image - dot(upper, basis_ref[...])
    basis_out[...] = basis
    image_out[...] = image
    rest_out[...] = rest
    mats[0] = alpha_t
    mats[1] = upper
    send(out, rest * scale, pad_lanes(dot_t(rest, stacked([basis, rest, trivial]))))


def third_kernel(
    recv, degree_ref, trivial_ref, basis_ref, image_ref, rest_ref, out, basis_out, rest_out, mats
):
    swept, small = receive(recv)
    scale = lax.rsqrt(degree_ref[...])
    trivial = trivial_ref[...]
    alpha_t = small[:, :VECS]
    gram = small[:, VECS : 2 * VECS] - dot_t(alpha_t, alpha_t)
    upper, inverse = factor_inverse(gram)
    width = trivial.shape[1]
    mixed = dot(alpha_t, jnp.concatenate([basis_ref[...], image_ref[...]], axis=1))
    residual = rest_ref[...] - mixed[:, :width]
    applied = swept * scale - small[:, 2 * VECS : 2 * VECS + 1] * trivial - mixed[:, width:]
    both = dot(inverse, jnp.concatenate([residual, applied], axis=1))
    basis, image = both[:, :width], both[:, width:]
    rest = image - dot(upper, basis_ref[...])
    basis_out[...] = basis
    rest_out[...] = rest
    mats[0] = alpha_t
    mats[1] = upper
    small = pad_lanes(
        dot_t(rest, jnp.concatenate([basis, rest], axis=0))
    )
    packed = small[0:4, :]
    for q in range(1, 4):
        packed = packed + pltpu.roll(small[4 * q : 4 * q + 4, :], 32 * q, 1)
    tile = jnp.concatenate([packed] * 4, axis=0).astype(BF16)
    for p in range(out.shape[0] // 16):
        out[p * 16 : (p + 1) * 16, :] = tile


def last_kernel(recv, basis_ref, rest_ref, mats_a, mats_b, alphas, betas, out, *, norm):
    tile = recv[0:16, :].astype(F32)
    for p in range(1, recv.shape[0] // 16):
        tile = tile + recv[p * 16 : (p + 1) * 16, :].astype(F32)
    packed = tile[0:4, :] + tile[4:8, :] + tile[8:12, :] + tile[12:16, :]
    lanes = iota((4, BLOCK), 1)
    rows = []
    for q in range(4):
        part = packed if q == 0 else pltpu.roll(packed, BLOCK - 32 * q, 1)
        rows.append(jnp.where(lanes < 32, part, 0.0))
    small = jnp.concatenate(rows, axis=0)
    alpha_t = small[:, :VECS]
    gram = small[:, VECS : 2 * VECS] - dot_t(alpha_t, alpha_t)
    upper, inverse = factor_inverse(gram)
    final = dot(inverse * norm, rest_ref[...] - dot(alpha_t, basis_ref[...]))
    for b in range(8):
        out[:, b, :] = final[:, b * BLOCK : (b + 1) * BLOCK]
    alphas[0] = mats_a[0].T
    alphas[1] = mats_b[0].T
    alphas[2] = alpha_t.T
    betas[0] = mats_a[1]
    betas[1] = mats_b[1]
    betas[2] = upper


def call(kernel, out_shape, mib, *args, scratch=(), specs=None, out_specs=None, aliases=None):
    outs = out_shape if isinstance(out_shape, (list, tuple)) else None
    return pl.pallas_call(
        kernel,
        out_shape=out_shape,
        in_specs=specs or [whole()] * len(args),
        out_specs=out_specs or ([whole()] * len(outs) if outs else whole()),
        scratch_shapes=list(scratch),
        input_output_aliases=aliases or {},
        compiler_params=params(mib),
    )(*args)


def exchange(values, axis):
    return lax.all_to_all(values, axis, split_axis=0, concat_axis=0, tiled=True)


def column_parts(own, rows):
    parts = [own] + [toggled(own, m, rows) for m in range(2, rows, 2)]
    return [p for part in parts for p in (part, toggled(part, 1, rows))]


def toggled(values, bits, size):
    return lax.ppermute(values, "row", [(i, i ^ bits) for i in range(size)])


def shape(dims, dtype=F32):
    return jax.ShapeDtypeStruct(dims, dtype)


def on_device(descriptors, send_slot, recv_slot, block_pairs, start):
    rows = lax.axis_size("row")
    cols = lax.axis_size("col")
    count = rows * cols
    feat, slots = descriptors.shape
    seg = recv_slot.shape[0]
    nblk = seg // BLOCK
    nrow, ncol = cols * nblk, rows * nblk
    own = jnp.arange(nblk, dtype=jnp.int32)
    me = lax.axis_index("row")
    row_idx = jnp.concatenate([block_pairs[0], lax.axis_index("col") * nblk + own, me[None]])
    col_idx = jnp.concatenate([block_pairs[1], me * nblk + own])
    skip_idx = col_idx + col_idx // nblk
    groups = col_idx.shape[0] // 4
    build_unroll = math.gcd(BUILD_UNROLL, groups // PIECES)
    sweep_unroll = math.gcd(SWEEP_UNROLL, groups // PIECES)

    with jax.named_scope("relay"):
        packed_rows = slots // 4
        outgoing, slots_in = call(
            relay_out_kernel,
            [shape((packed_rows, BLOCK), BF16), shape((nblk, BLOCK), jnp.int32)],
            16,
            pltpu.with_memory_space_constraint(send_slot.reshape(slots // BLOCK, BLOCK), pltpu.HBM),
            pltpu.with_memory_space_constraint(descriptors, pltpu.HBM),
            pltpu.with_memory_space_constraint(recv_slot.reshape(nblk, BLOCK), pltpu.HBM),
            scratch=[
                VMEM((slots // BLOCK, BLOCK), jnp.int32),
                VMEM((feat, slots), BF16),
                VMEM((packed_rows, slots), BF16),
                VMEM((BLOCK, slots), BF16),
                pltpu.SemaphoreType.DMA((3,)),
            ],
            specs=[pl.BlockSpec(memory_space=pltpu.HBM)] * 3,
        )
        received = exchange(outgoing, AXES)
        row_copies, own_desc = call(
            relay_in_kernel,
            [shape((nrow, FEAT, BLOCK), BF16), shape((nblk, FEAT, BLOCK), BF16)],
            16,
            slots_in,
            received,
        )
    with jax.named_scope("gather"):
        row_desc = exchange(row_copies, "col")
        left = call(
            left_kernel,
            shape((ncol, BLOCK, BLOCK), BF16),
            4,
            row_idx,
            *column_parts(own_desc, rows),
            specs=[smem()] + [whole()] * rows,
        )
    with jax.named_scope("build"):
        wshape = pltpu.VMEM((groups // PIECES, 2 * BLOCK, 2 * BLOCK), BF16)
        empty = call(
            empty_kernel,
            [wshape] * PIECES,
            1,
            row_desc,
            left,
            row_idx,
            col_idx,
            skip_idx,
            specs=[pl.BlockSpec(memory_space=pl.ANY)] * 5,
        )
        empty = [pltpu.with_memory_space_constraint(piece, pltpu.VMEM) for piece in empty]
        *weights, degree_part = call(
            functools.partial(build_kernel, unroll=build_unroll),
            [wshape] * PIECES + [shape((cols, nblk, BLOCK))],
            8,
            row_idx,
            col_idx,
            row_desc,
            left,
            *empty,
            scratch=[
                VMEM((nrow, BLOCK, BLOCK), BF16),
                VMEM((nrow, 8, BLOCK), F32),
            ],
            specs=[smem(), smem(), whole(), whole()] + [pl.BlockSpec(memory_space=pl.ANY)] * PIECES,
            aliases={4 + k: k for k in range(PIECES)},
        )
        weights = [pltpu.with_memory_space_constraint(piece, pltpu.VMEM) for piece in weights]
    with jax.named_scope("degree"):
        sent, degree, begin = call(
            scale_kernel,
            [shape((9, VECS, BLOCK), BF16), shape((1, seg)), shape((VECS, seg))],
            8,
            exchange(degree_part, "col"),
            start,
        )

    def sweep(sent):
        vectors = column_parts(sent, rows)
        partial_sum = call(
            functools.partial(sweep_kernel, unroll=sweep_unroll, peers=rows),
            shape((cols, 9, VECS, BLOCK), BF16),
            8,
            row_idx,
            skip_idx,
            *weights,
            *vectors,
            scratch=[VMEM((rows * 9, VECS, BLOCK), BF16), VMEM((nrow, VECS, BLOCK), F32)],
            specs=[smem(), smem()] + [whole()] * (PIECES + rows),
        )
        return exchange(partial_sum, "col")

    vec = shape((VECS, seg))
    sending = shape((9, VECS, BLOCK), BF16)
    mats = shape((2, VECS, VECS))
    with jax.named_scope("step0"):
        swept = sweep(sent)
        sent, basis0, image0, trivial = call(
            first_kernel, [sending, vec, vec, shape((1, seg))], 8, swept, degree, begin
        )
    with jax.named_scope("step1"):
        swept = sweep(sent)
        sent, basis1, image1, rest1, mats0 = call(
            second_kernel, [sending, vec, vec, vec, mats], 8, swept, degree, trivial, basis0, image0
        )
    with jax.named_scope("step2"):
        swept = sweep(sent)
        small, basis2, rest2, mats1 = call(
            third_kernel,
            [shape((count * 4, BLOCK), BF16), vec, vec, mats],
            8,
            swept,
            degree,
            trivial,
            basis1,
            image1,
            rest1,
        )
    with jax.named_scope("finish"):
        three = shape((3, VECS, VECS))
        return tuple(
            call(
                functools.partial(last_kernel, norm=math.sqrt(count * seg)),
                [three, three, shape((VECS, nblk, BLOCK))],
                8,
                exchange(small, AXES),
                basis2,
                rest2,
                mats0,
                mats1,
            )
        )


def solution(mesh):
    return jax.shard_map(
        on_device,
        mesh=mesh,
        in_specs=(
            P(None, ("row", "col")),
            P(("row", "col")),
            P(("row", "col")),
            P(None, ("row", "col")),
            P(None, ("row", "col"), None),
        ),
        out_specs=(P(), P(), P(None, ("row", "col"), None)),
        check_vma=False,
    )
```

```python
import functools
import math

import jax
import jax.numpy as jnp
from jax import lax
from jax.experimental import pallas as pl
from jax.experimental.pallas import tpu as pltpu
from jax.sharding import PartitionSpec as P

FEAT = 32
BLOCK = 128
VECS = 16
BUILD_UNROLL = 43
SWEEP_UNROLL = 43
PIECES = 2
EXP2_SCALE = math.log2(math.e) / (2.0 * FEAT)
AXES = ("row", "col")
F32 = jnp.float32
BF16 = jnp.bfloat16
HIGHEST = lax.Precision.HIGHEST
VMEM = pltpu.VMEM


def params(mib):
    return pltpu.CompilerParams(vmem_limit_bytes=mib << 20)


def whole():
    return pl.BlockSpec(memory_space=pltpu.VMEM)


def smem():
    return pl.BlockSpec(memory_space=pltpu.SMEM)


def iota(shape, dim):
    return lax.broadcasted_iota(jnp.int32, shape, dim)


def split3(x):
    high = x.astype(BF16).astype(F32)
    rest = x - high
    middle = rest.astype(BF16).astype(F32)
    low = (rest - middle).astype(BF16).astype(F32)
    return high, middle, low


def dot(left, right):
    return jnp.dot(left, right, precision=HIGHEST, preferred_element_type=F32)


def dot_t(left, right):
    return lax.dot_general(
        left, right, (((1,), (1,)), ((), ())), precision=HIGHEST, preferred_element_type=F32
    )


def encode(small):
    high, middle, low = split3(small)
    return (high + pltpu.roll(middle, 40, 1) + pltpu.roll(low, 80, 1)).astype(BF16)


def decode(tiles):
    total = sum(tiles)
    value = total + pltpu.roll(total, 88, 1) + pltpu.roll(total, 48, 1)
    return jnp.where(iota((VECS, BLOCK), 1) < 40, value, 0.0)


def pad_lanes(small):
    return jnp.concatenate([small, jnp.zeros((VECS, BLOCK - small.shape[1]), F32)], axis=1)


def factor_inverse(gram):
    rows = iota((VECS, BLOCK), 0)
    lanes = iota((VECS, BLOCK), 1)
    work = pad_lanes(gram) + jnp.where(lanes == rows + VECS, 1.0, 0.0)
    columns = [jnp.broadcast_to(work[:, k : k + 1], work.shape) for k in range(VECS)]
    for k in range(VECS):
        inverse = 1.0 / columns[k][k : k + 1, :]
        ratio = jnp.where(rows > k, columns[k], 0.0) * inverse
        for n in range(k + 1, VECS):
            columns[n] = columns[n] - ratio * columns[n][k : k + 1, :]
        work = work - ratio * work[k : k + 1, :]
    diagonal = jnp.sum(jnp.where(lanes == rows, work, 0.0), axis=1, keepdims=True)
    scaled = work * lax.rsqrt(diagonal)
    upper = jnp.where(lanes >= rows, scaled, 0.0)[:, :VECS]
    return upper, scaled[:, VECS : 2 * VECS]


def relay_out_kernel(
    slot_in, desc_in, recv_slot_in, out_ref, recv_slot_out, slot_ref, desc_ref, hot_ref, spread_ref, sems
):
    copies = [
        pltpu.make_async_copy(slot_in, slot_ref, sems.at[0]),
        pltpu.make_async_copy(desc_in, desc_ref, sems.at[1]),
        pltpu.make_async_copy(recv_slot_in, recv_slot_out, sems.at[2]),
    ]
    for copy in copies:
        copy.start()
    for copy in copies:
        copy.wait()
    slots = slot_ref.shape[0] * BLOCK
    rows = out_ref.shape[0]
    target = iota((rows, BLOCK), 0)
    for t in range(slots // BLOCK):
        cut = pl.ds(t * BLOCK, BLOCK)
        slot = slot_ref[t : t + 1, :]
        hot_ref[:, cut] = jnp.where(target == (slot >> 2), 1.0, 0.0).astype(BF16)
        desc = desc_ref[:, cut].astype(F32)
        quarter = slot & 3
        for q in range(4):
            spread_ref[q * FEAT : (q + 1) * FEAT, cut] = jnp.where(quarter == q, desc, 0.0).astype(
                BF16
            )
    out_ref[...] = lax.dot_general(
        hot_ref[...], spread_ref[...], (((1,), (1,)), ((), ())), preferred_element_type=F32
    ).astype(BF16)


def relay_in_kernel(slot_ref, recv_ref, row_ref, own_ref):
    rows = recv_ref.shape[0]
    nblk = slot_ref.shape[0]
    received = recv_ref[...].astype(F32).T.astype(BF16)
    source = iota((rows, BLOCK), 0)
    for b in range(nblk):
        slot = slot_ref[b : b + 1, :]
        hot = jnp.where(source == (slot >> 2), 1.0, 0.0).astype(BF16)
        picked = jnp.dot(received, hot, preferred_element_type=F32)
        quarter = slot & 3
        own = jnp.zeros((FEAT, BLOCK), F32)
        for q in range(4):
            own = own + jnp.where(quarter == q, picked[q * FEAT : (q + 1) * FEAT, :], 0.0)
        own = own.astype(BF16)
        for copy in range(row_ref.shape[0] // nblk):
            row_ref[copy * nblk + b] = own
        own_ref[b] = own


def empty_kernel(*refs):
    for ref in refs[-PIECES:]:
        ref[0, 0:16, 0:BLOCK] = jnp.zeros((16, BLOCK), BF16)


def features(block, sign):
    values = block.astype(F32)
    pieces = split3(jnp.sum(values * values, axis=0, keepdims=True))
    rows = iota((BLOCK - FEAT, BLOCK), 0)
    tail = jnp.zeros((BLOCK - FEAT, BLOCK), F32)
    for n in range(3):
        if sign:
            tail = jnp.where(rows == n, -pieces[n], tail)
            tail = jnp.where(rows == n + 3, 1.0, tail)
        else:
            tail = jnp.where(rows == n, 1.0, tail)
            tail = jnp.where(rows == n + 3, -pieces[n], tail)
    scale = 2.0 if sign else 1.0
    return jnp.concatenate([values * scale, tail], axis=0).astype(BF16)


def each_piece(pieces, body, unroll):
    count = pieces[0].shape[0]

    def step(n, carry):
        for k, weights in enumerate(pieces):
            body(n, carry, weights, k * count)
        return carry

    lax.fori_loop(0, count // unroll, step, 0)


def left_kernel(row_idx, *refs):
    col_desc, left = refs[:-1], refs[-1]
    me = row_idx[row_idx.shape[0] - 1]
    eye = jnp.where(
        iota((BLOCK, BLOCK), 0) == iota((BLOCK, BLOCK), 1), 1.0, 0.0
    ).astype(BF16)
    for m, part in enumerate(col_desc):
        nblk = part.shape[0]
        for k in range(nblk):
            rows = features(part[k], False)
            left[(me ^ m) * nblk + k] = lax.dot_general(
                eye, rows, (((1,), (1,)), ((), ())), preferred_element_type=F32
            ).astype(BF16)


def build_kernel(row_idx, col_idx, row_desc, left, *refs, unroll):
    pieces = refs[PIECES : 2 * PIECES]
    degree, right, total = refs[2 * PIECES :]
    nrow = row_desc.shape[0]

    def prepare_row(n, carry):
        for k in range(8):
            right[n * 8 + k] = features(row_desc[n * 8 + k], True)
            total[n * 8 + k] = jnp.zeros((8, BLOCK), F32)
        return carry

    lax.fori_loop(0, nrow // 8, prepare_row, 0)

    def several(step, carry, weights, first):
        for u in range(unroll):
            group = step * unroll + u
            for q in range(4):
                i = row_idx[(first + group) * 4 + q]
                j = col_idx[(first + group) * 4 + q]
                power = jnp.dot(left[j], right[i], preferred_element_type=F32)
                block = jnp.exp2(power * EXP2_SCALE).astype(BF16)
                r, c = q // 2, q % 2
                weights[group, r * BLOCK : (r + 1) * BLOCK, c * BLOCK : (c + 1) * BLOCK] = block
                total[i] += jnp.sum(block.astype(F32).reshape(BLOCK // 8, 8, BLOCK), axis=0)
        return carry

    each_piece(pieces, several, unroll)
    for n in range(nrow):
        degree[n // 8, n % 8 : n % 8 + 1, :] = jnp.sum(total[n], axis=0, keepdims=True)


def sweep_kernel(row_idx, col_idx, *refs, unroll, peers):
    pieces = refs[:PIECES]
    parts = refs[PIECES : PIECES + peers]
    out, vectors, total = refs[PIECES + peers :]
    me = row_idx[row_idx.shape[0] - 1]
    for m in range(peers):
        for b in range(9):
            vectors[(me ^ m) * 9 + b] = parts[m][b]
    total[...] = jnp.zeros_like(total)
    zero = jnp.zeros((VECS, BLOCK), BF16)

    def several(step, carry, weights, first):
        for u in range(unroll):
            group = step * unroll + u
            picked = [vectors[col_idx[(first + group) * 4 + q]] for q in range(4)]
            lhs = jnp.concatenate(
                [
                    jnp.concatenate([picked[0], zero], 1),
                    jnp.concatenate([zero, picked[2]], 1),
                    jnp.concatenate([picked[1], zero], 1),
                    jnp.concatenate([zero, picked[3]], 1),
                ],
                0,
            )
            result = jnp.dot(lhs, weights[group], preferred_element_type=F32)
            for place, q in enumerate((0, 2, 1, 3)):
                half = (q % 2) * BLOCK
                total[row_idx[(first + group) * 4 + q]] += result[
                    place * VECS : (place + 1) * VECS, half : half + BLOCK
                ]
        return carry

    each_piece(pieces, several, unroll)
    small = encode(decode([part[8].astype(F32) for part in parts]))
    for n in range(total.shape[0]):
        out[n // 8, n % 8] = total[n].astype(BF16)
    for p in range(out.shape[0]):
        out[p, 8] = small


def row_vector(block):
    return jnp.concatenate([block[b : b + 1, :] for b in range(8)], axis=1)


def send(out, vectors, small):
    tile = encode(small)
    for b in range(8):
        out[b] = vectors[:, b * BLOCK : (b + 1) * BLOCK].astype(BF16)
    out[8] = tile


def receive(recv):
    peers = recv.shape[0]
    tiles = []
    for b in range(8):
        tile = recv[0, b].astype(F32)
        for p in range(1, peers):
            tile = tile + recv[p, b].astype(F32)
        tiles.append(tile)
    return jnp.concatenate(tiles, axis=1), decode([recv[p, 8].astype(F32) for p in range(peers)])


def stacked(parts):
    width = parts[0].shape[1]
    return jnp.concatenate(parts + [jnp.zeros((7, width), F32)], axis=0)


def scale_kernel(degree_ref, start_ref, out, degree_out, start_out):
    degree = degree_ref[0]
    for p in range(1, degree_ref.shape[0]):
        degree = degree + degree_ref[p]
    flat = row_vector(degree)
    scale = lax.rsqrt(flat)
    start = jnp.concatenate([start_ref[:, b, :] for b in range(8)], axis=1)
    degree_out[...] = flat
    start_out[...] = start
    root = jnp.sqrt(flat)
    small = pad_lanes(dot_t(start, stacked([start, jnp.zeros_like(start), root])))
    whole_sum = jnp.sum(flat, axis=1, keepdims=True)
    first = (iota((VECS, BLOCK), 0) == 0) & (iota((VECS, BLOCK), 1) == 33)
    small = small + jnp.where(first, whole_sum, 0.0)
    send(out, start * scale, small)


def first_kernel(recv, degree_ref, start_ref, out, basis_out, image_out, trivial_out):
    swept, small = receive(recv)
    degree = degree_ref[...]
    scale = lax.rsqrt(degree)
    total = small[0:1, 33:34]
    trivial = jnp.sqrt(degree / total)
    coef = small[:, 32:33] * lax.rsqrt(total)
    lanes = iota((VECS, BLOCK), 1)
    wide = jnp.where(lanes == 0, coef, 0.0)
    gram = small[:, :VECS] - dot_t(wide, wide)
    upper, inverse = factor_inverse(gram)
    along = coef * trivial
    both = dot(
        inverse,
        jnp.concatenate([start_ref[...] - along, swept * scale - along], axis=1),
    )
    width = degree.shape[1]
    basis, image = both[:, :width], both[:, width:]
    basis_out[...] = basis
    image_out[...] = image
    trivial_out[...] = trivial
    send(out, image * scale, pad_lanes(dot_t(image, stacked([basis, image, trivial]))))


def second_kernel(
    recv, degree_ref, trivial_ref, basis_ref, image_ref, out, basis_out, image_out, rest_out, mats
):
    swept, small = receive(recv)
    scale = lax.rsqrt(degree_ref[...])
    trivial = trivial_ref[...]
    alpha_t = small[:, :VECS]
    gram = small[:, VECS : 2 * VECS] - dot_t(alpha_t, alpha_t)
    upper, inverse = factor_inverse(gram)
    width = trivial.shape[1]
    mixed = dot(alpha_t, jnp.concatenate([basis_ref[...], image_ref[...]], axis=1))
    residual = image_ref[...] - mixed[:, :width]
    applied = swept * scale - small[:, 2 * VECS : 2 * VECS + 1] * trivial - mixed[:, width:]
    both = dot(inverse, jnp.concatenate([residual, applied], axis=1))
    basis, image = both[:, :width], both[:, width:]
    rest = image - dot(upper, basis_ref[...])
    basis_out[...] = basis
    image_out[...] = image
    rest_out[...] = rest
    mats[0] = alpha_t
    mats[1] = upper
    send(out, rest * scale, pad_lanes(dot_t(rest, stacked([basis, rest, trivial]))))


def third_kernel(
    recv, degree_ref, trivial_ref, basis_ref, image_ref, rest_ref, out, basis_out, rest_out, mats
):
    swept, small = receive(recv)
    scale = lax.rsqrt(degree_ref[...])
    trivial = trivial_ref[...]
    alpha_t = small[:, :VECS]
    gram = small[:, VECS : 2 * VECS] - dot_t(alpha_t, alpha_t)
    upper, inverse = factor_inverse(gram)
    width = trivial.shape[1]
    mixed = dot(alpha_t, jnp.concatenate([basis_ref[...], image_ref[...]], axis=1))
    residual = rest_ref[...] - mixed[:, :width]
    applied = swept * scale - small[:, 2 * VECS : 2 * VECS + 1] * trivial - mixed[:, width:]
    both = dot(inverse, jnp.concatenate([residual, applied], axis=1))
    basis, image = both[:, :width], both[:, width:]
    rest = image - dot(upper, basis_ref[...])
    basis_out[...] = basis
    rest_out[...] = rest
    mats[0] = alpha_t
    mats[1] = upper
    small = pad_lanes(
        dot_t(rest, jnp.concatenate([basis, rest], axis=0))
    )
    packed = small[0:4, :]
    for q in range(1, 4):
        packed = packed + pltpu.roll(small[4 * q : 4 * q + 4, :], 32 * q, 1)
    tile = jnp.concatenate([packed] * 4, axis=0).astype(BF16)
    for p in range(out.shape[0] // 16):
        out[p * 16 : (p + 1) * 16, :] = tile


def last_kernel(recv, basis_ref, rest_ref, mats_a, mats_b, alphas, betas, out, *, norm):
    tile = recv[0:16, :].astype(F32)
    for p in range(1, recv.shape[0] // 16):
        tile = tile + recv[p * 16 : (p + 1) * 16, :].astype(F32)
    packed = tile[0:4, :] + tile[4:8, :] + tile[8:12, :] + tile[12:16, :]
    lanes = iota((4, BLOCK), 1)
    rows = []
    for q in range(4):
        part = packed if q == 0 else pltpu.roll(packed, BLOCK - 32 * q, 1)
        rows.append(jnp.where(lanes < 32, part, 0.0))
    small = jnp.concatenate(rows, axis=0)
    alpha_t = small[:, :VECS]
    gram = small[:, VECS : 2 * VECS] - dot_t(alpha_t, alpha_t)
    upper, inverse = factor_inverse(gram)
    final = dot(inverse * norm, rest_ref[...] - dot(alpha_t, basis_ref[...]))
    for b in range(8):
        out[:, b, :] = final[:, b * BLOCK : (b + 1) * BLOCK]
    alphas[0] = mats_a[0].T
    alphas[1] = mats_b[0].T
    alphas[2] = alpha_t.T
    betas[0] = mats_a[1]
    betas[1] = mats_b[1]
    betas[2] = upper


def call(kernel, out_shape, mib, *args, scratch=(), specs=None, out_specs=None, aliases=None):
    outs = out_shape if isinstance(out_shape, (list, tuple)) else None
    return pl.pallas_call(
        kernel,
        out_shape=out_shape,
        in_specs=specs or [whole()] * len(args),
        out_specs=out_specs or ([whole()] * len(outs) if outs else whole()),
        scratch_shapes=list(scratch),
        input_output_aliases=aliases or {},
        compiler_params=params(mib),
    )(*args)


def exchange(values, axis):
    return lax.all_to_all(values, axis, split_axis=0, concat_axis=0, tiled=True)


def column_parts(own, rows):
    parts = [own] + [toggled(own, m, rows) for m in range(2, rows, 2)]
    return [p for part in parts for p in (part, toggled(part, 1, rows))]


def toggled(values, bits, size):
    return lax.ppermute(values, "row", [(i, i ^ bits) for i in range(size)])


def shape(dims, dtype=F32):
    return jax.ShapeDtypeStruct(dims, dtype)


def on_device(descriptors, send_slot, recv_slot, block_pairs, start):
    rows = lax.axis_size("row")
    cols = lax.axis_size("col")
    count = rows * cols
    feat, slots = descriptors.shape
    seg = recv_slot.shape[0]
    nblk = seg // BLOCK
    nrow, ncol = cols * nblk, rows * nblk
    own = jnp.arange(nblk, dtype=jnp.int32)
    me = lax.axis_index("row")
    row_idx = jnp.concatenate([block_pairs[0], lax.axis_index("col") * nblk + own, me[None]])
    col_idx = jnp.concatenate([block_pairs[1], me * nblk + own])
    skip_idx = col_idx + col_idx // nblk
    groups = col_idx.shape[0] // 4
    build_unroll = math.gcd(BUILD_UNROLL, groups // PIECES)
    sweep_unroll = math.gcd(SWEEP_UNROLL, groups // PIECES)

    with jax.named_scope("relay"):
        packed_rows = slots // 4
        outgoing, slots_in = call(
            relay_out_kernel,
            [shape((packed_rows, BLOCK), BF16), shape((nblk, BLOCK), jnp.int32)],
            16,
            pltpu.with_memory_space_constraint(send_slot.reshape(slots // BLOCK, BLOCK), pltpu.HBM),
            pltpu.with_memory_space_constraint(descriptors, pltpu.HBM),
            pltpu.with_memory_space_constraint(recv_slot.reshape(nblk, BLOCK), pltpu.HBM),
            scratch=[
                VMEM((slots // BLOCK, BLOCK), jnp.int32),
                VMEM((feat, slots), BF16),
                VMEM((packed_rows, slots), BF16),
                VMEM((BLOCK, slots), BF16),
                pltpu.SemaphoreType.DMA((3,)),
            ],
            specs=[pl.BlockSpec(memory_space=pltpu.HBM)] * 3,
        )
        received = exchange(outgoing, AXES)
        row_copies, own_desc = call(
            relay_in_kernel,
            [shape((nrow, FEAT, BLOCK), BF16), shape((nblk, FEAT, BLOCK), BF16)],
            16,
            slots_in,
            received,
        )
    with jax.named_scope("gather"):
        row_desc = exchange(row_copies, "col")
        left = call(
            left_kernel,
            shape((ncol, BLOCK, BLOCK), BF16),
            4,
            row_idx,
            *column_parts(own_desc, rows),
            specs=[smem()] + [whole()] * rows,
        )
    with jax.named_scope("build"):
        wshape = pltpu.VMEM((groups // PIECES, 2 * BLOCK, 2 * BLOCK), BF16)
        empty = call(
            empty_kernel,
            [wshape] * PIECES,
            1,
            row_desc,
            left,
            row_idx,
            col_idx,
            skip_idx,
            specs=[pl.BlockSpec(memory_space=pl.ANY)] * 5,
        )
        empty = [pltpu.with_memory_space_constraint(piece, pltpu.VMEM) for piece in empty]
        *weights, degree_part = call(
            functools.partial(build_kernel, unroll=build_unroll),
            [wshape] * PIECES + [shape((cols, nblk, BLOCK))],
            8,
            row_idx,
            col_idx,
            row_desc,
            left,
            *empty,
            scratch=[
                VMEM((nrow, BLOCK, BLOCK), BF16),
                VMEM((nrow, 8, BLOCK), F32),
            ],
            specs=[smem(), smem(), whole(), whole()] + [pl.BlockSpec(memory_space=pl.ANY)] * PIECES,
            aliases={4 + k: k for k in range(PIECES)},
        )
        weights = [pltpu.with_memory_space_constraint(piece, pltpu.VMEM) for piece in weights]
    with jax.named_scope("degree"):
        sent, degree, begin = call(
            scale_kernel,
            [shape((9, VECS, BLOCK), BF16), shape((1, seg)), shape((VECS, seg))],
            8,
            exchange(degree_part, "col"),
            start,
        )

    def sweep(sent):
        vectors = column_parts(sent, rows)
        partial_sum = call(
            functools.partial(sweep_kernel, unroll=sweep_unroll, peers=rows),
            shape((cols, 9, VECS, BLOCK), BF16),
            8,
            row_idx,
            skip_idx,
            *weights,
            *vectors,
            scratch=[VMEM((rows * 9, VECS, BLOCK), BF16), VMEM((nrow, VECS, BLOCK), F32)],
            specs=[smem(), smem()] + [whole()] * (PIECES + rows),
        )
        return exchange(partial_sum, "col")

    vec = shape((VECS, seg))
    sending = shape((9, VECS, BLOCK), BF16)
    mats = shape((2, VECS, VECS))
    with jax.named_scope("step0"):
        swept = sweep(sent)
        sent, basis0, image0, trivial = call(
            first_kernel, [sending, vec, vec, shape((1, seg))], 8, swept, degree, begin
        )
    with jax.named_scope("step1"):
        swept = sweep(sent)
        sent, basis1, image1, rest1, mats0 = call(
            second_kernel, [sending, vec, vec, vec, mats], 8, swept, degree, trivial, basis0, image0
        )
    with jax.named_scope("step2"):
        swept = sweep(sent)
        small, basis2, rest2, mats1 = call(
            third_kernel,
            [shape((count * 4, BLOCK), BF16), vec, vec, mats],
            8,
            swept,
            degree,
            trivial,
            basis1,
            image1,
            rest1,
        )
    with jax.named_scope("finish"):
        three = shape((3, VECS, VECS))
        return tuple(
            call(
                functools.partial(last_kernel, norm=math.sqrt(count * seg)),
                [three, three, shape((VECS, nblk, BLOCK))],
                8,
                exchange(small, AXES),
                basis2,
                rest2,
                mats0,
                mats1,
            )
        )


def solution(mesh):
    return jax.shard_map(
        on_device,
        mesh=mesh,
        in_specs=(
            P(None, ("row", "col")),
            P(("row", "col")),
            P(("row", "col")),
            P(None, ("row", "col")),
            P(None, ("row", "col"), None),
        ),
        out_specs=(P(), P(), P(None, ("row", "col"), None)),
        check_vma=False,
    )
```

```python
import functools
import math

import jax
import jax.numpy as jnp
from jax import lax
from jax.experimental import pallas as pl
from jax.experimental.pallas import tpu as pltpu
from jax.sharding import PartitionSpec as P

FEAT = 32
BLOCK = 128
VECS = 16
BUILD_UNROLL = 43
SWEEP_UNROLL = 43
PIECES = 2
EXP2_SCALE = math.log2(math.e) / (2.0 * FEAT)
AXES = ("row", "col")
F32 = jnp.float32
BF16 = jnp.bfloat16
HIGHEST = lax.Precision.HIGHEST
VMEM = pltpu.VMEM


def params(mib):
    return pltpu.CompilerParams(vmem_limit_bytes=mib << 20)


def whole():
    return pl.BlockSpec(memory_space=pltpu.VMEM)


def smem():
    return pl.BlockSpec(memory_space=pltpu.SMEM)


def iota(shape, dim):
    return lax.broadcasted_iota(jnp.int32, shape, dim)


def split3(x):
    high = x.astype(BF16).astype(F32)
    rest = x - high
    middle = rest.astype(BF16).astype(F32)
    low = (rest - middle).astype(BF16).astype(F32)
    return high, middle, low


def dot(left, right):
    return jnp.dot(left, right, precision=HIGHEST, preferred_element_type=F32)


def dot_t(left, right):
    return lax.dot_general(
        left, right, (((1,), (1,)), ((), ())), precision=HIGHEST, preferred_element_type=F32
    )


def encode(small):
    high, middle, low = split3(small)
    return (high + pltpu.roll(middle, 40, 1) + pltpu.roll(low, 80, 1)).astype(BF16)


def decode(tiles):
    total = sum(tiles)
    value = total + pltpu.roll(total, 88, 1) + pltpu.roll(total, 48, 1)
    return jnp.where(iota((VECS, BLOCK), 1) < 40, value, 0.0)


def pad_lanes(small):
    return jnp.concatenate([small, jnp.zeros((VECS, BLOCK - small.shape[1]), F32)], axis=1)


def factor_inverse(gram):
    rows = iota((VECS, BLOCK), 0)
    lanes = iota((VECS, BLOCK), 1)
    work = pad_lanes(gram) + jnp.where(lanes == rows + VECS, 1.0, 0.0)
    columns = [jnp.broadcast_to(work[:, k : k + 1], work.shape) for k in range(VECS)]
    for k in range(VECS):
        inverse = 1.0 / columns[k][k : k + 1, :]
        ratio = jnp.where(rows > k, columns[k], 0.0) * inverse
        for n in range(k + 1, VECS):
            columns[n] = columns[n] - ratio * columns[n][k : k + 1, :]
        work = work - ratio * work[k : k + 1, :]
    diagonal = jnp.sum(jnp.where(lanes == rows, work, 0.0), axis=1, keepdims=True)
    scaled = work * lax.rsqrt(diagonal)
    upper = jnp.where(lanes >= rows, scaled, 0.0)[:, :VECS]
    return upper, scaled[:, VECS : 2 * VECS]


def relay_out_kernel(
    slot_in, desc_in, recv_slot_in, out_ref, recv_slot_out, slot_ref, desc_ref, hot_ref, spread_ref, sems
):
    copies = [
        pltpu.make_async_copy(slot_in, slot_ref, sems.at[0]),
        pltpu.make_async_copy(desc_in, desc_ref, sems.at[1]),
        pltpu.make_async_copy(recv_slot_in, recv_slot_out, sems.at[2]),
    ]
    for copy in copies:
        copy.start()
    for copy in copies:
        copy.wait()
    slots = slot_ref.shape[0] * BLOCK
    rows = out_ref.shape[0]
    target = iota((rows, BLOCK), 0)
    for t in range(slots // BLOCK):
        cut = pl.ds(t * BLOCK, BLOCK)
        slot = slot_ref[t : t + 1, :]
        hot_ref[:, cut] = jnp.where(target == (slot >> 2), 1.0, 0.0).astype(BF16)
        desc = desc_ref[:, cut].astype(F32)
        quarter = slot & 3
        for q in range(4):
            spread_ref[q * FEAT : (q + 1) * FEAT, cut] = jnp.where(quarter == q, desc, 0.0).astype(
                BF16
            )
    out_ref[...] = lax.dot_general(
        hot_ref[...], spread_ref[...], (((1,), (1,)), ((), ())), preferred_element_type=F32
    ).astype(BF16)


def relay_in_kernel(slot_ref, recv_ref, row_ref, own_ref):
    rows = recv_ref.shape[0]
    nblk = slot_ref.shape[0]
    received = recv_ref[...].astype(F32).T.astype(BF16)
    source = iota((rows, BLOCK), 0)
    for b in range(nblk):
        slot = slot_ref[b : b + 1, :]
        hot = jnp.where(source == (slot >> 2), 1.0, 0.0).astype(BF16)
        picked = jnp.dot(received, hot, preferred_element_type=F32)
        quarter = slot & 3
        own = jnp.zeros((FEAT, BLOCK), F32)
        for q in range(4):
            own = own + jnp.where(quarter == q, picked[q * FEAT : (q + 1) * FEAT, :], 0.0)
        own = own.astype(BF16)
        for copy in range(row_ref.shape[0] // nblk):
            row_ref[copy * nblk + b] = own
        own_ref[b] = own


def empty_kernel(*refs):
    for ref in refs[-PIECES:]:
        ref[0, 0:16, 0:BLOCK] = jnp.zeros((16, BLOCK), BF16)


def features(block, sign):
    values = block.astype(F32)
    pieces = split3(jnp.sum(values * values, axis=0, keepdims=True) * EXP2_SCALE)
    height = BLOCK - 3 * FEAT
    rows = iota((height, BLOCK), 0)
    tail = jnp.zeros((height, BLOCK), F32)
    for n in range(3):
        square, one = (n, n + 3) if sign else (n + 3, n)
        tail = jnp.where(rows == square, -pieces[n], tail)
        tail = jnp.where(rows == one, 1.0, tail)
    main = split3(values * (2.0 * EXP2_SCALE)) if sign else (values,) * 3
    return jnp.concatenate([*main, tail], axis=0).astype(BF16)


def each_piece(pieces, body, unroll):
    count = pieces[0].shape[0]

    def step(n, carry):
        for k, weights in enumerate(pieces):
            body(n, carry, weights, k * count)
        return carry

    lax.fori_loop(0, count // unroll, step, 0)


def left_kernel(row_idx, *refs):
    col_desc, left = refs[:-1], refs[-1]
    me = row_idx[row_idx.shape[0] - 1]
    eye = jnp.where(
        iota((BLOCK, BLOCK), 0) == iota((BLOCK, BLOCK), 1), 1.0, 0.0
    ).astype(BF16)
    for m, part in enumerate(col_desc):
        nblk = part.shape[0]
        for k in range(nblk):
            rows = features(part[k], False)
            left[(me ^ m) * nblk + k] = lax.dot_general(
                eye, rows, (((1,), (1,)), ((), ())), preferred_element_type=F32
            ).astype(BF16)


def build_kernel(row_idx, col_idx, row_desc, left, *refs, unroll):
    pieces = refs[PIECES : 2 * PIECES]
    degree, right, total = refs[2 * PIECES :]
    nrow = row_desc.shape[0]

    def prepare_row(n, carry):
        for k in range(8):
            right[n * 8 + k] = features(row_desc[n * 8 + k], True)
            total[n * 8 + k] = jnp.zeros((8, BLOCK), F32)
        return carry

    lax.fori_loop(0, nrow // 8, prepare_row, 0)

    def several(step, carry, weights, first):
        for u in range(unroll):
            group = step * unroll + u
            for q in range(4):
                i = row_idx[(first + group) * 4 + q]
                j = col_idx[(first + group) * 4 + q]
                power = jnp.dot(left[j], right[i], preferred_element_type=F32)
                block = jnp.exp2(power).astype(BF16)
                r, c = q // 2, q % 2
                weights[group, r * BLOCK : (r + 1) * BLOCK, c * BLOCK : (c + 1) * BLOCK] = block
                total[i] += jnp.sum(block.astype(F32).reshape(BLOCK // 8, 8, BLOCK), axis=0)
        return carry

    each_piece(pieces, several, unroll)
    for n in range(nrow):
        degree[n // 8, n % 8 : n % 8 + 1, :] = jnp.sum(total[n], axis=0, keepdims=True)


def sweep_kernel(row_idx, col_idx, *refs, unroll, peers):
    pieces = refs[:PIECES]
    parts = refs[PIECES : PIECES + peers]
    out, vectors, total = refs[PIECES + peers :]
    me = row_idx[row_idx.shape[0] - 1]
    for m in range(peers):
        for b in range(9):
            vectors[(me ^ m) * 9 + b] = parts[m][b]
    total[...] = jnp.zeros_like(total)
    zero = jnp.zeros((VECS, BLOCK), BF16)

    def several(step, carry, weights, first):
        for u in range(unroll):
            group = step * unroll + u
            picked = [vectors[col_idx[(first + group) * 4 + q]] for q in range(4)]
            lhs = jnp.concatenate(
                [
                    jnp.concatenate([picked[0], zero], 1),
                    jnp.concatenate([zero, picked[2]], 1),
                    jnp.concatenate([picked[1], zero], 1),
                    jnp.concatenate([zero, picked[3]], 1),
                ],
                0,
            )
            result = jnp.dot(lhs, weights[group], preferred_element_type=F32)
            for place, q in enumerate((0, 2, 1, 3)):
                half = (q % 2) * BLOCK
                total[row_idx[(first + group) * 4 + q]] += result[
                    place * VECS : (place + 1) * VECS, half : half + BLOCK
                ]
        return carry

    each_piece(pieces, several, unroll)
    small = encode(decode([part[8].astype(F32) for part in parts]))
    for n in range(total.shape[0]):
        out[n // 8, n % 8] = total[n].astype(BF16)
    for p in range(out.shape[0]):
        out[p, 8] = small


def row_vector(block):
    return jnp.concatenate([block[b : b + 1, :] for b in range(8)], axis=1)


def send(out, vectors, small):
    tile = encode(small)
    for b in range(8):
        out[b] = vectors[:, b * BLOCK : (b + 1) * BLOCK].astype(BF16)
    out[8] = tile


def receive(recv):
    peers = recv.shape[0]
    tiles = []
    for b in range(8):
        tile = recv[0, b].astype(F32)
        for p in range(1, peers):
            tile = tile + recv[p, b].astype(F32)
        tiles.append(tile)
    return jnp.concatenate(tiles, axis=1), decode([recv[p, 8].astype(F32) for p in range(peers)])


def stacked(parts):
    width = parts[0].shape[1]
    return jnp.concatenate(parts + [jnp.zeros((7, width), F32)], axis=0)


def scale_kernel(degree_ref, start_ref, out, degree_out, start_out):
    degree = degree_ref[0]
    for p in range(1, degree_ref.shape[0]):
        degree = degree + degree_ref[p]
    flat = row_vector(degree)
    scale = lax.rsqrt(flat)
    start = jnp.concatenate([start_ref[:, b, :] for b in range(8)], axis=1)
    degree_out[...] = flat
    start_out[...] = start
    root = jnp.sqrt(flat)
    small = pad_lanes(dot_t(start, stacked([start, jnp.zeros_like(start), root])))
    whole_sum = jnp.sum(flat, axis=1, keepdims=True)
    first = (iota((VECS, BLOCK), 0) == 0) & (iota((VECS, BLOCK), 1) == 33)
    small = small + jnp.where(first, whole_sum, 0.0)
    send(out, start * scale, small)


def first_kernel(recv, degree_ref, start_ref, out, basis_out, image_out, trivial_out):
    swept, small = receive(recv)
    degree = degree_ref[...]
    scale = lax.rsqrt(degree)
    total = small[0:1, 33:34]
    trivial = jnp.sqrt(degree / total)
    coef = small[:, 32:33] * lax.rsqrt(total)
    lanes = iota((VECS, BLOCK), 1)
    wide = jnp.where(lanes == 0, coef, 0.0)
    gram = small[:, :VECS] - dot_t(wide, wide)
    upper, inverse = factor_inverse(gram)
    along = coef * trivial
    both = dot(
        inverse,
        jnp.concatenate([start_ref[...] - along, swept * scale - along], axis=1),
    )
    width = degree.shape[1]
    basis, image = both[:, :width], both[:, width:]
    basis_out[...] = basis
    image_out[...] = image
    trivial_out[...] = trivial
    send(out, image * scale, pad_lanes(dot_t(image, stacked([basis, image, trivial]))))


def second_kernel(
    recv, degree_ref, trivial_ref, basis_ref, image_ref, out, basis_out, image_out, rest_out, mats
):
    swept, small = receive(recv)
    scale = lax.rsqrt(degree_ref[...])
    trivial = trivial_ref[...]
    alpha_t = small[:, :VECS]
    gram = small[:, VECS : 2 * VECS] - dot_t(alpha_t, alpha_t)
    upper, inverse = factor_inverse(gram)
    width = trivial.shape[1]
    mixed = dot(alpha_t, jnp.concatenate([basis_ref[...], image_ref[...]], axis=1))
    residual = image_ref[...] - mixed[:, :width]
    applied = swept * scale - small[:, 2 * VECS : 2 * VECS + 1] * trivial - mixed[:, width:]
    both = dot(inverse, jnp.concatenate([residual, applied], axis=1))
    basis, image = both[:, :width], both[:, width:]
    rest = image - dot(upper, basis_ref[...])
    basis_out[...] = basis
    image_out[...] = image
    rest_out[...] = rest
    mats[0] = alpha_t
    mats[1] = upper
    send(out, rest * scale, pad_lanes(dot_t(rest, stacked([basis, rest, trivial]))))


def third_kernel(
    recv, degree_ref, trivial_ref, basis_ref, image_ref, rest_ref, out, basis_out, rest_out, mats
):
    swept, small = receive(recv)
    scale = lax.rsqrt(degree_ref[...])
    trivial = trivial_ref[...]
    alpha_t = small[:, :VECS]
    gram = small[:, VECS : 2 * VECS] - dot_t(alpha_t, alpha_t)
    upper, inverse = factor_inverse(gram)
    width = trivial.shape[1]
    mixed = dot(alpha_t, jnp.concatenate([basis_ref[...], image_ref[...]], axis=1))
    residual = rest_ref[...] - mixed[:, :width]
    applied = swept * scale - small[:, 2 * VECS : 2 * VECS + 1] * trivial - mixed[:, width:]
    both = dot(inverse, jnp.concatenate([residual, applied], axis=1))
    basis, image = both[:, :width], both[:, width:]
    rest = image - dot(upper, basis_ref[...])
    basis_out[...] = basis
    rest_out[...] = rest
    mats[0] = alpha_t
    mats[1] = upper
    small = pad_lanes(
        dot_t(rest, jnp.concatenate([basis, rest], axis=0))
    )
    packed = small[0:4, :]
    for q in range(1, 4):
        packed = packed + pltpu.roll(small[4 * q : 4 * q + 4, :], 32 * q, 1)
    tile = jnp.concatenate([packed] * 4, axis=0).astype(BF16)
    for p in range(out.shape[0] // 16):
        out[p * 16 : (p + 1) * 16, :] = tile


def last_kernel(recv, basis_ref, rest_ref, mats_a, mats_b, alphas, betas, out, *, norm):
    tile = recv[0:16, :].astype(F32)
    for p in range(1, recv.shape[0] // 16):
        tile = tile + recv[p * 16 : (p + 1) * 16, :].astype(F32)
    packed = tile[0:4, :] + tile[4:8, :] + tile[8:12, :] + tile[12:16, :]
    lanes = iota((4, BLOCK), 1)
    rows = []
    for q in range(4):
        part = packed if q == 0 else pltpu.roll(packed, BLOCK - 32 * q, 1)
        rows.append(jnp.where(lanes < 32, part, 0.0))
    small = jnp.concatenate(rows, axis=0)
    alpha_t = small[:, :VECS]
    gram = small[:, VECS : 2 * VECS] - dot_t(alpha_t, alpha_t)
    upper, inverse = factor_inverse(gram)
    final = dot(inverse * norm, rest_ref[...] - dot(alpha_t, basis_ref[...]))
    for b in range(8):
        out[:, b, :] = final[:, b * BLOCK : (b + 1) * BLOCK]
    alphas[0] = mats_a[0].T
    alphas[1] = mats_b[0].T
    alphas[2] = alpha_t.T
    betas[0] = mats_a[1]
    betas[1] = mats_b[1]
    betas[2] = upper


def call(kernel, out_shape, mib, *args, scratch=(), specs=None, out_specs=None, aliases=None):
    outs = out_shape if isinstance(out_shape, (list, tuple)) else None
    return pl.pallas_call(
        kernel,
        out_shape=out_shape,
        in_specs=specs or [whole()] * len(args),
        out_specs=out_specs or ([whole()] * len(outs) if outs else whole()),
        scratch_shapes=list(scratch),
        input_output_aliases=aliases or {},
        compiler_params=params(mib),
    )(*args)


def exchange(values, axis):
    return lax.all_to_all(values, axis, split_axis=0, concat_axis=0, tiled=True)


def column_parts(own, rows):
    parts = [own] + [toggled(own, m, rows) for m in range(2, rows, 2)]
    return [p for part in parts for p in (part, toggled(part, 1, rows))]


def toggled(values, bits, size):
    return lax.ppermute(values, "row", [(i, i ^ bits) for i in range(size)])


def shape(dims, dtype=F32):
    return jax.ShapeDtypeStruct(dims, dtype)


def on_device(descriptors, send_slot, recv_slot, block_pairs, start):
    rows = lax.axis_size("row")
    cols = lax.axis_size("col")
    count = rows * cols
    feat, slots = descriptors.shape
    seg = recv_slot.shape[0]
    nblk = seg // BLOCK
    nrow, ncol = cols * nblk, rows * nblk
    own = jnp.arange(nblk, dtype=jnp.int32)
    me = lax.axis_index("row")
    row_idx = jnp.concatenate([block_pairs[0], lax.axis_index("col") * nblk + own, me[None]])
    col_idx = jnp.concatenate([block_pairs[1], me * nblk + own])
    skip_idx = col_idx + col_idx // nblk
    groups = col_idx.shape[0] // 4
    build_unroll = math.gcd(BUILD_UNROLL, groups // PIECES)
    sweep_unroll = math.gcd(SWEEP_UNROLL, groups // PIECES)

    with jax.named_scope("relay"):
        packed_rows = slots // 4
        outgoing, slots_in = call(
            relay_out_kernel,
            [shape((packed_rows, BLOCK), BF16), shape((nblk, BLOCK), jnp.int32)],
            16,
            pltpu.with_memory_space_constraint(send_slot.reshape(slots // BLOCK, BLOCK), pltpu.HBM),
            pltpu.with_memory_space_constraint(descriptors, pltpu.HBM),
            pltpu.with_memory_space_constraint(recv_slot.reshape(nblk, BLOCK), pltpu.HBM),
            scratch=[
                VMEM((slots // BLOCK, BLOCK), jnp.int32),
                VMEM((feat, slots), BF16),
                VMEM((packed_rows, slots), BF16),
                VMEM((BLOCK, slots), BF16),
                pltpu.SemaphoreType.DMA((3,)),
            ],
            specs=[pl.BlockSpec(memory_space=pltpu.HBM)] * 3,
        )
        received = exchange(outgoing, AXES)
        row_copies, own_desc = call(
            relay_in_kernel,
            [shape((nrow, FEAT, BLOCK), BF16), shape((nblk, FEAT, BLOCK), BF16)],
            16,
            slots_in,
            received,
        )
    with jax.named_scope("gather"):
        row_desc = exchange(row_copies, "col")
        left = call(
            left_kernel,
            shape((ncol, BLOCK, BLOCK), BF16),
            4,
            row_idx,
            *column_parts(own_desc, rows),
            specs=[smem()] + [whole()] * rows,
        )
    with jax.named_scope("build"):
        wshape = pltpu.VMEM((groups // PIECES, 2 * BLOCK, 2 * BLOCK), BF16)
        empty = call(
            empty_kernel,
            [wshape] * PIECES,
            1,
            row_desc,
            left,
            row_idx,
            col_idx,
            skip_idx,
            specs=[pl.BlockSpec(memory_space=pl.ANY)] * 5,
        )
        empty = [pltpu.with_memory_space_constraint(piece, pltpu.VMEM) for piece in empty]
        *weights, degree_part = call(
            functools.partial(build_kernel, unroll=build_unroll),
            [wshape] * PIECES + [shape((cols, nblk, BLOCK))],
            8,
            row_idx,
            col_idx,
            row_desc,
            left,
            *empty,
            scratch=[
                VMEM((nrow, BLOCK, BLOCK), BF16),
                VMEM((nrow, 8, BLOCK), F32),
            ],
            specs=[smem(), smem(), whole(), whole()] + [pl.BlockSpec(memory_space=pl.ANY)] * PIECES,
            aliases={4 + k: k for k in range(PIECES)},
        )
        weights = [pltpu.with_memory_space_constraint(piece, pltpu.VMEM) for piece in weights]
    with jax.named_scope("degree"):
        sent, degree, begin = call(
            scale_kernel,
            [shape((9, VECS, BLOCK), BF16), shape((1, seg)), shape((VECS, seg))],
            8,
            exchange(degree_part, "col"),
            start,
        )

    def sweep(sent):
        vectors = column_parts(sent, rows)
        partial_sum = call(
            functools.partial(sweep_kernel, unroll=sweep_unroll, peers=rows),
            shape((cols, 9, VECS, BLOCK), BF16),
            8,
            row_idx,
            skip_idx,
            *weights,
            *vectors,
            scratch=[VMEM((rows * 9, VECS, BLOCK), BF16), VMEM((nrow, VECS, BLOCK), F32)],
            specs=[smem(), smem()] + [whole()] * (PIECES + rows),
        )
        return exchange(partial_sum, "col")

    vec = shape((VECS, seg))
    sending = shape((9, VECS, BLOCK), BF16)
    mats = shape((2, VECS, VECS))
    with jax.named_scope("step0"):
        swept = sweep(sent)
        sent, basis0, image0, trivial = call(
            first_kernel, [sending, vec, vec, shape((1, seg))], 8, swept, degree, begin
        )
    with jax.named_scope("step1"):
        swept = sweep(sent)
        sent, basis1, image1, rest1, mats0 = call(
            second_kernel, [sending, vec, vec, vec, mats], 8, swept, degree, trivial, basis0, image0
        )
    with jax.named_scope("step2"):
        swept = sweep(sent)
        small, basis2, rest2, mats1 = call(
            third_kernel,
            [shape((count * 4, BLOCK), BF16), vec, vec, mats],
            8,
            swept,
            degree,
            trivial,
            basis1,
            image1,
            rest1,
        )
    with jax.named_scope("finish"):
        three = shape((3, VECS, VECS))
        return tuple(
            call(
                functools.partial(last_kernel, norm=math.sqrt(count * seg)),
                [three, three, shape((VECS, nblk, BLOCK))],
                8,
                exchange(small, AXES),
                basis2,
                rest2,
                mats0,
                mats1,
            )
        )


def solution(mesh):
    return jax.shard_map(
        on_device,
        mesh=mesh,
        in_specs=(
            P(None, ("row", "col")),
            P(("row", "col")),
            P(("row", "col")),
            P(None, ("row", "col")),
            P(None, ("row", "col"), None),
        ),
        out_specs=(P(), P(), P(None, ("row", "col"), None)),
        check_vma=False,
    )
```
